32 devices in a mesh: dp: 16 (over z, x, core), mp: 2 (over y).
Axes of the slice: x: 2, y: 2, z: 4, core: 2. Of those that a mesh axis runs over, the one named last changes fastest.
Arguments:
- tokens: bfloat16 [48, 512, 768], P('dp', 'mp'), may hold values from -6 to 6
- segment_ids: int32 [48, 512], P('dp'), may hold values from 0 to 3, never falling along the last dimension, each value on 1 to 256 neighbouring positions
- out_grad: bfloat16 [48, 512, 768], P('dp', 'mp'), may hold values from -6 to 6
- t_qkv: bfloat16 [3, 768, 768], P(None, 'dp', 'mp'), may hold values from -0.21875 to 0.21875
- t_qv_bias: bfloat16 [2, 768], P(None, 'mp'), may hold values from -3 to 3
- t_out: bfloat16 [768, 768], P('mp', 'dp'), may hold values from -2 to 2
- t_up: bfloat16 [768, 3072], P('dp', 'mp'), may hold values from -0.21875 to 0.21875
- t_up_bias: bfloat16 [3072], P('mp'), may hold values from -3 to 3
- t_down: bfloat16 [3072, 768], P('mp', 'dp'), may hold values from -0.21875 to 0.21875
- t_gains: bfloat16 [2, 768], P(None, 'dp'), may hold values from 0.5 to 1.5
- t_shifts: bfloat16 [4, 768], P(None, 'dp'), may hold values from -3 to 3
- s_qkv: bfloat16 [3, 768, 384], P(None, 'dp', 'mp'), may hold values from -0.21875 to 0.21875
- s_qv_bias: bfloat16 [2, 384], P(None, 'mp'), may hold values from -3 to 3
- s_out: bfloat16 [384, 768], P('mp', 'dp'), may hold values from -3 to 3
- s_up: bfloat16 [768, 1536], P('dp', 'mp'), may hold values from -0.21875 to 0.21875
- s_up_bias: bfloat16 [1536], P('mp'), may hold values from -3 to 3
- s_down: bfloat16 [1536, 768], P('mp', 'dp'), may hold values from -0.3125 to 0.3125
- s_gains: bfloat16 [2, 768], P(None, 'dp'), may hold values from 0.5 to 1.5
- s_shifts: bfloat16 [4, 768], P(None, 'dp'), may hold values from -3 to 3
Outputs:
- output: float32 [48, 512, 768], P('dp', 'mp')
- input_grad: float32 [48, 512, 768], P('dp', 'mp')
- grad_t_qkv: float32 [3, 768, 768], P(None, 'dp', 'mp')
- grad_t_qv_bias: float32 [2, 768], P(None, 'mp')
- grad_t_out: float32 [768, 768], P('mp', 'dp')
- grad_t_up: float32 [768, 3072], P('dp', 'mp')
- grad_t_up_bias: float32 [3072], P('mp')
- grad_t_down: float32 [3072, 768], P('mp', 'dp')
- grad_t_gains: float32 [2, 768], P(None, 'dp')
- grad_t_shifts: float32 [4, 768], P(None, 'dp')
- grad_s_qkv: float32 [3, 768, 384], P(None, 'dp', 'mp')
- grad_s_qv_bias: float32 [2, 384], P(None, 'mp')
- grad_s_out: float32 [384, 768], P('mp', 'dp')
- grad_s_up: float32 [768, 1536], P('dp', 'mp')
- grad_s_up_bias: float32 [1536], P('mp')
- grad_s_down: float32 [1536, 768], P('mp', 'dp')
- grad_s_gains: float32 [2, 768], P(None, 'dp')
- grad_s_shifts: float32 [4, 768], P(None, 'dp')
The draws below stay inside these ranges and needn't reach their ends.
Inputs may be any that keep to these rules, and one draw needn't show every extreme that they name: `segment_ids`: segment numbers never fall along a row; a segment holds at most 256 positions of one row.
All inputs are finite; a program needn't handle non-finite values.
Results may differ from the reference program's by a relative error of at most 0.035.
Values may be sent and summed in bfloat16 or wider, within the bound.
No kernel may reach another device: no remote copies, remote signals or barrier semaphores. Data moves between devices by JAX's collectives and lax.ppermute only.
A program may use at most 256 MiB of HBM per device.

```python
import math
import jax
import jax.numpy as jnp
import numpy as np
from jax import lax

D = 768
HEAD_DIM = 64
T_FF = 3072
S_FF = 1536
T_WIDTH = 768
S_WIDTH = 384
LEN = 512
ROWS = 48
N_MP = 2


def raised(entries, own_key, source, target, blocks, factor):
    owner, partner = [(jnp.arange(entries.shape[axis_at]) // (entries.shape[axis_at] // blocks)).reshape([-1 if axis == axis_at else 1 for axis in range(entries.ndim)]) for axis_at in (source, target)]
    chosen = jax.random.permutation(own_key, blocks)[partner]
    strong = (owner == chosen) | (owner == (partner + blocks // 2) % blocks)
    return jnp.where(strong, factor * entries, entries)


def level_of(stream_key, shape, shards, least, top_value):
    loudness, own = 1.0, jax.random.fold_in(stream_key, 6)
    for dim, blocks in shards:
        draws = jnp.exp(jax.random.uniform(jax.random.fold_in(own, dim), (blocks,), jnp.float32, least / len(shards), top_value / len(shards)))
        loudness = loudness * jnp.repeat(draws, shape[dim] // blocks).reshape([-1 if axis == dim else 1 for axis in range(len(shape))])
    return loudness


def profile(count, total, limit, lean):
    weights = [(1 << 20) // math.isqrt(rank ** lean) + 1 for rank in range(2, count + 1)]
    surplus, holding = total - limit - (count - 1), [1] * (count - 1)
    while surplus > 0:
        free = [i for i in range(count - 1) if holding[i] < limit]
        pool, remaining = sum([weights[i] for i in free]), surplus
        for i in free:
            more = min(limit - holding[i], max(1, remaining * weights[i] // pool), surplus)
            holding[i] = holding[i] + more
            surplus = surplus - more
    return np.array([limit] + holding)


def ragged(stream_key, amount, total, reach, lean):
    if amount == 2:
        one = jax.random.randint(stream_key, (), max(1, total - reach), min(reach, total - 1) + 1)
        return jnp.stack([one, total - one])
    sizes = jnp.asarray(profile(amount, total, reach, lean), jnp.int32)
    twos = (amount - 1) // 2
    source_of, receiver = sizes[1:1 + 2 * twos:2], sizes[2:2 + 2 * twos:2]
    room = jnp.minimum(source_of - 1, reach - receiver)
    moved = jax.random.randint(jax.random.fold_in(stream_key, 1), (twos,), 0, 1 << 20) % (room + 1)
    sizes = sizes.at[1:1 + 2 * twos:2].set(source_of - moved).at[2:2 + 2 * twos:2].set(receiver + moved)
    return sizes[jax.random.permutation(jax.random.fold_in(stream_key, 2), amount)]


def noise(rng, shape, deviation, reach, cuts=(), dtype=jnp.bfloat16):
    drawn = deviation * jax.random.normal(rng, shape, jnp.float32)
    if cuts:
        drawn = drawn * level_of(rng, shape, cuts, -0.22, 0.18)
    return jnp.clip(drawn, -reach, reach).astype(dtype)


def heavy_noise(own_key, extent, scale, reach, split, heavy, held_as=jnp.bfloat16):
    array = scale * jax.random.normal(own_key, extent, jnp.float32)
    if split:
        array = array * level_of(own_key, extent, split, -0.22, 0.18)
    return jnp.clip(raised(array, jax.random.fold_in(own_key, 3), *heavy), -reach, reach).astype(held_as)


def setup_inputs(seed: int = 0) -> dict:
    key_of = jax.random.split(jax.random.key(seed), 20)
    tokens = noise(key_of[0], (ROWS, LEN, D), 1.0, 6.0, ((0, 16), (1, 2)))
    segment_ids = jax.vmap(lambda own: jnp.searchsorted(jnp.cumsum(ragged(own, 4, LEN, LEN // 2, 2)), jnp.arange(LEN), side="right"))(jax.random.split(key_of[1], ROWS)).reshape((ROWS, LEN)).astype(jnp.int32)
    out_grad = heavy_noise(key_of[2], (ROWS, LEN, D), 1.0, 6.0, ((0, 16), (1, 2)), (0, 2, 16, 2.0))
    t_qkv = noise(key_of[3], (3, D, T_WIDTH), D ** -0.5, 0.21875, ((1, 16), (2, 2)))
    t_qv_bias = noise(key_of[4], (2, T_WIDTH), 0.5, 3.0, ((1, 2),))
    t_out = noise(key_of[5], (T_WIDTH, D), (max(T_WIDTH // 96, 2)) ** -0.5, 2.0, ((0, 2), (1, 16)))
    t_up = noise(key_of[6], (D, T_FF), D ** -0.5, 0.21875, ((0, 16), (1, 2)))
    t_up_bias = noise(key_of[7], (T_FF,), 0.5, 3.0, ((0, 2),))
    t_down = noise(key_of[8], (T_FF, D), (T_FF // 4) ** -0.5, 0.21875, ((0, 2), (1, 16)))
    t_gains = jnp.clip(1.0 + 0.1 * jax.random.normal(key_of[9], (2, D), jnp.float32), 0.5, 1.5).astype(jnp.bfloat16)
    t_shifts = noise(key_of[10], (4, D), 0.5, 3.0, ((1, 16),))
    s_qkv = noise(key_of[11], (3, D, S_WIDTH), D ** -0.5, 0.21875, ((1, 16), (2, 2)))
    s_qv_bias = noise(key_of[12], (2, S_WIDTH), 0.5, 3.0, ((1, 2),))
    s_out = noise(key_of[13], (S_WIDTH, D), (max(S_WIDTH // 96, 2)) ** -0.5, 3.0, ((0, 2), (1, 16)))
    s_up = noise(key_of[14], (D, S_FF), D ** -0.5, 0.21875, ((0, 16), (1, 2)))
    s_up_bias = noise(key_of[15], (S_FF,), 0.5, 3.0, ((0, 2),))
    s_down = noise(key_of[16], (S_FF, D), (S_FF // 4) ** -0.5, 0.3125, ((0, 2), (1, 16)))
    s_gains = jnp.clip(1.0 + 0.1 * jax.random.normal(key_of[17], (2, D), jnp.float32), 0.5, 1.5).astype(jnp.bfloat16)
    s_shifts = noise(key_of[18], (4, D), 0.5, 3.0, ((1, 16),))
    return {"tokens": tokens, "segment_ids": segment_ids, "out_grad": out_grad, "t_qkv": t_qkv, "t_qv_bias": t_qv_bias, "t_out": t_out, "t_up": t_up, "t_up_bias": t_up_bias, "t_down": t_down, "t_gains": t_gains, "t_shifts": t_shifts, "s_qkv": s_qkv, "s_qv_bias": s_qv_bias, "s_out": s_out, "s_up": s_up, "s_up_bias": s_up_bias, "s_down": s_down, "s_gains": s_gains, "s_shifts": s_shifts}


@jax.custom_vjp
def low(v):
    return lax.optimization_barrier(v.astype(jnp.bfloat16)).astype(jnp.float32)

@jax.custom_vjp
def low_back(v):
    return v

def low_keep(v):
    return (low(v), None)

def low_pass(kept, grad):
    return (grad,)

def back_keep(v):
    return (v, None)

def back_low(kept, grad):
    return (low(grad),)
low.defvjp(low_keep, low_pass)
low_back.defvjp(back_keep, back_low)

def matmul(left, right):
    return jnp.dot(left, right, precision=lax.Precision.HIGHEST, preferred_element_type=jnp.float32)

def norm_layer(value, gain, shift):
    center = value - lax.optimization_barrier(jnp.mean(value, axis=-1, keepdims=True))
    spread = lax.optimization_barrier(jnp.mean(center * center, axis=-1, keepdims=True))
    return center * lax.rsqrt(spread + 1e-06) * gain + shift

def encoder_layer(inputs, segs, qkv, qv_bias, out_w, up_w, up_bias, down_w, gains, shifts):
    rows, length = segs.shape
    scale = HEAD_DIM ** (-0.5)
    inputs_low = low(inputs)
    width = qkv.shape[2] // N_MP
    neurons = up_w.shape[1] // N_MP
    heads = width // HEAD_DIM
    same = (segs[:, :, None] == segs[:, None, :])[:, None]
    attn = jnp.zeros_like(inputs)
    for group in range(N_MP):
        part = slice(group * width, (group + 1) * width)
        inputs_g = low_back(inputs_low)
        query = low_back(low(matmul(inputs_g, qkv[0][:, part]) + qv_bias[0][part]))
        keys = low_back(low(matmul(inputs_g, qkv[1][:, part])))
        values = low_back(low(matmul(inputs_g, qkv[2][:, part]) + qv_bias[1][part]))
        query = query.reshape(rows, length, heads, HEAD_DIM)
        keys = keys.reshape(rows, length, heads, HEAD_DIM)
        values = values.reshape(rows, length, heads, HEAD_DIM)
        scores = jnp.einsum('rqhe,rkhe->rhqk', query, keys, precision=lax.Precision.HIGHEST)
        scores = low_back(scores * scale)
        scores = jnp.where(same, scores, -1000000000.0)
        top = lax.optimization_barrier(jnp.max(scores, axis=-1, keepdims=True))
        expo = jnp.exp(scores - top)
        probs = expo / lax.optimization_barrier(jnp.sum(expo, axis=-1, keepdims=True))
        context = jnp.einsum('rhqk,rkhe->rqhe', low(probs), values, precision=lax.Precision.HIGHEST)
        context = low_back(low(context.reshape(rows * length, width)))
        attn = attn + low_back(low(matmul(context, out_w[part])))
    mid = inputs + attn + shifts[0]
    hidden = norm_layer(mid, gains[0], shifts[1])
    hidden_low = low(hidden)
    ffn = jnp.zeros_like(inputs)
    for group in range(N_MP):
        part = slice(group * neurons, (group + 1) * neurons)
        hidden_g = low_back(hidden_low)
        pre = low_back(matmul(hidden_g, up_w[:, part]) + up_bias[part])
        act = low(jax.nn.gelu(pre, approximate=False))
        ffn = ffn + low_back(low(matmul(act, down_w[part])))
    final = hidden + ffn + shifts[2]
    return norm_layer(final, gains[1], shifts[3])

def reference(tokens, segment_ids, out_grad, t_qkv, t_qv_bias, t_out, t_up, t_up_bias, t_down, t_gains, t_shifts, s_qkv, s_qv_bias, s_out, s_up, s_up_bias, s_down, s_gains, s_shifts):
    params = tuple((arr.astype(jnp.float32) for arr in (t_qkv, t_qv_bias, t_out, t_up, t_up_bias, t_down, t_gains, t_shifts, s_qkv, s_qv_bias, s_out, s_up, s_up_bias, s_down, s_gains, s_shifts)))
    block = math.gcd(ROWS, 8)
    seg_blocks = segment_ids.reshape(ROWS // block, block, LEN)

    def forward(inputs, weights):
        blocks = inputs.reshape(ROWS // block, block, LEN, D)

        def one_block(pair):
            rows_in, segs = pair
            flat = rows_in.reshape(block * LEN, D)
            first = encoder_layer(flat, segs, *weights[:8])
            second = encoder_layer(first, segs, *weights[8:])
            return second.reshape(block, LEN, D)
        outs = lax.map(jax.checkpoint(one_block), (blocks, seg_blocks))
        return outs.reshape(ROWS, LEN, D)
    output, pull = jax.vjp(forward, tokens.astype(jnp.float32), params)
    input_grad, grads = pull(out_grad.astype(jnp.float32))
    return (output, input_grad, grads[0], grads[1], grads[2], grads[3], grads[4], grads[5], grads[6], grads[7], grads[8], grads[9], grads[10], grads[11], grads[12], grads[13], grads[14], grads[15])
```

```python
import math

import jax
import jax.numpy as jnp
from jax import lax
from jax.sharding import PartitionSpec as P

HEAD_DIM = 64
LOW = jnp.bfloat16
F32 = jnp.float32


def ring_of(count):
    return list(range(0, count, 2)) + list(range(1, count, 2))[::-1]


def swap_y(value):
    return lax.ppermute(value, "mp", [(0, 1), (1, 0)])


def swap_x(value):
    n = lax.axis_size("dp")
    return lax.ppermute(value, "dp", [(i, i ^ 2) for i in range(n)])


def swap_core(value):
    n = lax.axis_size("dp")
    return lax.ppermute(value, "dp", [(i, i ^ 1) for i in range(n)])


def ring_shift(value, step):
    count = lax.axis_size("dp") // 4
    ring = ring_of(count)
    pairs = []
    for place in range(count):
        for low in range(4):
            pairs.append((ring[place] * 4 + low, ring[(place + step) % count] * 4 + low))
    return lax.ppermute(value, "dp", pairs)


def feature_order(width):
    n = lax.axis_size("dp")
    count, rows = n // 4, width // n
    me = lax.axis_index("dp")
    z, x, core = me // 4, (me // 2) % 2, me % 2
    place = jnp.where(z % 2 == 0, z // 2, count - 1 - z // 2)
    at = lax.iota(jnp.int32, width)
    row = at % rows
    back = (at // rows) % count
    x_rel = (at // (rows * count)) % 2
    core_rel = at // (rows * count * 2)
    from_place = (place - back + count) % count
    half = (count + 1) // 2
    z_abs = jnp.where(from_place < half, 2 * from_place, 2 * (count - 1 - from_place) + 1)
    block = z_abs * 4 + (x ^ x_rel) * 2 + (core ^ core_rel)
    return block * rows + row


def gather_pair(parts_a, parts_b):
    count = lax.axis_size("dp") // 4
    a = jnp.concatenate(list(parts_a.values()), axis=1)
    b = jnp.concatenate(list(parts_b.values()), axis=1)
    cut = a.shape[1]
    pieces = [jnp.concatenate([a, b], axis=1)]
    for _ in range(count - 1):
        pieces.append(ring_shift(pieces[-1], 1))
    a = jnp.stack([piece[:, :cut] for piece in pieces])
    b = jnp.stack([piece[:, cut:] for piece in pieces])
    a = jnp.stack([a, swap_x(a)])
    b = jnp.stack([b, swap_y(b)])
    a = jnp.stack([a, swap_y(a)])
    b = jnp.stack([b, swap_x(b)], axis=1)
    a = jnp.stack([a, swap_core(a)], axis=1)
    b = jnp.stack([b, swap_core(b)], axis=1)
    out = {}
    for whole, parts in ((a, parts_a), (b, parts_b)):
        whole = whole.reshape(2, -1, whole.shape[-1])
        start = 0
        for name, part in parts.items():
            out[name] = whole[:, :, start : start + part.shape[1]]
            start += part.shape[1]
    return out


def reduce_pair(parts_a, parts_b):
    count = lax.axis_size("dp") // 4

    def start_of(parts):
        sends = jnp.concatenate([part[0] for part in parts.values()], axis=2)
        keeps = jnp.concatenate([part[1] for part in parts.values()], axis=2)
        return keeps + swap_core(sends).astype(F32)

    def fold_y(value):
        return value[0] + swap_y(value[1].astype(LOW)).astype(F32)

    def fold_x(value):
        half = value.shape[-2] // 2
        return value[..., :half, :] + swap_x(value[..., half:, :].astype(LOW)).astype(F32)

    a = fold_x(fold_y(start_of(parts_a)))
    b = fold_y(fold_x(start_of(parts_b)))
    both = jnp.concatenate([a, b], axis=1)
    both = both.reshape(count, -1, both.shape[1])
    total = both[count - 1]
    for back in range(count - 2, -1, -1):
        total = both[back] + ring_shift(total.astype(LOW), -1).astype(F32)
    out = {}
    start = 0
    for name, part in list(parts_a.items()) + list(parts_b.items()):
        out[name] = total[:, start : start + part[0].shape[2]]
        start += part[0].shape[2]
    return out


def weight_grad(left, right):
    half = left.shape[1] // 2
    send = jnp.einsum("nd,ync->ydc", left[:, half:], right, preferred_element_type=F32).astype(LOW)
    keep = jnp.einsum("nd,ync->ydc", left[:, :half], right, preferred_element_type=F32)
    return (send, keep)


def norm_layer(value, gain, shift):
    center = value - jnp.mean(value, axis=-1, keepdims=True)
    spread = jnp.mean(center * center, axis=-1, keepdims=True)
    recip = lax.rsqrt(spread + 1e-06)
    normed = center * recip
    return (normed * gain + shift, (normed, recip))


def norm_back(grad, kept, gain):
    normed, recip = kept
    scaled = grad * gain
    d_gain = jnp.sum(grad * normed, axis=0)
    d_shift = jnp.sum(grad, axis=0)
    mean_one = jnp.mean(scaled, axis=-1, keepdims=True)
    mean_two = jnp.mean(scaled * normed, axis=-1, keepdims=True)
    return (recip * (scaled - mean_one - normed * mean_two), d_gain, d_shift)


def heads_of(value):
    return value.reshape(value.shape[0], value.shape[1], -1, HEAD_DIM)


def scores_of(query, keys, same):
    scores = jnp.einsum("yqhe,ykhe->yhqk", query, keys, preferred_element_type=F32)
    return jnp.where(same, scores * HEAD_DIM ** (-0.5), -1000000000.0)


def attend(query, keys, values, same):
    query, keys, values = heads_of(query), heads_of(keys), heads_of(values)
    scores = scores_of(query, keys, same)
    top = jnp.max(scores, axis=-1, keepdims=True)
    expo = jnp.exp(scores - top)
    total = jnp.sum(expo, axis=-1, keepdims=True)
    probs = (expo / total).astype(LOW)
    context = jnp.einsum("yhqk,ykhe->yqhe", probs, values, preferred_element_type=F32)
    context = context.reshape(context.shape[0], context.shape[1], -1).astype(LOW)
    return context, top + jnp.log(total)


def attend_back(query, keys, values, same, logsum, d_context):
    flat = lambda value: value.reshape(value.shape[0], value.shape[1], -1).astype(LOW)
    scale = HEAD_DIM ** (-0.5)
    query, keys, values, d_context = (
        heads_of(query), heads_of(keys), heads_of(values), heads_of(d_context)
    )
    probs = jnp.exp(scores_of(query, keys, same) - logsum)
    d_values = jnp.einsum("yhqk,yqhe->ykhe", probs.astype(LOW), d_context, preferred_element_type=F32)
    d_probs = jnp.einsum("yqhe,ykhe->yhqk", d_context, values, preferred_element_type=F32)
    inner = jnp.sum(probs * d_probs, axis=-1, keepdims=True)
    d_scores = (probs * (d_probs - inner)).astype(LOW)
    d_query = jnp.einsum("yhqk,ykhe->yqhe", d_scores, keys, preferred_element_type=F32) * scale
    d_keys = jnp.einsum("yhqk,yqhe->ykhe", d_scores, query, preferred_element_type=F32) * scale
    return flat(d_query), flat(d_keys), flat(d_values)


def forward_layer(inputs, away, masks, full, biases, norms):
    same_own, same_shared = masks
    n = inputs.shape[0]
    own = n - away.shape[0]
    gains, shifts = norms
    inputs_low = jnp.concatenate([inputs.astype(LOW), away], axis=0)
    project = lambda name: jnp.einsum("nd,ydc->ync", inputs_low, full[name], preferred_element_type=F32)
    query = (project("q")[:, :n] + biases["q"][:, None]).astype(LOW)
    keys = project("k").astype(LOW)
    values = (project("v") + biases["v"][:, None]).astype(LOW)
    context_a, logsum_a = attend(query[:, :own], keys[:, :own], values[:, :own], same_own)
    context_b, logsum_b = attend(query[:, own:], keys[:, own:], values[:, own:], same_shared)
    context = jnp.concatenate([context_a, context_b], axis=1)
    attn = jnp.einsum("ynw,ydw->nd", context, full["out"], preferred_element_type=F32)
    hidden, first_norm = norm_layer(inputs + attn + shifts[0], gains[0], shifts[1])
    hidden_low = hidden.astype(LOW)
    pre = jnp.einsum("nd,ydf->ynf", hidden_low, full["up"], preferred_element_type=F32)
    pre = pre + biases["up"][:, None]
    bell = 0.5 * (1.0 + lax.erf(pre * math.sqrt(0.5)))
    act = (pre * bell).astype(LOW)
    slope = (bell + pre * (jnp.exp(-0.5 * pre * pre) * (1.0 / math.sqrt(2.0 * math.pi)))).astype(LOW)
    ffn = jnp.einsum("ynf,ydf->nd", act, full["down"], preferred_element_type=F32)
    output, second_norm = norm_layer(hidden + ffn + shifts[2], gains[1], shifts[3])
    saved = (
        inputs_low, query, keys, values, logsum_a, logsum_b, context, first_norm, hidden_low,
        act, slope, second_norm,
    )
    return output, saved


def backward_ffn(grad_out, full, norms, saved):
    gains, _ = norms
    (_, _, _, _, _, _, _, first_norm, hidden_low, act, slope, second_norm) = saved
    d_final, d_gain_two, d_shift_three = norm_back(grad_out, second_norm, gains[1])
    d_shift_two = jnp.sum(d_final, axis=0)
    d_final_low = d_final.astype(LOW)
    d_down = weight_grad(d_final_low, act)
    d_act = jnp.einsum("nd,ydf->ynf", d_final_low, full["down"], preferred_element_type=F32)
    d_pre = (d_act * slope.astype(F32)).astype(LOW)
    d_up_bias = jnp.sum(d_pre.astype(F32), axis=1)
    d_up = weight_grad(hidden_low, d_pre)
    d_hidden = d_final + jnp.einsum("ynf,ydf->nd", d_pre, full["up"], preferred_element_type=F32)
    d_mid, d_gain_one, d_shift_one = norm_back(d_hidden, first_norm, gains[0])
    d_shift_zero = jnp.sum(d_mid, axis=0)
    norm_grads = [d_gain_one, d_gain_two, d_shift_zero, d_shift_one, d_shift_two, d_shift_three]
    return d_mid, d_up, d_down, d_up_bias, norm_grads


def backward_attn(d_mid, masks, full, saved):
    same_own, same_shared = masks
    (inputs_low, query, keys, values, logsum_a, logsum_b, context, _, _, _, _, _) = saved
    n = d_mid.shape[0]
    own = n - (inputs_low.shape[0] - n)
    d_mid_low = d_mid.astype(LOW)
    d_out = weight_grad(d_mid_low, context)
    d_context = jnp.einsum("nd,ydw->ynw", d_mid_low, full["out"], preferred_element_type=F32).astype(LOW)
    dq_b, dk_b, dv_b = attend_back(
        query[:, own:], keys[:, own:], values[:, own:], same_shared, logsum_b, d_context[:, own:]
    )
    half = n - own
    back = lambda one, name: jnp.einsum("ync,ydc->nd", one, full[name], preferred_element_type=F32)
    away = back(dk_b[:, half:], "k") + back(dv_b[:, half:], "v")
    from_away = swap_y(away.astype(LOW))
    dq_a, dk_a, dv_a = attend_back(
        query[:, :own], keys[:, :own], values[:, :own], same_own, logsum_a, d_context[:, :own]
    )
    d_query = jnp.concatenate([dq_a, dq_b], axis=1)
    d_keys = jnp.concatenate([dk_a, dk_b], axis=1)
    d_values = jnp.concatenate([dv_a, dv_b], axis=1)
    d_qv_bias = (jnp.sum(d_query.astype(F32), axis=1), jnp.sum(d_values.astype(F32), axis=1))
    grads = {
        "q": weight_grad(inputs_low[:n], d_query),
        "k": weight_grad(inputs_low, d_keys),
        "v": weight_grad(inputs_low, d_values),
        "out": d_out,
    }
    d_inputs = d_mid + back(d_query, "q") + back(d_keys[:, :n], "k") + back(d_values[:, :n], "v")
    d_inputs = jnp.concatenate([d_inputs[:own], d_inputs[own:] + from_away.astype(F32)], axis=0)
    return d_inputs, grads, d_qv_bias


def on_device(
    tokens, segment_ids, out_grad,
    t_qkv, t_qv_bias, t_out, t_up, t_up_bias, t_down, t_gains, t_shifts,
    s_qkv, s_qv_bias, s_out, s_up, s_up_bias, s_down, s_gains, s_shifts,
):
    rows, half, width = tokens.shape
    first = lax.axis_index("mp") == 0

    norm_rows = jnp.concatenate([t_gains, t_shifts, s_gains, s_shifts], axis=0).T
    norm_rows = jnp.pad(norm_rows, ((0, 0), (0, 128 - norm_rows.shape[1])))
    t_full = gather_pair(
        {"q": t_qkv[0], "k": t_qkv[1]}, {"v": t_qkv[2], "out": t_out.T, "norm": norm_rows}
    )
    t_full.update(gather_pair({"up": t_up}, {"down": t_down.T}))
    s_full = gather_pair(
        {"up": s_up, "q": s_qkv[0], "out": s_out.T}, {"down": s_down.T, "k": s_qkv[1], "v": s_qkv[2]}
    )
    norm_all = t_full["norm"][0, :, :12].T.astype(F32)
    t_norms = (norm_all[0:2], norm_all[2:6])
    s_norms = (norm_all[6:8], norm_all[8:12])
    bias_parts = [t_qv_bias[0], t_qv_bias[1], t_up_bias, s_qv_bias[0], s_qv_bias[1], s_up_bias]
    bias_own = jnp.concatenate(bias_parts)
    bias_all = jnp.stack([bias_own, swap_y(bias_own)]).astype(F32)
    cuts = [0]
    for part in bias_parts:
        cuts.append(cuts[-1] + part.shape[0])
    pick = [bias_all[:, cuts[i] : cuts[i + 1]] for i in range(6)]
    t_bias = {"q": pick[0], "v": pick[1], "up": pick[2]}
    s_bias = {"q": pick[3], "v": pick[4], "up": pick[5]}

    to_own = feature_order(width)
    into = (lax.iota(jnp.int32, width)[:, None] == to_own[None, :]).astype(LOW)
    own_row = lambda value: jnp.where(first, value[0], value[2])
    far_row = lambda value: jnp.where(first, value[2], value[0])
    got = swap_y(jnp.stack([far_row(tokens), tokens[1]]))
    local = jnp.concatenate([own_row(tokens), got[0], tokens[1], got[1]], axis=0)
    local = jnp.dot(local, into, preferred_element_type=F32).astype(LOW)
    inputs, away = local[: rows * half].astype(F32), local[rows * half :]
    grad_in = jnp.concatenate([own_row(out_grad), swap_y(far_row(out_grad)), out_grad[1]], axis=0)
    grad_in = jnp.dot(grad_in, into, preferred_element_type=F32)
    spin = lambda segs: jnp.where(first, segs, jnp.roll(segs, half))
    seg_own = spin(own_row(segment_ids))
    seg_shared = spin(segment_ids[1])
    same_own = (seg_own[:, None] == seg_own[None, :])[None, None]
    same_shared = (seg_shared[:half, None] == seg_shared[None, :])[None, None]
    masks = (same_own, same_shared)

    middle, t_saved = forward_layer(inputs, away, masks, t_full, t_bias, t_norms)
    away = swap_y(middle[2 * half :].astype(LOW))
    last, s_saved = forward_layer(middle, away, masks, s_full, s_bias, s_norms)

    def to_rows(value):
        far = swap_y(value[half : 2 * half].astype(LOW))
        mine = jnp.concatenate([value[:half], value[2 * half :]], axis=0)
        high = mine.astype(LOW)
        low = (mine - high.astype(F32)).astype(LOW)
        back = lambda part: jnp.einsum("nd,ed->ne", part, into, preferred_element_type=F32)
        mine = back(high) + back(low)
        far = back(far)
        return jnp.stack([jnp.where(first, mine[:half], far), mine[half:], jnp.where(first, far, mine[:half])])

    output = to_rows(last)

    d_mid, d_up, d_down, s_up_grad, s_norm_grads = backward_ffn(grad_in, s_full, s_norms, s_saved)
    d_first, grads, s_qv_grad = backward_attn(d_mid, masks, s_full, s_saved)
    s_sum = reduce_pair(
        {"up": d_up, "q": grads["q"], "out": grads["out"]}, {"down": d_down, "k": grads["k"], "v": grads["v"]}
    )
    d_mid, d_up, d_down, t_up_grad, t_norm_grads = backward_ffn(d_first, t_full, t_norms, t_saved)
    t_sum = reduce_pair({"up": d_up}, {"down": d_down})
    d_tokens, grads, t_qv_grad = backward_attn(d_mid, masks, t_full, t_saved)
    norm_grads = jnp.stack(t_norm_grads + s_norm_grads)
    norm_cols = jnp.pad(norm_grads, ((0, 128 - norm_grads.shape[0]), (0, 0))).T
    core_half = width // 2
    spread = lambda value: jnp.broadcast_to(value[None], (2,) + value.shape)
    norm_pair = (spread(norm_cols[core_half:].astype(LOW)), spread(norm_cols[:core_half]))
    t_sum.update(
        reduce_pair(
            {"q": grads["q"], "k": grads["k"]}, {"v": grads["v"], "out": grads["out"], "norm": norm_pair}
        )
    )
    input_grad = to_rows(d_tokens)

    bias_grads = jnp.concatenate(
        [t_qv_grad[0], t_qv_grad[1], t_up_grad, s_qv_grad[0], s_qv_grad[1], s_up_grad], axis=1
    )
    bias_sum = lax.psum(bias_grads[0] + swap_y(bias_grads[1]), "dp")
    pick = [bias_sum[cuts[i] : cuts[i + 1]] for i in range(6)]
    norm_sum = t_sum["norm"][:, :12].T
    qkv = lambda sums: jnp.stack([sums["q"], sums["k"], sums["v"]])
    return (
        output, input_grad,
        qkv(t_sum), jnp.stack([pick[0], pick[1]]), t_sum["out"].T, t_sum["up"], pick[2], t_sum["down"].T,
        norm_sum[0:2], norm_sum[2:6],
        qkv(s_sum), jnp.stack([pick[3], pick[4]]), s_sum["out"].T, s_sum["up"], pick[5], s_sum["down"].T,
        norm_sum[6:8], norm_sum[8:12],
    )


def solution(mesh):
    layer = (
        P(None, "dp", "mp"), P(None, "mp"), P("mp", "dp"), P("dp", "mp"), P("mp"), P("mp", "dp"),
        P(None, "dp"), P(None, "dp"),
    )
    rows = P("dp", "mp", None)
    return jax.shard_map(
        on_device,
        mesh=mesh,
        in_specs=(rows, P("dp", None), rows) + layer + layer,
        out_specs=(rows, rows) + layer + layer,
        check_vma=False,
    )
```

```python
import functools
import math

import jax
import jax.numpy as jnp
from jax import lax
from jax.experimental import pallas as pl
from jax.experimental.pallas import tpu as pltpu
from jax.sharding import PartitionSpec as P

HEAD_DIM = 64
LOW = jnp.bfloat16
F32 = jnp.float32


def ring_of(count):
    return list(range(0, count, 2)) + list(range(1, count, 2))[::-1]


def swap_y(value):
    return lax.ppermute(value, "mp", [(0, 1), (1, 0)])


def swap_x(value):
    n = lax.axis_size("dp")
    return lax.ppermute(value, "dp", [(i, i ^ 2) for i in range(n)])


def swap_core(value):
    n = lax.axis_size("dp")
    return lax.ppermute(value, "dp", [(i, i ^ 1) for i in range(n)])


def ring_shift(value, step):
    count = lax.axis_size("dp") // 4
    ring = ring_of(count)
    pairs = []
    for place in range(count):
        for low in range(4):
            pairs.append((ring[place] * 4 + low, ring[(place + step) % count] * 4 + low))
    return lax.ppermute(value, "dp", pairs)


def feature_order(width):
    n = lax.axis_size("dp")
    count, rows = n // 4, width // n
    me = lax.axis_index("dp")
    z, x, core = me // 4, (me // 2) % 2, me % 2
    place = jnp.where(z % 2 == 0, z // 2, count - 1 - z // 2)
    at = lax.iota(jnp.int32, width)
    row = at % rows
    back = (at // rows) % count
    x_rel = (at // (rows * count)) % 2
    core_rel = at // (rows * count * 2)
    from_place = (place - back + count) % count
    half = (count + 1) // 2
    z_abs = jnp.where(from_place < half, 2 * from_place, 2 * (count - 1 - from_place) + 1)
    block = z_abs * 4 + (x ^ x_rel) * 2 + (core ^ core_rel)
    return block * rows + row


def after(value, *others):
    return lax.optimization_barrier((value, others))[0]


VMEM_BYTES = 48 << 20
TILE = 256


def dot(left, right, left_at, right_at):
    return lax.dot_general(
        left, right, (((left_at,), (right_at,)), ((), ())), preferred_element_type=F32
    )


def call(body, steps, inputs, outputs, scratch, flops, exps=0):
    size = lambda shape, dtype: math.prod(shape) * jnp.dtype(dtype).itemsize
    moved = sum(size(array.shape, array.dtype) for array, _, _ in inputs)
    moved += sum(size(shape, dtype) for shape, dtype, _, _ in outputs)
    return pl.pallas_call(
        body,
        grid=(steps,),
        in_specs=[pl.BlockSpec(block, index) for _, block, index in inputs],
        out_specs=[pl.BlockSpec(block, index) for _, _, block, index in outputs],
        out_shape=[jax.ShapeDtypeStruct(shape, dtype) for shape, dtype, _, _ in outputs],
        scratch_shapes=scratch,
        compiler_params=pltpu.CompilerParams(
            dimension_semantics=("arbitrary",), vmem_limit_bytes=VMEM_BYTES
        ),
        cost_estimate=pl.CostEstimate(
            flops=flops, bytes_accessed=moved, transcendentals=exps
        ),
    )(*[array for array, _, _ in inputs])


def whole(array):
    rank = array.ndim
    return (array, array.shape, lambda i: (0,) * rank)


def per_group(array, at=lambda i: i):
    return (array, (1,) + array.shape[1:], lambda i: (at(i),) + (0,) * (array.ndim - 1))


def out_whole(shape, dtype):
    return (shape, dtype, shape, lambda i: (0,) * len(shape))


def out_group(shape, dtype, at=lambda i: i):
    return (shape, dtype, (1,) + shape[1:], lambda i: (at(i),) + (0,) * (len(shape) - 1))


class Layer:
    def __init__(self, every, width, up, down, qkv, out, out_from, norms, bias_qkv, bias_up):
        self.every = every
        self.width, self.up_at, self.down_at = width, up, down
        self.qkv_blocks, self.out_block, self.out_from = qkv, out, out_from
        self.norms, self.bias_qkv, self.bias_up = norms, bias_qkv, bias_up

    def columns(self, block, at):
        size, place = block
        depth = self.every.shape[1]
        return (self.every, (1, depth, size), lambda i: (at(i), 0, place))

    def qkv(self, at=lambda i: i):
        return [self.columns(block, at) for block in self.qkv_blocks]

    def out(self, at=lambda i: i):
        return self.columns(self.out_block, at)

    def ffn(self, base, first):
        size, per = self.bias_up.shape[2], self.bias_up.shape[0] // 2
        depth = self.every.shape[1]

        def index(i):
            step = jnp.maximum(i - first, 0)
            return (step // per, 0, base + step % per)

        return (self.every, (1, depth, size), index)


def put_projection(rows, weights, bias, target):
    start = 0
    wide = target.shape[1]
    for weight in weights:
        cols = min(weight.shape[2], wide - start)
        part = dot(rows, weight[0, :, :cols], 1, 0) + bias[0, :, start : start + cols]
        target[:, start : start + cols] = part.astype(LOW)
        start += cols


def through_projection(grads, weights):
    start = 0
    total = None
    for weight in weights:
        cols = min(weight.shape[2], grads.shape[1] - start)
        part = dot(grads[:, start : start + cols], weight[0, :, :cols], 1, 1)
        total = part if total is None else total + part
        start += cols
    return total


def head_at(width, part, head):
    return slice(part * width + head * HEAD_DIM, part * width + (head + 1) * HEAD_DIM)


def join(parts, cols):
    picked = [part[:, cols] for part in parts]
    return picked[0] if len(picked) == 1 else jnp.concatenate(picked, axis=0)


def attend(width, kept, mask, logsum):
    scale = jnp.asarray(HEAD_DIM**-0.5, LOW)
    out = []
    for head in range(width // HEAD_DIM):
        query = kept[0][:, head_at(width, 0, head)] * scale
        scores = dot(join(kept, head_at(width, 1, head)), query, 1, 1) + mask[...]
        top = jnp.max(scores, axis=0, keepdims=True)
        expo = jnp.exp(scores - top)
        total = jnp.sum(expo, axis=0, keepdims=True)
        out.append(dot(join(kept, head_at(width, 2, head)), expo.astype(LOW), 0, 0) * (1.0 / total))
        logsum[head : head + 1, :] = top + jnp.log(total)
    return jnp.concatenate(out, axis=0).T.astype(LOW)


def attend_back(width, kept, mask, logsum, d_context, grads, sums):
    scale = jnp.asarray(HEAD_DIM**-0.5, LOW)
    for head in range(width // HEAD_DIM):
        at_q, at_k, at_v = (head_at(width, part, head) for part in range(3))
        query = kept[0][:, at_q] * scale
        keys = join(kept, at_k)
        d_ctx = d_context[:, head * HEAD_DIM : (head + 1) * HEAD_DIM]
        probs = jnp.exp(dot(keys, query, 1, 1) + mask[...] - logsum[head : head + 1, :])
        d_probs = dot(join(kept, at_v), d_ctx, 1, 1)
        both = probs * d_probs
        inner = jnp.sum(both, axis=0, keepdims=True)
        d_scores = (both - probs * inner).astype(LOW)
        d_values = dot(probs.astype(LOW), d_ctx, 1, 0).astype(LOW)
        d_keys = dot(d_scores, query, 1, 0).astype(LOW)
        d_query = dot(keys * scale, d_scores, 0, 0).T.astype(LOW)
        grads[0][:, at_q] = d_query
        start = 0
        for grad in grads:
            rows = grad.shape[0]
            grad[:, at_k] = d_keys[start : start + rows]
            grad[:, at_v] = d_values[start : start + rows]
            start += rows
        for grad in grads[1:]:
            grad[:, at_q] = jnp.zeros((grad.shape[0], HEAD_DIM), LOW)
        sums[0:1, at_q] = jnp.sum(d_query.astype(F32), axis=0, keepdims=True)
        sums[0:1, at_k] = jnp.zeros((1, HEAD_DIM), F32)
        sums[0:1, at_v] = jnp.sum(d_values.astype(F32), axis=0, keepdims=True)


def make_mask(segs_q, segs_k, mask):
    @pl.when(pl.program_id(0) == 0)
    def _():
        mask[...] = jnp.where(segs_k[...] == segs_q[...], 0.0, -1e9)


def normalize(value, gain, shift):
    center = value - jnp.mean(value, axis=-1, keepdims=True)
    recip = lax.rsqrt(jnp.mean(center * center, axis=-1, keepdims=True) + 1e-06)
    normed = center * recip
    return normed * gain + shift, normed, recip


def normalize_back(grad, normed, recip, gain):
    scaled = grad * gain
    mean_one = jnp.mean(scaled, axis=-1, keepdims=True)
    mean_two = jnp.mean(scaled * normed, axis=-1, keepdims=True)
    return recip * (scaled - mean_one - normed * mean_two)


def row_tiles(rows):
    return [slice(start, start + TILE) for start in range(0, rows, TILE)]


def project_call(layer, rows_low, segs, half):
    n, depth = rows_low.shape
    width, wide, own = layer.width, 3 * layer.width, 2 * half
    count = len(layer.qkv_blocks)

    def body(rows, *refs):
        weights = refs[:count]
        bias, segs_q, segs_k, proj, context, logsum, mask = refs[count:]
        make_mask(segs_q, segs_k, mask)
        put_projection(rows[...], weights, bias, proj.at[0])
        context[0] = attend(width, [proj.at[0, :own]], mask, logsum.at[0])

    return call(
        body, 2,
        [whole(rows_low)] + layer.qkv() + [
            per_group(layer.bias_qkv), whole(segs[None, :]), whole(segs[:, None])
        ],
        [
            out_group((2, n, wide), LOW), out_group((2, own, width), LOW), out_group((2, 8, own), F32),
        ],
        [pltpu.VMEM((own, own), F32)],
        flops=4 * n * depth * wide + 8 * own * own * width,
        exps=2 * own * own * width // HEAD_DIM,
    )


def rest_call(layer, rows, proj, away_low, context_own, segs, half):
    n, depth = rows.shape
    width, wide, own = layer.width, 3 * layer.width, 2 * half
    count = len(layer.qkv_blocks)
    steps, _, size = layer.bias_up.shape
    per = steps // 2
    group = lambda i: jnp.minimum(i, 1)
    block = lambda i: jnp.maximum(i - 2, 0)

    def body(rows, proj, away, *refs):
        weights = refs[:count]
        (
            out_w, bias, segs_q, segs_k, context_own, norms, up, bias_up, down,
            proj_away, context, logsum, hidden_low, normed_one, recip_one, act, slope,
            output, output_low, normed_two, recip_two,
            mask, hidden, total,
        ) = refs[count:]
        i = pl.program_id(0)
        make_mask(segs_q, segs_k, mask)
        gain = lambda at: norms[at : at + 1, :]

        @pl.when(i < 2)
        def _():
            put_projection(away[...], weights, bias, proj_away.at[0])
            context[0, :own] = context_own[0]
            context[0, own:] = attend(width, [proj.at[0], proj_away.at[0]], mask, logsum.at[0])
            out_cols = out_w[0, :, layer.out_from : layer.out_from + width]
            part = dot(context[0], out_cols, 1, 1)

            @pl.when(i == 0)
            def _():
                total[...] = part

            @pl.when(i == 1)
            def _():
                total[...] += part
                for at in row_tiles(n):
                    value = rows[at, :].astype(F32) + total[at, :] + gain(2)
                    value, normed, recip = normalize(value, gain(0), gain(3))
                    hidden[at, :] = value
                    hidden_low[at, :] = value.astype(LOW)
                    normed_one[at, :] = normed.astype(LOW)
                    recip_one[at, :] = recip

        @pl.when(i >= 2)
        def _():
            for at in row_tiles(n):
                pre = dot(hidden_low[at, :], up[0], 1, 0) + bias_up[0]
                bell = 0.5 + 0.5 * lax.erf(pre * math.sqrt(0.5))
                low = (pre * bell).astype(LOW)
                act[0, at, :] = low
                slope[0, at, :] = (
                    bell + pre * (jnp.exp(-0.5 * pre * pre) * (1.0 / math.sqrt(2.0 * math.pi)))
                ).astype(LOW)
                part = dot(low, down[0], 1, 1)

                @pl.when(i == 2)
                def _():
                    total[at, :] = part

                @pl.when(i > 2)
                def _():
                    total[at, :] += part

        @pl.when(i == steps + 1)
        def _():
            for at in row_tiles(n):
                value = hidden[at, :] + total[at, :] + gain(4)
                value, normed, recip = normalize(value, gain(1), gain(5))
                output[at, :] = value
                output_low[at, :] = value.astype(LOW)
                normed_two[at, :] = normed.astype(LOW)
                recip_two[at, :] = recip

    neurons = per * size
    ffn_out = ((2, n, neurons), LOW, (1, n, size), lambda i: (block(i) // per, 0, block(i) % per))
    return call(
        body, steps + 2,
        [
            whole(rows), (proj, (1, half, wide), lambda i: (group(i), 2, 0)), whole(away_low),
        ] + layer.qkv(group) + [
            layer.out(group), per_group(layer.bias_qkv, group), whole(segs[None, :half]),
            whole(segs[:, None]), per_group(context_own, group), whole(layer.norms),
            layer.ffn(layer.up_at, 2), per_group(layer.bias_up, block), layer.ffn(layer.down_at, 2),
        ],
        [
            out_group((2, half, wide), LOW, group), out_group((2, n, width), LOW, group),
            out_group((2, 8, half), F32, group), out_whole((n, depth), LOW), out_whole((n, depth), LOW),
            out_whole((n, 1), F32), ffn_out, ffn_out, out_whole((n, depth), F32), out_whole((n, depth), LOW),
            out_whole((n, depth), LOW), out_whole((n, 1), F32),
        ],
        [pltpu.VMEM((own, half), F32), pltpu.VMEM((n, depth), F32), pltpu.VMEM((n, depth), F32)],
        flops=4 * depth * (n * width + half * wide + 2 * n * neurons) + 8 * own * half * width,
        exps=2 * own * half * width // HEAD_DIM + 4 * n * neurons,
    )


def add_rows(sums, row, value, at):
    value = jnp.sum(value, axis=0, keepdims=True)
    if at.start == 0:
        sums[row : row + 1, :] = value
    else:
        sums[row : row + 1, :] += value


def ffn_back_call(layer, grad, extra, kept, half):
    n, depth = grad.shape
    steps, _, size = layer.bias_up.shape
    per = steps // 2
    has_extra = extra is not None

    def body(grad, *refs):
        extra = refs[0] if has_extra else None
        (
            normed_one, recip_one, normed_two, recip_two, norms, slope, up, down,
            d_final_low, d_pre, d_mid, d_mid_low, sums, bias_sums, d_final, total,
        ) = refs[1:] if has_extra else refs
        i = pl.program_id(0)
        gain = lambda at: norms[at : at + 1, :]

        @pl.when(i == 0)
        def _():
            sums[...] = jnp.zeros_like(sums)
            for at in row_tiles(n):
                value = grad[at, :].astype(F32)
                if has_extra and at.start >= 2 * half:
                    value = value + extra[at.start - 2 * half : at.stop - 2 * half, :].astype(F32)
                normed = normed_two[at, :].astype(F32)
                back = normalize_back(value, normed, recip_two[at, :], gain(1))
                d_final[at, :] = back
                d_final_low[at, :] = back.astype(LOW)
                add_rows(sums, 1, value * normed, at)
                add_rows(sums, 5, value, at)
                add_rows(sums, 4, back, at)

        bias = None
        for at in row_tiles(n):
            d_act = dot(d_final_low[at, :], down[0], 1, 0)
            low = (d_act * slope[0, at, :].astype(F32)).astype(LOW)
            d_pre[0, at, :] = low
            one = jnp.sum(low.astype(F32), axis=0, keepdims=True)
            bias = one if bias is None else bias + one
            part = dot(low, up[0], 1, 1)

            @pl.when(i == 0)
            def _():
                total[at, :] = part

            @pl.when(i > 0)
            def _():
                total[at, :] += part

        bias_sums[0] = bias

        @pl.when(i == steps - 1)
        def _():
            for at in row_tiles(n):
                value = d_final[at, :] + total[at, :]
                normed = normed_one[at, :].astype(F32)
                back = normalize_back(value, normed, recip_one[at, :], gain(0))
                d_mid[at, :] = back
                d_mid_low[at, :] = back.astype(LOW)
                add_rows(sums, 0, value * normed, at)
                add_rows(sums, 3, value, at)
                add_rows(sums, 2, back, at)

    neurons = per * size
    blocks = ((1, n, size), lambda i: (i // per, 0, i % per))
    return call(
        body, steps,
        [whole(grad)] + ([whole(extra)] if has_extra else []) + [
            whole(kept["normed_one"]), whole(kept["recip_one"]), whole(kept["normed_two"]),
            whole(kept["recip_two"]), whole(layer.norms), (kept["slope"],) + blocks,
            layer.ffn(layer.up_at, 0), layer.ffn(layer.down_at, 0),
        ],
        [
            out_whole((n, depth), LOW), ((2, n, neurons), LOW) + blocks, out_whole((n, depth), F32),
            out_whole((n, depth), LOW), out_whole((8, depth), F32), out_group((steps, 1, size), F32),
        ],
        [pltpu.VMEM((n, depth), F32), pltpu.VMEM((n, depth), F32)],
        flops=8 * n * depth * neurons,
    )


def ffn_back_first_call(layer, grad, extra, kept, half):
    n, depth = grad.shape
    steps, _, size = layer.bias_up.shape
    per = steps // 2

    def body(
        grad, extra, normed_two, recip_two, norms, slope, down,
        d_final, d_final_low, d_pre, sums, bias_sums,
    ):
        i = pl.program_id(0)

        @pl.when(i == 0)
        def _():
            sums[...] = jnp.zeros_like(sums)
            for at in row_tiles(n):
                value = grad[at, :]
                if at.start >= 2 * half:
                    value = value + extra[at.start - 2 * half : at.stop - 2 * half, :].astype(F32)
                normed = normed_two[at, :].astype(F32)
                back = normalize_back(value, normed, recip_two[at, :], norms[1:2, :])
                d_final[at, :] = back
                d_final_low[at, :] = back.astype(LOW)
                add_rows(sums, 1, value * normed, at)
                add_rows(sums, 5, value, at)
                add_rows(sums, 4, back, at)

        bias = None
        for at in row_tiles(n):
            d_act = dot(d_final_low[at, :], down[0], 1, 0)
            low = (d_act * slope[0, at, :].astype(F32)).astype(LOW)
            d_pre[0, at, :] = low
            one = jnp.sum(low.astype(F32), axis=0, keepdims=True)
            bias = one if bias is None else bias + one
        bias_sums[0] = bias

    neurons = per * size
    blocks = ((1, n, size), lambda i: (i // per, 0, i % per))
    return call(
        body, steps,
        [
            whole(grad), whole(extra), whole(kept["normed_two"]), whole(kept["recip_two"]),
            whole(layer.norms), (kept["slope"],) + blocks, layer.ffn(layer.down_at, 0),
        ],
        [
            out_whole((n, depth), F32), out_whole((n, depth), LOW), ((2, n, neurons), LOW) + blocks,
            out_whole((8, depth), F32), out_group((steps, 1, size), F32),
        ],
        [],
        flops=4 * n * depth * neurons,
    )


def ffn_back_second_call(layer, d_final, d_pre, kept):
    n, depth = d_final.shape
    steps, _, size = layer.bias_up.shape
    per = steps // 2

    def body(d_final, d_pre, normed_one, recip_one, norms, up, d_mid, d_mid_low, sums):
        i = pl.program_id(0)
        for at in row_tiles(n):
            part = dot(d_pre[0, at, :], up[0], 1, 1)

            @pl.when(i == 0)
            def _():
                d_mid[at, :] = d_final[at, :] + part

            @pl.when(i > 0)
            def _():
                d_mid[at, :] += part

        @pl.when(i == steps - 1)
        def _():
            sums[...] = jnp.zeros_like(sums)
            for at in row_tiles(n):
                value = d_mid[at, :]
                normed = normed_one[at, :].astype(F32)
                back = normalize_back(value, normed, recip_one[at, :], norms[0:1, :])
                d_mid[at, :] = back
                d_mid_low[at, :] = back.astype(LOW)
                add_rows(sums, 0, value * normed, at)
                add_rows(sums, 3, value, at)
                add_rows(sums, 2, back, at)

    blocks = ((1, n, size), lambda i: (i // per, 0, i % per))
    return call(
        body, steps,
        [
            whole(d_final), (d_pre,) + blocks, whole(kept["normed_one"]), whole(kept["recip_one"]),
            whole(layer.norms), layer.ffn(layer.up_at, 0),
        ],
        [out_whole((n, depth), F32), out_whole((n, depth), LOW), out_whole((8, depth), F32)],
        [],
        flops=4 * n * depth * per * size,
    )


def shared_back_call(layer, d_mid_low, kept, segs, half):
    n, depth = d_mid_low.shape
    width, wide, own = layer.width, 3 * layer.width, 2 * half
    count = len(layer.qkv_blocks)

    def body(d_mid, proj, away, logsum, *refs):
        weights = refs[:count]
        out_w, segs_q, segs_k, d_proj, d_away, sums, back, mask, total = refs[count:]
        i = pl.program_id(0)
        make_mask(segs_q, segs_k, mask)
        out_cols = out_w[0, :, layer.out_from : layer.out_from + width]
        d_context = dot(d_mid[...], out_cols, 1, 0).astype(LOW)
        attend_back(
            width, [proj.at[0], away.at[0]], mask, logsum.at[0], d_context,
            [d_proj.at[0], d_away.at[0]], sums.at[0],
        )
        part = through_projection(d_away[0], weights)

        @pl.when(i == 0)
        def _():
            total[...] = part

        @pl.when(i == 1)
        def _():
            back[...] = (total[...] + part).astype(LOW)

    return call(
        body, 2,
        [
            (d_mid_low, (half, depth), lambda i: (2, 0)), (kept["proj"], (1, half, wide), lambda i: (i, 2, 0)),
            per_group(kept["proj_away"]), per_group(kept["logsum_shared"]),
        ] + layer.qkv() + [layer.out(), whole(segs[None, :half]), whole(segs[:, None])],
        [
            out_group((2, half, wide), LOW), out_group((2, half, wide), LOW), out_group((2, 8, wide), F32),
            out_whole((half, depth), LOW),
        ],
        [pltpu.VMEM((own, half), F32), pltpu.VMEM((half, depth), F32)],
        flops=4 * half * depth * (wide + width) + 20 * own * half * width,
        exps=2 * own * half * width // HEAD_DIM,
    )


def own_back_call(layer, d_mid, d_mid_low, d_shared, kept, segs, half):
    n, depth = d_mid_low.shape
    width, wide, own = layer.width, 3 * layer.width, 2 * half
    count = len(layer.qkv_blocks)

    def body(d_mid, d_mid_low, d_shared, proj, logsum, *refs):
        weights = refs[:count]
        out_w, segs_q, segs_k, d_proj, sums, d_rows, mask = refs[count:]
        i = pl.program_id(0)
        make_mask(segs_q, segs_k, mask)
        out_cols = out_w[0, :, layer.out_from : layer.out_from + width]
        d_context = dot(d_mid_low[...], out_cols, 1, 0).astype(LOW)
        attend_back(
            width, [proj.at[0]], mask, logsum.at[0], d_context, [d_proj.at[0, :own]], sums.at[0]
        )
        d_proj[0, own:] = d_shared[0]
        part = through_projection(d_proj[0], weights)

        @pl.when(i == 0)
        def _():
            d_rows[...] = d_mid[...] + part

        @pl.when(i == 1)
        def _():
            d_rows[...] += part

    return call(
        body, 2,
        [
            whole(d_mid), (d_mid_low, (own, depth), lambda i: (0, 0)), per_group(d_shared),
            (kept["proj"], (1, own, wide), lambda i: (i, 0, 0)), per_group(kept["logsum_own"]),
        ] + layer.qkv() + [layer.out(), whole(segs[None, :]), whole(segs[:, None])],
        [
            out_group((2, n, wide), LOW), out_group((2, 8, wide), F32), out_whole((n, depth), F32),
        ],
        [pltpu.VMEM((own, own), F32)],
        flops=4 * depth * (n * wide + own * width) + 20 * own * own * width,
        exps=2 * own * own * width // HEAD_DIM,
    )


class Grads:
    def __init__(self, entries, columns, cut):
        self.entries, self.columns, self.cut = entries, columns, cut
        sizes = [end - start for _, start, end in columns]
        self.size_a, self.size_b = sum(sizes[:cut]), sum(sizes[cut:])

    def inputs(self, at):
        out = []
        for pairs in self.entries:
            for left, right in pairs:
                out += [whole(left), per_group(right, at)]
        return out

    def scratch(self, rows):
        return [pltpu.VMEM((rows, left.shape[0]), LOW) for pairs in self.entries for left, _ in pairs]

    def flops(self, rows):
        depth = self.entries[0][0][0].shape[1]
        return sum(
            2 * rows * left.shape[0] * (2 * right.shape[2] + depth)
            for pairs in self.entries for left, right in pairs
        )

    def turn(self, pick, refs, turned):
        @pl.when(pl.program_id(0) == 0)
        def _():
            for at in range(len(turned)):
                turned[at][...] = dot(pick[...], refs[2 * at][...], 1, 1).astype(LOW)

    def product(self, refs, turned, entry, start, end):
        first = sum(len(pairs) for pairs in self.entries[:entry])
        total = None
        for at in range(first, first + len(self.entries[entry])):
            one = dot(turned[at][...], refs[2 * at + 1][0, :, start:end], 1, 0)
            total = one if total is None else total + one
        return total

    def send(self, pick):
        rows = pick.shape[0]
        size = self.size_a + self.size_b

        def body(pick, *refs):
            count = 2 * sum(len(pairs) for pairs in self.entries)
            out, turned = refs[count], refs[count + 1 :]
            self.turn(pick, refs, turned)
            col = 0
            for entry, start, end in self.columns:
                part = self.product(refs, turned, entry, start, end)
                out[0, :, col : col + end - start] = part.astype(LOW)
                col += end - start

        return call(
            body, 2, [whole(pick)] + self.inputs(lambda i: i), [out_group((2, rows, size), LOW)],
            self.scratch(rows), self.flops(rows),
        )[0]

    def keep(self, pick, got, group):
        rows = pick.shape[0]
        half = rows // 2
        size = self.size_a + self.size_b
        order = jnp.stack([1 - group, group]).astype(jnp.int32)

        def body(order, pick, got, *refs):
            count = 2 * sum(len(pairs) for pairs in self.entries)
            send_a, keep_a, send_b, keep_b = refs[count : count + 4]
            turned = refs[count + 4 :]
            i = pl.program_id(0)
            self.turn(pick, refs, turned)
            col = 0
            for at, (entry, start, end) in enumerate(self.columns):
                part = self.product(refs, turned, entry, start, end)
                part = part + got[0, :, col : col + end - start].astype(F32)
                if at < self.cut:
                    place = slice(col, col + end - start)

                    @pl.when(i == 0)
                    def _():
                        send_a[:, place] = part.astype(LOW)

                    @pl.when(i == 1)
                    def _():
                        keep_a[:, place] = part
                else:
                    place = slice(col - self.size_a, col - self.size_a + end - start)
                    keep_b[0, :, place] = part[:half]
                    send_b[0, :, place] = part[half:].astype(LOW)
                col += end - start

        inputs = [whole(pick), per_group(got, None)] + self.inputs(None)
        specs = []
        for array, block, index in inputs:
            rank = array.ndim
            if rank == 3:
                specs.append(pl.BlockSpec(block, lambda i, order: (order[i], 0, 0)))
            else:
                specs.append(pl.BlockSpec(block, lambda i, order: (0, 0)))
        flat = lambda shape: pl.BlockSpec(shape, lambda i, order: (0, 0))
        each = lambda shape: pl.BlockSpec((1,) + shape, lambda i, order: (i, 0, 0))
        return pl.pallas_call(
            body,
            grid_spec=pltpu.PrefetchScalarGridSpec(
                num_scalar_prefetch=1,
                grid=(2,),
                in_specs=specs,
                out_specs=[
                    flat((rows, self.size_a)), flat((rows, self.size_a)),
                    each((half, self.size_b)), each((half, self.size_b)),
                ],
                scratch_shapes=self.scratch(rows),
            ),
            out_shape=[
                jax.ShapeDtypeStruct((rows, self.size_a), LOW), jax.ShapeDtypeStruct((rows, self.size_a), F32),
                jax.ShapeDtypeStruct((2, half, self.size_b), LOW),
                jax.ShapeDtypeStruct((2, half, self.size_b), F32),
            ],
            compiler_params=pltpu.CompilerParams(
                dimension_semantics=("arbitrary",), vmem_limit_bytes=VMEM_BYTES
            ),
            cost_estimate=pl.CostEstimate(
                flops=self.flops(rows), bytes_accessed=10 * rows * size, transcendentals=0
            ),
        )(order, *[array for array, _, _ in inputs])


class Reduce:
    def __init__(self, grads, pick_send, pick_keep):
        self.grads, self.pick_keep = grads, pick_keep
        self.sends = (grads.send(pick_send),)
        self.got = (swap_core(self.sends[0]),)
        self.work = self._run()

    def _run(self):
        count = lax.axis_size("dp") // 4
        send_a, keep_a, send_b, keep_b = self.grads.keep(self.pick_keep, self.got[0], lax.axis_index("mp"))
        fourth = keep_a.shape[0] // 2
        self.sends = (send_a, send_b)
        self.got = (swap_y(send_a), swap_x(send_b))
        yield
        a = keep_a + self.got[0].astype(F32)
        b = keep_b + self.got[1].astype(F32)
        self.sends = (a[fourth:].astype(LOW), b[0].astype(LOW))
        self.got = (swap_x(self.sends[0]), swap_y(self.sends[1]))
        a, b = a[:fourth], b[1]
        yield
        both = jnp.concatenate([a + self.got[0].astype(F32), b + self.got[1].astype(F32)], axis=1)
        both = both.reshape((count, -1) + both.shape[1:])
        total = both[count - 1]
        for back in range(count - 2, -1, -1):
            self.sends = (total.astype(LOW),)
            self.got = (ring_shift(self.sends[0], -1),)
            yield
            total = both[back] + self.got[0].astype(F32)
        self.total = total
        self.got = self.sends = ()

    def step(self):
        next(self.work, None)


class Total:
    def __init__(self, value):
        self.total = value
        self.work = self._run()
        self.step()

    def _run(self):
        n = lax.axis_size("dp")
        self.sends = (self.total,)
        self.got = (swap_y(self.total),)
        yield
        self.total = self.total + self.got[0]
        step = 1
        while step < n:
            self.sends = (self.total,)
            self.got = (lax.ppermute(self.total, "dp", [(i, i ^ step) for i in range(n)]),)
            yield
            self.total = self.total + self.got[0]
            step *= 2
        self.got = self.sends = ()

    def step(self):
        next(self.work, None)


def round_of(*works):
    ended = lax.optimization_barrier(tuple(work.got for work in works))
    for work, got in zip(works, ended):
        work.got = got
    for work in works:
        work.step()


def before(value, *works):
    value, ended = lax.optimization_barrier((value, tuple(work.got for work in works)))
    for work, got in zip(works, ended):
        work.got = got
    return value


def forward_layer(layer, rows, rows_low, away_low, segs, half):
    proj, context_own, logsum_own = project_call(layer, rows_low, segs[0], half)
    away_low = away_low()
    (
        proj_away, context, logsum_shared, hidden_low, normed_one, recip_one, act, slope, output,
        output_low, normed_two, recip_two,
    ) = rest_call(layer, rows, proj, away_low, context_own, segs[1], half)
    kept = dict(
        rows_low=rows_low, away_low=away_low, proj=proj, proj_away=proj_away, context=context,
        logsum_own=logsum_own, logsum_shared=logsum_shared, hidden_low=hidden_low,
        normed_one=normed_one, recip_one=recip_one, act=act, slope=slope, normed_two=normed_two,
        recip_two=recip_two,
    )
    return output, output_low, kept


def backward_ffn(layer, grad, extra, kept, half):
    d_final_low, d_pre, d_mid, d_mid_low, sums, bias_sums = ffn_back_call(layer, grad, extra, kept, half)
    per = bias_sums.shape[0] // 2
    entries = [[(kept["hidden_low"], d_pre)], [(d_final_low, kept["act"])]]
    return d_mid, d_mid_low, sums[:6], bias_sums.reshape(2, per * bias_sums.shape[2]), entries


def attn_entries(kept, d_proj, d_away, d_mid_low):
    return [[(kept["rows_low"], d_proj), (kept["away_low"], d_away)], [(d_mid_low, kept["context"])]]


def on_device(
    tokens, segment_ids, out_grad,
    t_qkv, t_qv_bias, t_out, t_up, t_up_bias, t_down, t_gains, t_shifts,
    s_qkv, s_qv_bias, s_out, s_up, s_up_bias, s_down, s_gains, s_shifts,
):
    rows, half, width = tokens.shape
    group = lax.axis_index("mp")
    first = group == 0
    own_row = lambda value: jnp.where(first, value[0], value[2])
    far_row = lambda value: jnp.where(first, value[2], value[0])

    norm_rows = jnp.concatenate([t_gains, t_shifts, s_gains, s_shifts], axis=0).T
    norm_rows = jnp.pad(norm_rows, ((0, 0), (0, 128 - norm_rows.shape[1])))
    t_width, s_width = t_qkv.shape[2], s_qkv.shape[2]
    weight_parts = [
        t_up, t_down.T, t_qkv[0], t_qkv[1], t_qkv[2], t_out.T,
        s_up, s_down.T, s_qkv[0], s_qkv[1], s_qkv[2], s_out.T, norm_rows,
    ]
    every = lax.all_gather(jnp.concatenate(weight_parts, axis=1), ("mp", "dp"), axis=0, tiled=True)
    every = every.reshape(2, width, -1)
    norms = every[0, :, -128:-116].T.astype(F32)
    norms_of = lambda at: jnp.pad(norms[at : at + 6], ((0, 2), (0, 0)))

    bias_parts = [t_qv_bias[0], t_qv_bias[1], t_up_bias, s_qv_bias[0], s_qv_bias[1], s_up_bias]
    bias_own = jnp.concatenate(bias_parts)
    bias_far = swap_y(bias_own)
    bias_all = jnp.where(first, jnp.stack([bias_own, bias_far]), jnp.stack([bias_far, bias_own])).astype(F32)
    cuts = [0]
    for part in bias_parts:
        cuts.append(cuts[-1] + part.shape[0])
    pick = [bias_all[:, cuts[i] : cuts[i + 1]] for i in range(6)]
    bias_qkv = lambda q, v: jnp.concatenate([q, jnp.zeros_like(q), v], axis=1)[:, None, :]

    size = s_up.shape[1]
    per = t_up.shape[1] // size
    t_end = t_up.shape[1] + t_down.shape[0] + 4 * t_width
    t_ffn = t_up.shape[1] + t_down.shape[0]
    s_ffn = t_end + s_up.shape[1] + s_down.shape[0]
    teacher = Layer(
        every, t_width, 0, per, [(t_width, t_ffn // t_width + i) for i in range(3)],
        (t_width, t_ffn // t_width + 3), 0, norms_of(0), bias_qkv(pick[0], pick[1]),
        pick[2].reshape(2 * per, 1, size),
    )
    student = Layer(
        every, s_width, t_end // size, t_end // size + 1, [(4 * s_width, s_ffn // (4 * s_width))],
        (4 * s_width, s_ffn // (4 * s_width)), 3 * s_width, norms_of(6), bias_qkv(pick[3], pick[4]),
        pick[5].reshape(2, 1, size),
    )

    to_own = feature_order(width)
    pick_all = (lax.iota(jnp.int32, width)[None, :] == to_own[:, None]).astype(LOW)
    pick_keep, pick_send = pick_all[: width // 2], pick_all[width // 2 :]

    got = swap_y(jnp.stack([far_row(tokens), tokens[1]]))
    inputs = jnp.concatenate([own_row(tokens), got[0], tokens[1]], axis=0)
    grad_in = jnp.concatenate([own_row(out_grad), swap_y(far_row(out_grad)), out_grad[1]], axis=0)
    spin = lambda segs: jnp.where(first, segs, jnp.roll(segs, half))
    segs = (spin(own_row(segment_ids)), spin(segment_ids[1]))

    middle, middle_low, t_kept = forward_layer(teacher, inputs, inputs, lambda: got[1], segs, half)
    last, _, s_kept = forward_layer(
        student, middle, middle_low, lambda: swap_y(middle_low[2 * half :]), segs, half
    )

    def to_rows(value):
        far = swap_y(value[half : 2 * half].astype(LOW)).astype(F32)
        near = value[:half]
        return jnp.stack([jnp.where(first, near, far), value[2 * half :], jnp.where(first, far, near)])

    output = to_rows(last)

    d_mid, d_mid_low, s_norm_grads, s_up_grad, s_entries = backward_ffn(student, grad_in, None, s_kept, half)
    d_shared, d_away, s_sums_b, back = shared_back_call(student, d_mid_low, s_kept, segs[1], half)
    extra = swap_y(back)
    d_proj, s_sums_a, d_rows = own_back_call(student, d_mid, d_mid_low, d_shared, s_kept, segs[0], half)
    d_proj, extra = lax.optimization_barrier((d_proj, extra))
    s_entries += attn_entries(s_kept, d_proj, d_away, d_mid_low)
    s_columns = [(0, 0, size), (2, 0, s_width), (3, 0, s_width), (1, 0, size), (2, s_width, 3 * s_width)]
    reduce_s = Reduce(Grads(s_entries, s_columns, 3), pick_send, pick_keep)

    d_rows = after(d_rows, reduce_s.sends)
    d_final, d_final_low, d_pre, t_sums_two, t_up_grad = ffn_back_first_call(
        teacher, d_rows, extra, t_kept, half
    )
    t_up_grad = t_up_grad.reshape(2, -1)
    d_pre = before(d_pre, reduce_s)
    reduce_s.step()
    d_pre = after(d_pre, reduce_s.sends)
    f_entries = [[(t_kept["hidden_low"], d_pre)], [(d_final_low, t_kept["act"])]]
    reduce_f = Reduce(
        Grads(f_entries, [(0, 0, per * size), (1, 0, per * size)], 1), pick_send, pick_keep
    )
    d_pre = after(d_pre, reduce_f.sends)
    d_mid, d_mid_low, t_sums_one = ffn_back_second_call(teacher, d_final, d_pre, t_kept)
    t_norm_grads = (t_sums_one + t_sums_two)[:6]
    d_mid_low = before(d_mid_low, reduce_s)
    reduce_s.step()
    d_mid_low = after(before(d_mid_low, reduce_f), reduce_s.sends)
    reduce_f.step()
    d_mid_low = after(d_mid_low, reduce_f.sends)
    d_shared, d_away, t_sums_b, back = shared_back_call(teacher, d_mid_low, t_kept, segs[1], half)
    extra = swap_y(back)
    d_shared = before(d_shared, reduce_s)
    reduce_s.step()
    d_shared = after(d_shared, reduce_s.sends)
    d_proj, t_sums_a, d_rows = own_back_call(teacher, d_mid, d_mid_low, d_shared, t_kept, segs[0], half)
    d_proj = before(d_proj, reduce_f, reduce_s)
    reduce_f.step()
    reduce_s.step()
    d_proj = after(d_proj, reduce_f.sends)
    t_entries = attn_entries(t_kept, d_proj, d_away, d_mid_low)
    reduce_t = Reduce(
        Grads(t_entries, [(0, 0, 2 * t_width), (0, 2 * t_width, 3 * t_width), (1, 0, t_width)], 1),
        pick_send, pick_keep,
    )
    d_rows = jnp.concatenate([d_rows[: 2 * half], d_rows[2 * half :] + extra.astype(F32)], axis=0)
    input_grad = to_rows(d_rows)

    def qv_grad(first, second, wide):
        sums = first[:, 0] + second[:, 0]
        return [sums[:, :wide], sums[:, 2 * wide :]]

    small = jnp.concatenate([t_norm_grads, s_norm_grads], axis=0).reshape(-1)
    bias_grads = jnp.concatenate(
        qv_grad(t_sums_a, t_sums_b, t_width) + [t_up_grad]
        + qv_grad(s_sums_a, s_sums_b, s_width) + [s_up_grad], axis=1,
    )
    small = Total(jnp.concatenate([small, bias_grads.reshape(-1)]))
    for _ in range(6):
        round_of(reduce_t, reduce_f, reduce_s, small)
    for work in (reduce_t, reduce_f, reduce_s, small):
        while work.got:
            work.step()
    s_sum, f_sum, t_sum, small = reduce_s.total, reduce_f.total, reduce_t.total, small.total

    piece = width // lax.axis_size("dp")
    norm_sum = small[: 12 * width].reshape(12, width)
    norm_sum = lax.dynamic_slice_in_dim(norm_sum, lax.axis_index("dp") * piece, piece, 1)
    bias_sum = small[12 * width :].reshape(2, -1)
    bias_sum = jnp.where(first, bias_sum[0], bias_sum[1])
    pick = [bias_sum[cuts[i] : cuts[i + 1]] for i in range(6)]

    def cut(value, *sizes):
        out = []
        for one in sizes:
            out.append(value[:, :one])
            value = value[:, one:]
        return out

    tq, tk, tv, to = cut(t_sum, t_width, t_width, t_width, t_width)
    t_up_sum, t_down_sum = cut(f_sum, per * size, per * size)
    s_up_sum, sq, so, s_down_sum, sk, sv = cut(s_sum, size, s_width, s_width, size, s_width, s_width)
    return (
        output, input_grad,
        jnp.stack([tq, tk, tv]), jnp.stack([pick[0], pick[1]]), to.T, t_up_sum, pick[2], t_down_sum.T,
        norm_sum[0:2], norm_sum[2:6],
        jnp.stack([sq, sk, sv]), jnp.stack([pick[3], pick[4]]), so.T, s_up_sum, pick[5], s_down_sum.T,
        norm_sum[6:8], norm_sum[8:12],
    )


def solution(mesh):
    layer = (
        P(None, "dp", "mp"), P(None, "mp"), P("mp", "dp"), P("dp", "mp"), P("mp"), P("mp", "dp"),
        P(None, "dp"), P(None, "dp"),
    )
    rows = P("dp", "mp", None)
    return jax.shard_map(
        on_device,
        mesh=mesh,
        in_specs=(rows, P("dp", None), rows) + layer + layer,
        out_specs=(rows, rows) + layer + layer,
        check_vma=False,
    )
```

```python
import functools
import math

import jax
import jax.numpy as jnp
from jax import lax
from jax.experimental import pallas as pl
from jax.experimental.pallas import tpu as pltpu
from jax.sharding import PartitionSpec as P

HEAD_DIM = 64
LOW = jnp.bfloat16
F32 = jnp.float32


def ring_of(count):
    return list(range(0, count, 2)) + list(range(1, count, 2))[::-1]


def swap_y(value):
    return lax.ppermute(value, "mp", [(0, 1), (1, 0)])


def swap_x(value):
    n = lax.axis_size("dp")
    return lax.ppermute(value, "dp", [(i, i ^ 2) for i in range(n)])


def swap_core(value):
    n = lax.axis_size("dp")
    return lax.ppermute(value, "dp", [(i, i ^ 1) for i in range(n)])


def ring_shift(value, step):
    count = lax.axis_size("dp") // 4
    ring = ring_of(count)
    pairs = []
    for place in range(count):
        for low in range(4):
            pairs.append((ring[place] * 4 + low, ring[(place + step) % count] * 4 + low))
    return lax.ppermute(value, "dp", pairs)


def feature_order(width):
    n = lax.axis_size("dp")
    count, rows = n // 4, width // n
    me = lax.axis_index("dp")
    z, x, core = me // 4, (me // 2) % 2, me % 2
    place = jnp.where(z % 2 == 0, z // 2, count - 1 - z // 2)
    at = lax.iota(jnp.int32, width)
    row = at % rows
    back = (at // rows) % count
    x_rel = (at // (rows * count)) % 2
    core_rel = at // (rows * count * 2)
    from_place = (place - back + count) % count
    half = (count + 1) // 2
    z_abs = jnp.where(from_place < half, 2 * from_place, 2 * (count - 1 - from_place) + 1)
    block = z_abs * 4 + (x ^ x_rel) * 2 + (core ^ core_rel)
    return block * rows + row


def after(value, *others):
    return lax.optimization_barrier((value, others))[0]


VMEM_BYTES = 48 << 20
TILE = 256


def dot(left, right, left_at, right_at):
    return lax.dot_general(
        left, right, (((left_at,), (right_at,)), ((), ())), preferred_element_type=F32
    )


def call(body, steps, inputs, outputs, scratch, flops, exps=0):
    size = lambda shape, dtype: math.prod(shape) * jnp.dtype(dtype).itemsize
    moved = sum(size(array.shape, array.dtype) for array, _, _ in inputs)
    moved += sum(size(shape, dtype) for shape, dtype, _, _ in outputs)
    return pl.pallas_call(
        body,
        grid=(steps,),
        in_specs=[pl.BlockSpec(block, index) for _, block, index in inputs],
        out_specs=[pl.BlockSpec(block, index) for _, _, block, index in outputs],
        out_shape=[jax.ShapeDtypeStruct(shape, dtype) for shape, dtype, _, _ in outputs],
        scratch_shapes=scratch,
        compiler_params=pltpu.CompilerParams(
            dimension_semantics=("arbitrary",), vmem_limit_bytes=VMEM_BYTES
        ),
        cost_estimate=pl.CostEstimate(
            flops=flops // 2, bytes_accessed=moved // 2, transcendentals=exps // 2
        ),
    )(*[array for array, _, _ in inputs])


def whole(array):
    rank = array.ndim
    return (array, array.shape, lambda i: (0,) * rank)


def per_group(array, at=lambda i: i):
    return (array, (1,) + array.shape[1:], lambda i: (at(i),) + (0,) * (array.ndim - 1))


def out_whole(shape, dtype):
    return (shape, dtype, shape, lambda i: (0,) * len(shape))


def out_group(shape, dtype, at=lambda i: i):
    return (shape, dtype, (1,) + shape[1:], lambda i: (at(i),) + (0,) * (len(shape) - 1))


class Layer:
    def __init__(self, width, up, down, qkv, out, out_from, norms, bias_qkv, bias_up):
        self.width, self.up, self.down = width, up, down
        self.qkv_blocks, self.out_block, self.out_from = qkv, out, out_from
        self.norms, self.bias_qkv, self.bias_up = norms, bias_qkv, bias_up
        self.used = [block[3] for block in qkv]

    def columns(self, block, at):
        pair, size, place, _ = block
        return [(half, (1, half.shape[1], size), lambda i: (at(i), 0, place)) for half in pair]

    def qkv(self, at=lambda i: i):
        return [one for block in self.qkv_blocks for one in self.columns(block, at)]

    def out(self, at=lambda i: i):
        return self.columns(self.out_block, at)

    def ffn(self, pair):
        size, per = self.bias_up.shape[2], self.bias_up.shape[0] // 2
        return [(half, (1, half.shape[1], size), lambda i: (i // per, 0, i % per)) for half in pair]


def joined(pair, cols=slice(None)):
    return jnp.concatenate([half[0, :, cols] for half in pair], axis=0)


def pairs_of(refs):
    return [refs[at : at + 2] for at in range(0, len(refs), 2)]


def put_projection(rows, weights, used, bias, target):
    start = 0
    for weight, cols in zip(weights, used):
        part = dot(rows, joined(weight, slice(0, cols)), 1, 0) + bias[0, :, start : start + cols]
        target[:, start : start + cols] = part.astype(LOW)
        start += cols


def through_projection(grads, weights, used):
    start = 0
    total = None
    for weight, cols in zip(weights, used):
        part = dot(grads[:, start : start + cols], joined(weight, slice(0, cols)), 1, 1)
        total = part if total is None else total + part
        start += cols
    return total


def head_at(width, part, head):
    return slice(part * width + head * HEAD_DIM, part * width + (head + 1) * HEAD_DIM)


def join(parts, cols):
    picked = [part[:, cols] for part in parts]
    return picked[0] if len(picked) == 1 else jnp.concatenate(picked, axis=0)


def attend(width, kept, mask, logsum):
    scale = jnp.asarray(HEAD_DIM**-0.5, LOW)
    out = []
    for head in range(width // HEAD_DIM):
        query = kept[0][:, head_at(width, 0, head)] * scale
        scores = dot(join(kept, head_at(width, 1, head)), query, 1, 1) + mask[...]
        top = jnp.max(scores, axis=0, keepdims=True)
        expo = jnp.exp(scores - top)
        total = jnp.sum(expo, axis=0, keepdims=True)
        out.append(dot(join(kept, head_at(width, 2, head)), expo.astype(LOW), 0, 0) * (1.0 / total))
        logsum[head : head + 1, :] = top + jnp.log(total)
    return jnp.concatenate(out, axis=0).T.astype(LOW)


def attend_back(width, kept, mask, logsum, d_context, grads, sums):
    scale = jnp.asarray(HEAD_DIM**-0.5, LOW)
    for head in range(width // HEAD_DIM):
        at_q, at_k, at_v = (head_at(width, part, head) for part in range(3))
        query = kept[0][:, at_q] * scale
        keys = join(kept, at_k)
        d_ctx = d_context[:, head * HEAD_DIM : (head + 1) * HEAD_DIM]
        probs = jnp.exp(dot(keys, query, 1, 1) + mask[...] - logsum[head : head + 1, :])
        d_probs = dot(join(kept, at_v), d_ctx, 1, 1)
        both = probs * d_probs
        inner = jnp.sum(both, axis=0, keepdims=True)
        d_scores = (both - probs * inner).astype(LOW)
        d_values = dot(probs.astype(LOW), d_ctx, 1, 0).astype(LOW)
        d_keys = dot(d_scores, query, 1, 0).astype(LOW)
        d_query = dot(keys * scale, d_scores, 0, 0).T.astype(LOW)
        grads[0][:, at_q] = d_query
        start = 0
        for grad in grads:
            rows = grad.shape[0]
            grad[:, at_k] = d_keys[start : start + rows]
            grad[:, at_v] = d_values[start : start + rows]
            start += rows
        for grad in grads[1:]:
            grad[:, at_q] = jnp.zeros((grad.shape[0], HEAD_DIM), LOW)
        sums[0:1, at_q] = jnp.sum(d_query.astype(F32), axis=0, keepdims=True)
        sums[0:1, at_k] = jnp.zeros((1, HEAD_DIM), F32)
        sums[0:1, at_v] = jnp.sum(d_values.astype(F32), axis=0, keepdims=True)


def make_mask(segs_q, segs_k, mask):
    @pl.when(pl.program_id(0) == 0)
    def _():
        mask[...] = jnp.where(segs_k[...] == segs_q[...], 0.0, -1e9)


def normalize(value, gain, shift):
    center = value - jnp.mean(value, axis=-1, keepdims=True)
    recip = lax.rsqrt(jnp.mean(center * center, axis=-1, keepdims=True) + 1e-06)
    normed = center * recip
    return normed * gain + shift, normed, recip


def normalize_back(grad, normed, recip, gain):
    scaled = grad * gain
    mean_one = jnp.mean(scaled, axis=-1, keepdims=True)
    mean_two = jnp.mean(scaled * normed, axis=-1, keepdims=True)
    return recip * (scaled - mean_one - normed * mean_two)


def row_tiles(rows):
    return [slice(start, start + TILE) for start in range(0, rows, TILE)]


def project_call(layer, rows_low, segs, half):
    n, depth = rows_low.shape
    width, wide, own = layer.width, 3 * layer.width, 2 * half
    count = 2 * len(layer.qkv_blocks)

    def body(rows, *refs):
        weights = pairs_of(refs[:count])
        bias, segs_q, segs_k, proj, context, logsum, mask = refs[count:]
        make_mask(segs_q, segs_k, mask)
        put_projection(rows[...], weights, layer.used, bias, proj.at[0])
        context[0] = attend(width, [proj.at[0, :own]], mask, logsum.at[0])

    return call(
        body, 2,
        [whole(rows_low)] + layer.qkv() + [
            per_group(layer.bias_qkv), whole(segs[None, :]), whole(segs[:, None])
        ],
        [
            out_group((2, n, wide), LOW), out_group((2, own, width), LOW), out_group((2, 8, own), F32),
        ],
        [pltpu.VMEM((own, own), F32)],
        flops=4 * n * depth * wide + 8 * own * own * width,
        exps=2 * own * own * width // HEAD_DIM,
    )


def shared_call(layer, rows, proj, away_low, context_own, segs, half):
    n, depth = rows.shape
    width, wide, own = layer.width, 3 * layer.width, 2 * half
    count = 2 * len(layer.qkv_blocks)

    def body(rows, proj, away, *refs):
        weights = pairs_of(refs[:count])
        (
            out_one, out_two, bias, segs_q, segs_k, context_own, norms,
            proj_away, context, logsum, hidden, hidden_low, normed_one, recip_one, mask, total,
        ) = refs[count:]
        i = pl.program_id(0)
        make_mask(segs_q, segs_k, mask)
        put_projection(away[...], weights, layer.used, bias, proj_away.at[0])
        context[0, :own] = context_own[0]
        context[0, own:] = attend(width, [proj.at[0], proj_away.at[0]], mask, logsum.at[0])
        out_cols = joined((out_one, out_two), slice(layer.out_from, layer.out_from + width))

        @pl.when(i == 0)
        def _():
            total[...] = dot(context[0], out_cols, 1, 1)

        @pl.when(i == 1)
        def _():
            for at in row_tiles(n):
                value = rows[at, :].astype(F32) + norms[2:3, :]
                value = value + (total[at, :] + dot(context[0, at], out_cols, 1, 1))
                value, normed, recip = normalize(value, norms[0:1, :], norms[3:4, :])
                hidden[at, :] = value
                hidden_low[at, :] = value.astype(LOW)
                normed_one[at, :] = normed.astype(LOW)
                recip_one[at, :] = recip

    return call(
        body, 2,
        [
            whole(rows), (proj, (1, half, wide), lambda i: (i, 2, 0)), whole(away_low),
        ] + layer.qkv() + layer.out() + [
            per_group(layer.bias_qkv), whole(segs[None, :half]),
            whole(segs[:, None]), per_group(context_own), whole(layer.norms),
        ],
        [
            out_group((2, half, wide), LOW), out_group((2, n, width), LOW), out_group((2, 8, half), F32),
            out_whole((n, depth), F32), out_whole((n, depth), LOW), out_whole((n, depth), LOW),
            out_whole((n, 1), F32),
        ],
        [pltpu.VMEM((own, half), F32), pltpu.VMEM((n, depth), F32)],
        flops=4 * depth * (n * width + half * wide) + 8 * own * half * width,
        exps=2 * own * half * width // HEAD_DIM,
    )


def ffn_call(layer, hidden, hidden_low):
    n, depth = hidden.shape
    steps, _, size = layer.bias_up.shape
    per = steps // 2

    def body(
        hidden, hidden_low, norms, bias_up, up_one, up_two, down_one, down_two,
        act, slope, output, output_low, normed_two, recip_two,
    ):
        i = pl.program_id(0)

        @pl.when(i == 0)
        def _():
            output[...] = hidden[...] + norms[4:5, :]

        up, down = joined((up_one, up_two)), joined((down_one, down_two))
        for at in row_tiles(n):
            pre = dot(hidden_low[at, :], up, 1, 0) + bias_up[0]
            bell = 0.5 + 0.5 * lax.erf(pre * math.sqrt(0.5))
            low = (pre * bell).astype(LOW)
            act[0, at, :] = low
            slope[0, at, :] = (
                bell + pre * (jnp.exp(-0.5 * pre * pre) * (1.0 / math.sqrt(2.0 * math.pi)))
            ).astype(LOW)
            output[at, :] += dot(low, down, 1, 1)

        @pl.when(i == steps - 1)
        def _():
            for at in row_tiles(n):
                value, normed, recip = normalize(output[at, :], norms[1:2, :], norms[5:6, :])
                output[at, :] = value
                output_low[at, :] = value.astype(LOW)
                normed_two[at, :] = normed.astype(LOW)
                recip_two[at, :] = recip

    neurons = per * size
    ffn_out = ((2, n, neurons), LOW, (1, n, size), lambda i: (i // per, 0, i % per))
    return call(
        body, steps,
        [
            whole(hidden), whole(hidden_low), whole(layer.norms), per_group(layer.bias_up),
        ] + layer.ffn(layer.up) + layer.ffn(layer.down),
        [
            ffn_out, ffn_out, out_whole((n, depth), F32), out_whole((n, depth), LOW),
            out_whole((n, depth), LOW), out_whole((n, 1), F32),
        ],
        [],
        flops=8 * n * depth * neurons,
        exps=4 * n * neurons,
    )


def add_rows(sums, row, value, at):
    value = jnp.sum(value, axis=0, keepdims=True)
    if at.start == 0:
        sums[row : row + 1, :] = value
    else:
        sums[row : row + 1, :] += value


def ffn_back_call(layer, grad, extra, kept, half):
    n, depth = grad.shape
    steps, _, size = layer.bias_up.shape
    per = steps // 2
    has_extra = extra is not None

    def body(grad, *refs):
        extra = refs[0] if has_extra else None
        (
            normed_one, recip_one, normed_two, recip_two, norms, slope, up_one, up_two, down_one, down_two,
            d_final_low, d_pre, d_mid, d_mid_low, sums, bias_sums, total,
        ) = refs[1:] if has_extra else refs
        i = pl.program_id(0)
        gain = lambda at: norms[at : at + 1, :]

        @pl.when(i == 0)
        def _():
            sums[...] = jnp.zeros_like(sums)
            for at in row_tiles(n):
                value = grad[at, :].astype(F32)
                if has_extra and at.start >= 2 * half:
                    value = value + extra[at.start - 2 * half : at.stop - 2 * half, :].astype(F32)
                normed = normed_two[at, :].astype(F32)
                back = normalize_back(value, normed, recip_two[at, :], gain(1))
                total[at, :] = back
                d_final_low[at, :] = back.astype(LOW)
                add_rows(sums, 1, value * normed, at)
                add_rows(sums, 5, value, at)
                add_rows(sums, 4, back, at)

        bias = None
        up, down = joined((up_one, up_two)), joined((down_one, down_two))
        for at in row_tiles(n):
            d_act = dot(d_final_low[at, :], down, 1, 0)
            low = (d_act * slope[0, at, :].astype(F32)).astype(LOW)
            d_pre[0, at, :] = low
            one = jnp.sum(low.astype(F32), axis=0, keepdims=True)
            bias = one if bias is None else bias + one
            total[at, :] += dot(low, up, 1, 1)
        bias_sums[0] = bias

        @pl.when(i == steps - 1)
        def _():
            for at in row_tiles(n):
                value = total[at, :]
                normed = normed_one[at, :].astype(F32)
                back = normalize_back(value, normed, recip_one[at, :], gain(0))
                d_mid[at, :] = back
                d_mid_low[at, :] = back.astype(LOW)
                add_rows(sums, 0, value * normed, at)
                add_rows(sums, 3, value, at)
                add_rows(sums, 2, back, at)

    neurons = per * size
    blocks = ((1, n, size), lambda i: (i // per, 0, i % per))
    return call(
        body, steps,
        [whole(grad)] + ([whole(extra)] if has_extra else []) + [
            whole(kept["normed_one"]), whole(kept["recip_one"]), whole(kept["normed_two"]),
            whole(kept["recip_two"]), whole(layer.norms), (kept["slope"],) + blocks,
        ] + layer.ffn(layer.up) + layer.ffn(layer.down),
        [
            out_whole((n, depth), LOW), ((2, n, neurons), LOW) + blocks, out_whole((n, depth), F32),
            out_whole((n, depth), LOW), out_whole((8, depth), F32), out_group((steps, 1, size), F32),
        ],
        [pltpu.VMEM((n, depth), F32)],
        flops=8 * n * depth * neurons,
    )


def ffn_back_first_call(layer, grad, extra, kept, half):
    n, depth = grad.shape
    steps, _, size = layer.bias_up.shape
    per = steps // 2

    def body(
        grad, extra, normed_two, recip_two, norms, slope, down_one, down_two,
        d_final, d_final_low, d_pre, sums, bias_sums,
    ):
        i = pl.program_id(0)

        @pl.when(i == 0)
        def _():
            sums[...] = jnp.zeros_like(sums)
            for at in row_tiles(n):
                value = grad[at, :]
                if at.start >= 2 * half:
                    value = value + extra[at.start - 2 * half : at.stop - 2 * half, :].astype(F32)
                normed = normed_two[at, :].astype(F32)
                back = normalize_back(value, normed, recip_two[at, :], norms[1:2, :])
                d_final[at, :] = back
                d_final_low[at, :] = back.astype(LOW)
                add_rows(sums, 1, value * normed, at)
                add_rows(sums, 5, value, at)
                add_rows(sums, 4, back, at)

        bias = None
        down = joined((down_one, down_two))
        for at in row_tiles(n):
            d_act = dot(d_final_low[at, :], down, 1, 0)
            low = (d_act * slope[0, at, :].astype(F32)).astype(LOW)
            d_pre[0, at, :] = low
            one = jnp.sum(low.astype(F32), axis=0, keepdims=True)
            bias = one if bias is None else bias + one
        bias_sums[0] = bias

    neurons = per * size
    blocks = ((1, n, size), lambda i: (i // per, 0, i % per))
    return call(
        body, steps,
        [
            whole(grad), whole(extra), whole(kept["normed_two"]), whole(kept["recip_two"]),
            whole(layer.norms), (kept["slope"],) + blocks,
        ] + layer.ffn(layer.down),
        [
            out_whole((n, depth), F32), out_whole((n, depth), LOW), ((2, n, neurons), LOW) + blocks,
            out_whole((8, depth), F32), out_group((steps, 1, size), F32),
        ],
        [],
        flops=4 * n * depth * neurons,
    )


def ffn_back_second_call(layer, d_final, d_pre, kept):
    n, depth = d_final.shape
    steps, _, size = layer.bias_up.shape
    per = steps // 2

    def body(d_final, d_pre, normed_one, recip_one, norms, up_one, up_two, d_mid, d_mid_low, sums):
        i = pl.program_id(0)

        @pl.when(i == 0)
        def _():
            d_mid[...] = d_final[...]

        up = joined((up_one, up_two))
        for at in row_tiles(n):
            d_mid[at, :] += dot(d_pre[0, at, :], up, 1, 1)

        @pl.when(i == steps - 1)
        def _():
            sums[...] = jnp.zeros_like(sums)
            for at in row_tiles(n):
                value = d_mid[at, :]
                normed = normed_one[at, :].astype(F32)
                back = normalize_back(value, normed, recip_one[at, :], norms[0:1, :])
                d_mid[at, :] = back
                d_mid_low[at, :] = back.astype(LOW)
                add_rows(sums, 0, value * normed, at)
                add_rows(sums, 3, value, at)
                add_rows(sums, 2, back, at)

    blocks = ((1, n, size), lambda i: (i // per, 0, i % per))
    return call(
        body, steps,
        [
            whole(d_final), (d_pre,) + blocks, whole(kept["normed_one"]), whole(kept["recip_one"]),
            whole(layer.norms),
        ] + layer.ffn(layer.up),
        [out_whole((n, depth), F32), out_whole((n, depth), LOW), out_whole((8, depth), F32)],
        [],
        flops=4 * n * depth * per * size,
    )


def shared_back_call(layer, d_mid_low, kept, segs, half):
    n, depth = d_mid_low.shape
    width, wide, own = layer.width, 3 * layer.width, 2 * half
    count = 2 * len(layer.qkv_blocks)

    def body(d_mid, proj, away, logsum, *refs):
        weights = pairs_of(refs[:count])
        out_one, out_two, segs_q, segs_k, d_proj, d_away, sums, back, mask, total = refs[count:]
        i = pl.program_id(0)
        make_mask(segs_q, segs_k, mask)
        out_cols = joined((out_one, out_two), slice(layer.out_from, layer.out_from + width))
        d_context = dot(d_mid[...], out_cols, 1, 0).astype(LOW)
        attend_back(
            width, [proj.at[0], away.at[0]], mask, logsum.at[0], d_context,
            [d_proj.at[0], d_away.at[0]], sums.at[0],
        )
        part = through_projection(d_away[0], weights, layer.used)

        @pl.when(i == 0)
        def _():
            total[...] = part

        @pl.when(i == 1)
        def _():
            back[...] = (total[...] + part).astype(LOW)

    return call(
        body, 2,
        [
            (d_mid_low, (half, depth), lambda i: (2, 0)), (kept["proj"], (1, half, wide), lambda i: (i, 2, 0)),
            per_group(kept["proj_away"]), per_group(kept["logsum_shared"]),
        ] + layer.qkv() + layer.out() + [whole(segs[None, :half]), whole(segs[:, None])],
        [
            out_group((2, half, wide), LOW), out_group((2, half, wide), LOW), out_group((2, 8, wide), F32),
            out_whole((half, depth), LOW),
        ],
        [pltpu.VMEM((own, half), F32), pltpu.VMEM((half, depth), F32)],
        flops=4 * half * depth * (wide + width) + 20 * own * half * width,
        exps=2 * own * half * width // HEAD_DIM,
    )


def own_back_call(layer, d_mid, d_mid_low, d_shared, kept, segs, half):
    n, depth = d_mid_low.shape
    width, wide, own = layer.width, 3 * layer.width, 2 * half
    count = 2 * len(layer.qkv_blocks)

    def body(d_mid, d_mid_low, d_shared, proj, logsum, *refs):
        weights = pairs_of(refs[:count])
        out_one, out_two, segs_q, segs_k, d_proj, sums, d_rows, mask = refs[count:]
        i = pl.program_id(0)
        make_mask(segs_q, segs_k, mask)
        out_cols = joined((out_one, out_two), slice(layer.out_from, layer.out_from + width))
        d_context = dot(d_mid_low[...], out_cols, 1, 0).astype(LOW)
        attend_back(
            width, [proj.at[0]], mask, logsum.at[0], d_context, [d_proj.at[0, :own]], sums.at[0]
        )
        d_proj[0, own:] = d_shared[0]
        part = through_projection(d_proj[0], weights, layer.used)

        @pl.when(i == 0)
        def _():
            d_rows[...] = d_mid[...] + part

        @pl.when(i == 1)
        def _():
            d_rows[...] += part

    return call(
        body, 2,
        [
            whole(d_mid), (d_mid_low, (own, depth), lambda i: (0, 0)), per_group(d_shared),
            (kept["proj"], (1, own, wide), lambda i: (i, 0, 0)), per_group(kept["logsum_own"]),
        ] + layer.qkv() + layer.out() + [whole(segs[None, :]), whole(segs[:, None])],
        [
            out_group((2, n, wide), LOW), out_group((2, 8, wide), F32), out_whole((n, depth), F32),
        ],
        [pltpu.VMEM((own, own), F32)],
        flops=4 * depth * (n * wide + own * width) + 20 * own * own * width,
        exps=2 * own * own * width // HEAD_DIM,
    )


class Grads:
    def __init__(self, entries, columns, cut):
        self.entries, self.columns, self.cut = entries, columns, cut
        sizes = [end - start for _, start, end in columns]
        self.size_a, self.size_b = sum(sizes[:cut]), sum(sizes[cut:])

    def inputs(self, at):
        out = []
        for pairs in self.entries:
            for left, right in pairs:
                out += [whole(left), per_group(right, at)]
        return out

    def scratch(self, rows):
        return [pltpu.VMEM((rows, left.shape[0]), LOW) for pairs in self.entries for left, _ in pairs]

    def flops(self, rows):
        depth = self.entries[0][0][0].shape[1]
        return sum(
            2 * rows * left.shape[0] * (2 * right.shape[2] + depth)
            for pairs in self.entries for left, right in pairs
        )

    def turn(self, pick, refs, turned):
        @pl.when(pl.program_id(0) == 0)
        def _():
            for at in range(len(turned)):
                turned[at][...] = dot(pick[...], refs[2 * at][...], 1, 1).astype(LOW)

    def product(self, refs, turned, entry, start, end):
        first = sum(len(pairs) for pairs in self.entries[:entry])
        total = None
        for at in range(first, first + len(self.entries[entry])):
            one = dot(turned[at][...], refs[2 * at + 1][0, :, start:end], 1, 0)
            total = one if total is None else total + one
        return total

    def send(self, pick):
        rows = pick.shape[0]
        size = self.size_a + self.size_b

        def body(pick, *refs):
            count = 2 * sum(len(pairs) for pairs in self.entries)
            out, turned = refs[count], refs[count + 1 :]
            self.turn(pick, refs, turned)
            col = 0
            for entry, start, end in self.columns:
                part = self.product(refs, turned, entry, start, end)
                out[0, :, col : col + end - start] = part.astype(LOW)
                col += end - start

        return call(
            body, 2, [whole(pick)] + self.inputs(lambda i: i), [out_group((2, rows, size), LOW)],
            self.scratch(rows), self.flops(rows),
        )[0]

    def keep(self, pick, got):
        rows = pick.shape[0]
        half = rows // 2
        size = self.size_a + self.size_b

        def body(pick, got, *refs):
            count = 2 * sum(len(pairs) for pairs in self.entries)
            send_a, keep_a, send_b, keep_b = refs[count : count + 4]
            turned = refs[count + 4 :]
            i = pl.program_id(0)
            self.turn(pick, refs, turned)
            col = 0
            for at, (entry, start, end) in enumerate(self.columns):
                part = self.product(refs, turned, entry, start, end)
                part = part + got[0, :, col : col + end - start].astype(F32)
                if at < self.cut:
                    place = slice(col, col + end - start)

                    @pl.when(i == 0)
                    def _():
                        send_a[:, place] = part.astype(LOW)

                    @pl.when(i == 1)
                    def _():
                        keep_a[:, place] = part
                else:
                    place = slice(col - self.size_a, col - self.size_a + end - start)
                    keep_b[0, :, place] = part[:half]
                    send_b[0, :, place] = part[half:].astype(LOW)
                col += end - start

        return call(
            body, 2,
            [whole(pick), per_group(got, lambda i: 1 - i)] + self.inputs(lambda i: 1 - i),
            [
                out_whole((rows, self.size_a), LOW), out_whole((rows, self.size_a), F32),
                out_group((2, half, self.size_b), LOW), out_group((2, half, self.size_b), F32),
            ],
            self.scratch(rows), self.flops(rows),
        )


class Reduce:
    def __init__(self, grads, pick_send, pick_keep):
        self.grads, self.pick_keep = grads, pick_keep
        self.sends = (grads.send(pick_send),)
        self.got = (swap_core(self.sends[0]),)
        self.work = self._run()

    def _run(self):
        count = lax.axis_size("dp") // 4
        send_a, keep_a, send_b, keep_b = self.grads.keep(self.pick_keep, self.got[0])
        fourth = keep_a.shape[0] // 2
        self.sends = (send_a, send_b)
        self.got = (swap_y(send_a), swap_x(send_b))
        yield
        a = keep_a + self.got[0].astype(F32)
        b = keep_b + self.got[1].astype(F32)
        self.sends = (a[fourth:].astype(LOW), b[0].astype(LOW))
        self.got = (swap_x(self.sends[0]), swap_y(self.sends[1]))
        a, b = a[:fourth], b[1]
        yield
        both = jnp.concatenate([a + self.got[0].astype(F32), b + self.got[1].astype(F32)], axis=1)
        both = both.reshape((count, -1) + both.shape[1:])
        self.sends = tuple(both[back].astype(LOW) for back in range(1, count))
        self.got = tuple(ring_shift(send, -back) for back, send in enumerate(self.sends, 1))
        yield
        total = both[0] + sum(got.astype(F32) for got in self.got)
        self.total = total
        self.got = self.sends = ()

    def step(self):
        next(self.work, None)


class Total:
    def __init__(self, value):
        self.total = value
        self.work = self._run()
        self.step()

    def _run(self):
        n = lax.axis_size("dp")
        self.sends = (self.total,)
        self.got = (swap_y(self.total),)
        yield
        self.total = self.total + self.got[0]
        step = 1
        while step < n:
            self.sends = (self.total,)
            self.got = (lax.ppermute(self.total, "dp", [(i, i ^ step) for i in range(n)]),)
            yield
            self.total = self.total + self.got[0]
            step *= 2
        self.got = self.sends = ()

    def step(self):
        next(self.work, None)


def round_of(*works):
    ended = lax.optimization_barrier(tuple(work.got for work in works))
    for work, got in zip(works, ended):
        work.got = got
    for work in works:
        work.step()


def before(value, *works):
    value, ended = lax.optimization_barrier((value, tuple(work.got for work in works)))
    for work, got in zip(works, ended):
        work.got = got
    return value


def forward_attn(layer, rows, proj, context_own, logsum_own, rows_low, away_low, segs, half):
    proj_away, context, logsum_shared, hidden, hidden_low, normed_one, recip_one = shared_call(
        layer, rows, proj, away_low, context_own, segs[1], half
    )
    kept = dict(
        rows_low=rows_low, away_low=away_low, proj=proj, proj_away=proj_away, context=context,
        logsum_own=logsum_own, logsum_shared=logsum_shared, hidden_low=hidden_low,
        normed_one=normed_one, recip_one=recip_one,
    )
    return hidden, kept


def forward_ffn(layer, hidden, kept):
    act, slope, output, output_low, normed_two, recip_two = ffn_call(layer, hidden, kept["hidden_low"])
    kept.update(act=act, slope=slope, normed_two=normed_two, recip_two=recip_two)
    return output, output_low


def backward_ffn(layer, grad, extra, kept, half):
    d_final_low, d_pre, d_mid, d_mid_low, sums, bias_sums = ffn_back_call(layer, grad, extra, kept, half)
    entries = [[(kept["hidden_low"], d_pre)], [(d_final_low, kept["act"])]]
    return d_mid, d_mid_low, sums[:6], bias_sums, entries


def attn_entries(kept, d_proj, d_away, d_mid_low):
    return [[(kept["rows_low"], d_proj), (kept["away_low"], d_away)], [(d_mid_low, kept["context"])]]


def on_device(
    tokens, segment_ids, out_grad,
    t_qkv, t_qv_bias, t_out, t_up, t_up_bias, t_down, t_gains, t_shifts,
    s_qkv, s_qv_bias, s_out, s_up, s_up_bias, s_down, s_gains, s_shifts,
):
    rows, half, width = tokens.shape
    first = lax.axis_index("mp") == 0
    own_row = lambda value: jnp.where(first, value[0], value[2])
    far_row = lambda value: jnp.where(first, value[2], value[0])

    norm_rows = jnp.concatenate([t_gains, t_shifts, s_gains, s_shifts], axis=0).T
    norm_rows = jnp.pad(norm_rows, ((0, 0), (0, 128 - norm_rows.shape[1])))
    t_width, s_width = t_qkv.shape[2], s_qkv.shape[2]
    beside = lambda *parts: jnp.concatenate(parts, axis=1)
    attn_a, attn_b = beside(t_qkv[0], t_qkv[1]), beside(t_qkv[2], t_out.T, norm_rows)
    ffn_a, ffn_b = t_up, t_down.T
    student_a, student_b = beside(s_up, s_qkv[0], s_out.T), beside(s_down.T, s_qkv[1], s_qkv[2])
    count = lax.axis_size("dp") // 4
    together = lambda *values: lax.optimization_barrier(values)

    class Ring:
        def __init__(self, a, b):
            self.cut = a.shape[-1]
            self.pieces = [jnp.concatenate([a, b], axis=-1)]

        def step(self):
            self.pieces.append(ring_shift(self.pieces[-1], 1))

        def direct(self):
            self.pieces += [ring_shift(self.pieces[0], at) for at in range(1, count)]

        def result(self):
            axis = self.pieces[0].ndim - 2
            return (
                jnp.concatenate([piece[..., : self.cut] for piece in self.pieces], axis=axis),
                jnp.concatenate([piece[..., self.cut :] for piece in self.pieces], axis=axis),
            )

    def all_planes(a, b, got_a, got_b):
        return jnp.stack([a, got_a]), jnp.concatenate([b, got_b], axis=1)

    def with_core(own):
        return own, swap_core(own)

    bias_parts = [t_qv_bias[0], t_qv_bias[1], t_up_bias, s_qv_bias[0], s_qv_bias[1], s_up_bias]
    ring_t = Ring(attn_a, attn_b)
    ring_t.direct()
    tokens, ffn_a, ffn_b, student_a = after((tokens, ffn_a, ffn_b, student_a), ring_t.pieces[0])
    own_tokens = jnp.concatenate([own_row(tokens), tokens[1]], axis=0)
    got_tokens = swap_y(jnp.stack([far_row(tokens), tokens[1]]))
    ffn_x, ffn_y = swap_x(ffn_a), swap_y(ffn_b)
    ring_t.pieces, ffn_x, ffn_y = together(ring_t.pieces, ffn_x, ffn_y)
    student_x = swap_x(student_a)
    bias_own = jnp.concatenate(bias_parts)
    attn_a, attn_b = ring_t.result()
    ring_f = Ring(jnp.stack([ffn_a, ffn_x]), jnp.stack([ffn_b, ffn_y]))
    got_a, got_b = swap_x(attn_a), swap_y(attn_b)
    ring_f.step()
    got_a, got_b, got_tokens, student_x = together(got_a, got_b, got_tokens, student_x)
    attn_a, attn_b = jnp.concatenate([attn_a, got_a], axis=0), jnp.stack([attn_b, got_b])
    got_a, got_b = swap_y(attn_a), swap_x(attn_b)
    ring_f.pieces[-1], got_a, got_b = together(ring_f.pieces[-1], got_a, got_b)
    ring_f.step()
    attn_a, attn_b = all_planes(attn_a, attn_b, got_a, got_b)
    attn_a, attn_b = with_core(attn_a), with_core(attn_b)
    student_y, bias_far = swap_y(student_b), swap_y(bias_own)
    for at in range(3, count):
        ring_f.step()
    attn_a, attn_b, ring_f.pieces[-1], student_y, bias_far = together(
        attn_a, attn_b, ring_f.pieces[-1], student_y, bias_far
    )
    ffn_a, ffn_b = ring_f.result()
    ffn_a = ffn_a.reshape(-1, ffn_a.shape[-1])
    got_a, got_b = swap_y(ffn_a), swap_x(ffn_b)
    ring_s = Ring(jnp.stack([student_a, student_x]), jnp.stack([student_b, student_y]))
    ring_s.step()
    norms = jnp.concatenate([half[0, :, -128:-116] for half in attn_b], axis=0).T.astype(F32)
    norms_of = lambda at: jnp.pad(norms[at : at + 6], ((0, 2), (0, 0)))
    bias_all = jnp.stack([bias_own, bias_far]).astype(F32)
    cuts = [0]
    for part in bias_parts:
        cuts.append(cuts[-1] + part.shape[0])
    pick = [bias_all[:, cuts[i] : cuts[i + 1]] for i in range(6)]
    bias_qkv = lambda q, v: jnp.concatenate([q, jnp.zeros_like(q), v], axis=1)[:, None, :]
    size = s_up.shape[1]
    per = t_up.shape[1] // size
    teacher = Layer(
        t_width, None, None,
        [(attn_a, t_width, 0, t_width), (attn_a, t_width, 1, t_width), (attn_b, t_width, 0, t_width)],
        (attn_b, t_width, 1, t_width), 0, norms_of(0), bias_qkv(pick[0], pick[1]),
        pick[2].reshape(2 * per, 1, size),
    )

    to_own = feature_order(width)
    into = (lax.iota(jnp.int32, width)[:, None] == to_own[None, :]).astype(LOW)
    reorder = lambda value: jnp.dot(value, into, preferred_element_type=F32).astype(LOW)
    pick_all = jnp.eye(width, dtype=LOW)
    pick_keep, pick_send = pick_all[: width // 2], pick_all[width // 2 :]

    inputs = reorder(jnp.concatenate([own_tokens[:half], got_tokens[0], own_tokens[half:], got_tokens[1]], axis=0))
    inputs, away_low = inputs[: 3 * half], inputs[3 * half :]
    spin = lambda segs: jnp.where(first, segs, jnp.roll(segs, half))
    segs = (spin(own_row(segment_ids)), spin(segment_ids[1]))

    grad_in = jnp.concatenate([own_row(out_grad), swap_y(far_row(out_grad)), out_grad[1]], axis=0)
    grad_in = reorder(grad_in)

    inputs, grad_in = together(inputs, grad_in)
    proj, context_own, logsum_own = project_call(teacher, inputs, segs[0], half)
    proj, ring_s.pieces[-1] = together(proj, ring_s.pieces[-1])
    ring_s.step()
    proj, got_a, got_b, ring_s.pieces[-1] = together(proj, got_a, got_b, ring_s.pieces[-1])
    ffn_a, ffn_b = all_planes(ffn_a, ffn_b, got_a, got_b)
    teacher.up, teacher.down = with_core(ffn_a), with_core(ffn_b)
    for at in range(3, count):
        ring_s.step()
    hidden, t_kept = forward_attn(
        teacher, inputs, proj, context_own, logsum_own, inputs, away_low, segs, half
    )
    hidden, teacher.up, teacher.down, ring_s.pieces[-1] = together(
        hidden, teacher.up, teacher.down, ring_s.pieces[-1]
    )
    student_a, student_b = ring_s.result()
    student_a = student_a.reshape(-1, student_a.shape[-1])
    got_a, got_b = swap_y(student_a), swap_x(student_b)
    middle, middle_low = forward_ffn(teacher, hidden, t_kept)
    away_low = swap_y(middle_low[2 * half :])
    middle_low, got_a, got_b = together(middle_low, got_a, got_b)
    student_a, student_b = all_planes(student_a, student_b, got_a, got_b)
    student_a, student_b = with_core(student_a), with_core(student_b)
    narrow = 2 * s_width
    student = Layer(
        s_width, student_a, student_b,
        [(student_a, narrow, size // narrow, s_width), (student_b, narrow, size // narrow, narrow)],
        (student_a, narrow, size // narrow, s_width), s_width, norms_of(6), bias_qkv(pick[3], pick[4]),
        pick[5].reshape(2, 1, size),
    )
    proj, context_own, logsum_own = project_call(student, middle_low, segs[0], half)
    proj, away_low = together(proj, away_low)
    hidden, s_kept = forward_attn(
        student, middle, proj, context_own, logsum_own, middle_low, away_low, segs, half
    )
    last, _ = forward_ffn(student, hidden, s_kept)

    def far_half(value):
        return swap_y(value[half : 2 * half].astype(LOW))

    def to_rows(value, far):
        near = jnp.concatenate([value[:half], value[2 * half :]], axis=0)
        high = near.astype(LOW)
        low = (near - high.astype(F32)).astype(LOW)
        back = lambda part: jnp.einsum("nr,dr->nd", part, into, preferred_element_type=F32)
        near, far = back(high) + back(low), back(far)
        return jnp.stack([jnp.where(first, near[:half], far), near[half:], jnp.where(first, far, near[:half])])

    far_last = far_half(last)

    d_mid, d_mid_low, s_norm_grads, s_up_grad, s_entries = backward_ffn(student, grad_in, None, s_kept, half)
    d_shared, d_away, s_sums_b, back = shared_back_call(student, d_mid_low, s_kept, segs[1], half)
    extra = swap_y(back)
    d_shared, far_last = together(d_shared, far_last)
    d_proj, s_sums_a, d_rows = own_back_call(student, d_mid, d_mid_low, d_shared, s_kept, segs[0], half)
    d_proj, extra = lax.optimization_barrier((d_proj, extra))
    s_entries += attn_entries(s_kept, d_proj, d_away, d_mid_low)
    s_columns = [(0, 0, size), (2, 0, s_width), (3, 0, s_width), (1, 0, size), (2, s_width, 3 * s_width)]
    reduce_s = Reduce(Grads(s_entries, s_columns, 3), pick_send, pick_keep)

    d_rows = after(d_rows, reduce_s.sends)
    d_final, d_final_low, d_pre, t_sums_two, t_up_grad = ffn_back_first_call(
        teacher, d_rows, extra, t_kept, half
    )
    d_pre = before(d_pre, reduce_s)
    reduce_s.step()
    d_pre = after(d_pre, reduce_s.sends)
    f_entries = [[(t_kept["hidden_low"], d_pre)], [(d_final_low, t_kept["act"])]]
    reduce_f = Reduce(
        Grads(f_entries, [(0, 0, per * size), (1, 0, per * size)], 1), pick_send, pick_keep
    )
    d_pre = after(d_pre, reduce_f.sends)
    d_mid, d_mid_low, t_sums_one = ffn_back_second_call(teacher, d_final, d_pre, t_kept)
    t_norm_grads = (t_sums_one + t_sums_two)[:6]
    d_mid_low = before(d_mid_low, reduce_s)
    reduce_s.step()
    d_mid_low = after(before(d_mid_low, reduce_f), reduce_s.sends)
    reduce_f.step()
    d_mid_low = after(d_mid_low, reduce_f.sends)
    d_shared, d_away, t_sums_b, back = shared_back_call(teacher, d_mid_low, t_kept, segs[1], half)
    extra = swap_y(back)
    d_shared = before(d_shared, reduce_s)
    reduce_s.step()
    d_shared = after(d_shared, reduce_s.sends)
    d_proj, t_sums_a, d_rows = own_back_call(teacher, d_mid, d_mid_low, d_shared, t_kept, segs[0], half)
    t_entries = attn_entries(t_kept, d_proj, d_away, d_mid_low)
    reduce_t = Reduce(
        Grads(t_entries, [(0, 0, 2 * t_width), (0, 2 * t_width, 3 * t_width), (1, 0, t_width)], 1),
        pick_send, pick_keep,
    )
    far_rows = far_half(d_rows)

    def qv_grad(one, two, wide):
        sums = one[:, 0] + two[:, 0]
        sums = jnp.concatenate([sums[:, :wide], sums[:, 2 * wide :]], axis=1)
        return jnp.pad(sums, ((0, 0), (0, width - 2 * wide)))

    norm_grads = jnp.concatenate([t_norm_grads, s_norm_grads], axis=0)
    norm_grads = jnp.einsum("nr,dr->nd", norm_grads, into.astype(F32), precision=lax.Precision.HIGHEST)
    qv_t, qv_s = qv_grad(t_sums_a, t_sums_b, t_width), qv_grad(s_sums_a, s_sums_b, s_width)
    mine = jnp.concatenate([t_up_grad[:per, 0], s_up_grad[:1, 0], qv_t[:1], qv_s[:1]], axis=0)
    other = jnp.concatenate([t_up_grad[per:, 0], s_up_grad[1:, 0], qv_t[1:], qv_s[1:]], axis=0)
    small = Total(jnp.concatenate(
        [norm_grads, jnp.where(first, mine, other), jnp.where(first, other, mine)], axis=0
    ))
    reduce_f.got = after(reduce_f.got, reduce_t.sends)
    round_of(reduce_f, small)
    reduce_t.got = after(reduce_t.got, reduce_f.sends)
    reduce_t.step()
    reduce_f.got = after(reduce_f.got, reduce_t.sends)
    round_of(reduce_f, reduce_s)
    round_of(reduce_t, small)
    d_rows, last = after((d_rows, last), reduce_t.sends)
    d_rows = jnp.concatenate([d_rows[: 2 * half], d_rows[2 * half :] + extra.astype(F32)], axis=0)
    input_grad, output = to_rows(d_rows, far_rows), to_rows(last, far_last)
    round_of(reduce_t, reduce_f, small)
    round_of(reduce_t, small)
    for work in (reduce_t, reduce_f, reduce_s, small):
        while work.got:
            work.step()
    s_sum, f_sum, t_sum, small = reduce_s.total, reduce_f.total, reduce_t.total, small.total

    piece = width // lax.axis_size("dp")
    norm_sum = lax.dynamic_slice_in_dim(small[:12], lax.axis_index("dp") * piece, piece, 1)
    bias_sum = small[12:].reshape(2, -1, width)
    bias_sum = jnp.where(first, bias_sum[0], bias_sum[1])
    t_qv_sum, s_qv_sum = bias_sum[per + 1], bias_sum[per + 2, : 2 * s_width]

    def cut(value, *sizes):
        out = []
        for one in sizes:
            out.append(value[:, :one])
            value = value[:, one:]
        return out

    tq, tk, tv, to = cut(t_sum, t_width, t_width, t_width, t_width)
    t_up_sum, t_down_sum = cut(f_sum, per * size, per * size)
    s_up_sum, sq, so, s_down_sum, sk, sv = cut(s_sum, size, s_width, s_width, size, s_width, s_width)
    return (
        output, input_grad,
        jnp.stack([tq, tk, tv]), t_qv_sum.reshape(2, -1), to.T, t_up_sum, bias_sum[:per].reshape(-1),
        t_down_sum.T,
        norm_sum[0:2], norm_sum[2:6],
        jnp.stack([sq, sk, sv]), s_qv_sum.reshape(2, -1), so.T, s_up_sum, bias_sum[per], s_down_sum.T,
        norm_sum[6:8], norm_sum[8:12],
    )


def solution(mesh):
    layer = (
        P(None, "dp", "mp"), P(None, "mp"), P("mp", "dp"), P("dp", "mp"), P("mp"), P("mp", "dp"),
        P(None, "dp"), P(None, "dp"),
    )
    rows = P("dp", "mp", None)
    return jax.shard_map(
        on_device,
        mesh=mesh,
        in_specs=(rows, P("dp", None), rows) + layer + layer,
        out_specs=(rows, rows) + layer + layer,
        check_vma=False,
    )
```

```python
import functools
import math

import jax
import jax.numpy as jnp
from jax import lax
from jax.experimental import pallas as pl
from jax.experimental.pallas import tpu as pltpu
from jax.sharding import PartitionSpec as P

HEAD_DIM = 64
LOW = jnp.bfloat16
F32 = jnp.float32


def ring_of(count):
    return list(range(0, count, 2)) + list(range(1, count, 2))[::-1]


def swap_y(value):
    return lax.ppermute(value, "mp", [(0, 1), (1, 0)])


def swap_x(value):
    n = lax.axis_size("dp")
    return lax.ppermute(value, "dp", [(i, i ^ 2) for i in range(n)])


def swap_core(value):
    n = lax.axis_size("dp")
    return lax.ppermute(value, "dp", [(i, i ^ 1) for i in range(n)])


def ring_shift(value, step):
    count = lax.axis_size("dp") // 4
    ring = ring_of(count)
    pairs = []
    for place in range(count):
        for low in range(4):
            pairs.append((ring[place] * 4 + low, ring[(place + step) % count] * 4 + low))
    return lax.ppermute(value, "dp", pairs)


def feature_order(width):
    n = lax.axis_size("dp")
    count, rows = n // 4, width // n
    me = lax.axis_index("dp")
    z, x, core = me // 4, (me // 2) % 2, me % 2
    place = jnp.where(z % 2 == 0, z // 2, count - 1 - z // 2)
    at = lax.iota(jnp.int32, width)
    row = at % rows
    back = (at // rows) % count
    x_rel = (at // (rows * count)) % 2
    core_rel = at // (rows * count * 2)
    from_place = (place - back + count) % count
    half = (count + 1) // 2
    z_abs = jnp.where(from_place < half, 2 * from_place, 2 * (count - 1 - from_place) + 1)
    block = z_abs * 4 + (x ^ x_rel) * 2 + (core ^ core_rel)
    return block * rows + row


def after(value, *others):
    return lax.optimization_barrier((value, others))[0]


VMEM_BYTES = 48 << 20
TILE = 256


def dot(left, right, left_at, right_at):
    return lax.dot_general(
        left, right, (((left_at,), (right_at,)), ((), ())), preferred_element_type=F32
    )


def call(body, steps, inputs, outputs, scratch, flops, exps=0):
    size = lambda shape, dtype: math.prod(shape) * jnp.dtype(dtype).itemsize
    moved = sum(size(array.shape, array.dtype) for array, _, _ in inputs)
    moved += sum(size(shape, dtype) for shape, dtype, _, _ in outputs)
    return pl.pallas_call(
        body,
        grid=(steps,),
        in_specs=[pl.BlockSpec(block, index) for _, block, index in inputs],
        out_specs=[pl.BlockSpec(block, index) for _, _, block, index in outputs],
        out_shape=[jax.ShapeDtypeStruct(shape, dtype) for shape, dtype, _, _ in outputs],
        scratch_shapes=scratch,
        compiler_params=pltpu.CompilerParams(
            dimension_semantics=("arbitrary",), vmem_limit_bytes=VMEM_BYTES
        ),
        cost_estimate=pl.CostEstimate(
            flops=flops // 2, bytes_accessed=moved // 2, transcendentals=exps // 2
        ),
    )(*[array for array, _, _ in inputs])


def moves(arrays, shapes, copies):
    def body(*refs):
        for source, taken, target, place in copies:
            refs[len(arrays) + target][place] = refs[source][taken]

    moved = 2 * sum(math.prod(shape) for shape in shapes)
    return pl.pallas_call(
        body,
        out_shape=[jax.ShapeDtypeStruct(shape, LOW) for shape in shapes],
        compiler_params=pltpu.CompilerParams(vmem_limit_bytes=VMEM_BYTES),
        cost_estimate=pl.CostEstimate(flops=0, bytes_accessed=moved, transcendentals=0),
    )(*arrays)


def pack(straight, turned, shapes, copies):
    count = len(straight)

    def body(*refs):
        outs = refs[count + len(turned) :]
        rows = turned[0].shape[1]
        at = lambda axis: lax.broadcasted_iota(jnp.int32, (rows, rows), axis)
        same = jnp.where(at(0) == at(1), 1.0, 0.0).astype(LOW)
        for source, taken, target, place in copies:
            if source < count:
                outs[target][place] = refs[source][taken]
            else:
                outs[target][place] = dot(same, refs[source][...], 1, 1).astype(LOW)

    moved = 2 * sum(math.prod(shape) for shape in shapes)
    return pl.pallas_call(
        body,
        out_shape=[jax.ShapeDtypeStruct(shape, LOW) for shape in shapes],
        compiler_params=pltpu.CompilerParams(vmem_limit_bytes=VMEM_BYTES),
        cost_estimate=pl.CostEstimate(flops=0, bytes_accessed=moved, transcendentals=0),
    )(*straight, *turned)


def whole(array):
    rank = array.ndim
    return (array, array.shape, lambda i: (0,) * rank)


def per_group(array, at=lambda i: i):
    return (array, (1,) + array.shape[1:], lambda i: (at(i),) + (0,) * (array.ndim - 1))


def out_whole(shape, dtype):
    return (shape, dtype, shape, lambda i: (0,) * len(shape))


def out_group(shape, dtype, at=lambda i: i):
    return (shape, dtype, (1,) + shape[1:], lambda i: (at(i),) + (0,) * (len(shape) - 1))


class Layer:
    def __init__(self, width, up, down, qkv, out, out_from, norms, bias_qkv, bias_up):
        self.width, self.up, self.down = width, up, down
        self.qkv_blocks, self.out_block, self.out_from = qkv, out, out_from
        self.norms, self.bias_qkv, self.bias_up = norms, bias_qkv, bias_up
        self.used = [block[3] for block in qkv]

    def columns(self, block, at):
        pair, size, place, _ = block
        return [(half, (1, half.shape[1], size), lambda i: (at(i), 0, place)) for half in pair]

    def qkv(self, at=lambda i: i):
        return [one for block in self.qkv_blocks for one in self.columns(block, at)]

    def out(self, at=lambda i: i):
        return self.columns(self.out_block, at)

    def ffn(self, where):
        pair, base = where
        size, per = self.bias_up.shape[2], self.bias_up.shape[0] // 2
        return [(half, (1, half.shape[1], size), lambda i: (i // per, 0, base + i % per)) for half in pair]


def joined(pair, cols=slice(None)):
    return jnp.concatenate([half[0, :, cols] for half in pair], axis=0)


def pairs_of(refs):
    return [refs[at : at + 2] for at in range(0, len(refs), 2)]


def put_projection(rows, weights, used, bias, target):
    start = 0
    for weight, cols in zip(weights, used):
        part = dot(rows, joined(weight, slice(0, cols)), 1, 0) + bias[0, :, start : start + cols]
        target[:, start : start + cols] = part.astype(LOW)
        start += cols


def through_projection(grads, weights, used):
    start = 0
    total = None
    for weight, cols in zip(weights, used):
        part = dot(grads[:, start : start + cols], joined(weight, slice(0, cols)), 1, 1)
        total = part if total is None else total + part
        start += cols
    return total


def head_at(width, part, head):
    return slice(part * width + head * HEAD_DIM, part * width + (head + 1) * HEAD_DIM)


def join(parts, cols):
    picked = [part[:, cols] for part in parts]
    return picked[0] if len(picked) == 1 else jnp.concatenate(picked, axis=0)


def attend(width, kept, mask, logsum):
    scale = jnp.asarray(HEAD_DIM**-0.5, LOW)
    out = []
    for head in range(width // HEAD_DIM):
        query = kept[0][:, head_at(width, 0, head)] * scale
        scores = dot(join(kept, head_at(width, 1, head)), query, 1, 1) + mask[...]
        top = jnp.max(scores, axis=0, keepdims=True)
        expo = jnp.exp(scores - top)
        total = jnp.sum(expo, axis=0, keepdims=True)
        out.append(dot(join(kept, head_at(width, 2, head)), expo.astype(LOW), 0, 0) * (1.0 / total))
        logsum[head : head + 1, :] = top + jnp.log(total)
    return jnp.concatenate(out, axis=0).T.astype(LOW)


def attend_back(width, kept, mask, logsum, d_context, grads, sums):
    scale = jnp.asarray(HEAD_DIM**-0.5, LOW)
    for head in range(width // HEAD_DIM):
        at_q, at_k, at_v = (head_at(width, part, head) for part in range(3))
        query = kept[0][:, at_q] * scale
        keys = join(kept, at_k)
        d_ctx = d_context[:, head * HEAD_DIM : (head + 1) * HEAD_DIM]
        probs = jnp.exp(dot(keys, query, 1, 1) + mask[...] - logsum[head : head + 1, :])
        d_probs = dot(join(kept, at_v), d_ctx, 1, 1)
        both = probs * d_probs
        inner = jnp.sum(both, axis=0, keepdims=True)
        d_scores = (both - probs * inner).astype(LOW)
        d_values = dot(probs.astype(LOW), d_ctx, 1, 0).astype(LOW)
        d_keys = dot(d_scores, query, 1, 0).astype(LOW)
        d_query = dot(keys * scale, d_scores, 0, 0).T.astype(LOW)
        grads[0][:, at_q] = d_query
        start = 0
        for grad in grads:
            rows = grad.shape[0]
            grad[:, at_k] = d_keys[start : start + rows]
            grad[:, at_v] = d_values[start : start + rows]
            start += rows
        for grad in grads[1:]:
            grad[:, at_q] = jnp.zeros((grad.shape[0], HEAD_DIM), LOW)
        sums[0:1, at_q] = jnp.sum(d_query.astype(F32), axis=0, keepdims=True)
        sums[0:1, at_k] = jnp.zeros((1, HEAD_DIM), F32)
        sums[0:1, at_v] = jnp.sum(d_values.astype(F32), axis=0, keepdims=True)


def make_mask(segs_q, segs_k, mask):
    @pl.when(pl.program_id(0) == 0)
    def _():
        mask[...] = jnp.where(segs_k[...] == segs_q[...], 0.0, -1e9)


def normalize(value, gain, shift):
    center = value - jnp.mean(value, axis=-1, keepdims=True)
    recip = lax.rsqrt(jnp.mean(center * center, axis=-1, keepdims=True) + 1e-06)
    normed = center * recip
    return normed * gain + shift, normed, recip


def normalize_back(grad, normed, recip, gain):
    scaled = grad * gain
    mean_one = jnp.mean(scaled, axis=-1, keepdims=True)
    mean_two = jnp.mean(scaled * normed, axis=-1, keepdims=True)
    return recip * (scaled - mean_one - normed * mean_two)


def row_tiles(rows):
    return [slice(start, start + TILE) for start in range(0, rows, TILE)]


def project_call(layer, rows_low, segs, half):
    n, depth = rows_low.shape
    width, wide, own = layer.width, 3 * layer.width, 2 * half
    count = 2 * len(layer.qkv_blocks)

    def body(rows, *refs):
        weights = pairs_of(refs[:count])
        bias, segs_q, segs_k, proj, context, logsum, mask = refs[count:]
        make_mask(segs_q, segs_k, mask)
        put_projection(rows[...], weights, layer.used, bias, proj.at[0])
        context[0] = attend(width, [proj.at[0, :own]], mask, logsum.at[0])

    return call(
        body, 2,
        [whole(rows_low)] + layer.qkv() + [
            per_group(layer.bias_qkv), whole(segs[None, :]), whole(segs[:, None])
        ],
        [
            out_group((2, n, wide), LOW), out_group((2, own, width), LOW), out_group((2, 8, own), F32),
        ],
        [pltpu.VMEM((own, own), F32)],
        flops=4 * n * depth * wide + 8 * own * own * width,
        exps=2 * own * own * width // HEAD_DIM,
    )


def shared_call(layer, rows, proj, away_low, context_own, segs, half):
    n, depth = rows.shape
    width, wide, own = layer.width, 3 * layer.width, 2 * half
    count = 2 * len(layer.qkv_blocks)

    def body(rows, proj, away, *refs):
        weights = pairs_of(refs[:count])
        (
            out_one, out_two, bias, segs_q, segs_k, context_own, norms,
            proj_away, context, logsum, hidden, hidden_low, normed_one, recip_one, mask, total,
        ) = refs[count:]
        i = pl.program_id(0)
        make_mask(segs_q, segs_k, mask)
        put_projection(away[...], weights, layer.used, bias, proj_away.at[0])
        context[0, :own] = context_own[0]
        context[0, own:] = attend(width, [proj.at[0], proj_away.at[0]], mask, logsum.at[0])
        out_cols = joined((out_one, out_two), slice(layer.out_from, layer.out_from + width))

        @pl.when(i == 0)
        def _():
            total[...] = dot(context[0], out_cols, 1, 1)

        @pl.when(i == 1)
        def _():
            for at in row_tiles(n):
                value = rows[at, :].astype(F32) + norms[2:3, :]
                value = value + (total[at, :] + dot(context[0, at], out_cols, 1, 1))
                value, normed, recip = normalize(value, norms[0:1, :], norms[3:4, :])
                hidden[at, :] = value
                hidden_low[at, :] = value.astype(LOW)
                normed_one[at, :] = normed.astype(LOW)
                recip_one[at, :] = recip

    return call(
        body, 2,
        [
            whole(rows), (proj, (1, half, wide), lambda i: (i, 2, 0)), whole(away_low),
        ] + layer.qkv() + layer.out() + [
            per_group(layer.bias_qkv), whole(segs[None, :half]),
            whole(segs[:, None]), per_group(context_own), whole(layer.norms),
        ],
        [
            out_group((2, half, wide), LOW), out_group((2, n, width), LOW), out_group((2, 8, half), F32),
            out_whole((n, depth), F32), out_whole((n, depth), LOW), out_whole((n, depth), LOW),
            out_whole((n, 1), F32),
        ],
        [pltpu.VMEM((own, half), F32), pltpu.VMEM((n, depth), F32)],
        flops=4 * depth * (n * width + half * wide) + 8 * own * half * width,
        exps=2 * own * half * width // HEAD_DIM,
    )


def ffn_call(layer, hidden, hidden_low):
    n, depth = hidden.shape
    steps, _, size = layer.bias_up.shape
    per = steps // 2

    def body(
        hidden, hidden_low, norms, bias_up, up_one, up_two, down_one, down_two,
        act, slope, output, output_low, normed_two, recip_two,
    ):
        i = pl.program_id(0)

        @pl.when(i == 0)
        def _():
            output[...] = hidden[...] + norms[4:5, :]

        up, down = joined((up_one, up_two)), joined((down_one, down_two))
        for at in row_tiles(n):
            pre = dot(hidden_low[at, :], up, 1, 0) + bias_up[0]
            bell = 0.5 + 0.5 * lax.erf(pre * math.sqrt(0.5))
            low = (pre * bell).astype(LOW)
            act[0, at, :] = low
            slope[0, at, :] = (
                bell + pre * (jnp.exp(-0.5 * pre * pre) * (1.0 / math.sqrt(2.0 * math.pi)))
            ).astype(LOW)
            output[at, :] += dot(low, down, 1, 1)

        @pl.when(i == steps - 1)
        def _():
            for at in row_tiles(n):
                value, normed, recip = normalize(output[at, :], norms[1:2, :], norms[5:6, :])
                output[at, :] = value
                output_low[at, :] = value.astype(LOW)
                normed_two[at, :] = normed.astype(LOW)
                recip_two[at, :] = recip

    neurons = per * size
    ffn_out = ((2, n, neurons), LOW, (1, n, size), lambda i: (i // per, 0, i % per))
    return call(
        body, steps,
        [
            whole(hidden), whole(hidden_low), whole(layer.norms), per_group(layer.bias_up),
        ] + layer.ffn(layer.up) + layer.ffn(layer.down),
        [
            ffn_out, ffn_out, out_whole((n, depth), F32), out_whole((n, depth), LOW),
            out_whole((n, depth), LOW), out_whole((n, 1), F32),
        ],
        [],
        flops=8 * n * depth * neurons,
        exps=4 * n * neurons,
    )


def add_rows(sums, row, value, at):
    value = jnp.sum(value, axis=0, keepdims=True)
    if at.start == 0:
        sums[row : row + 1, :] = value
    else:
        sums[row : row + 1, :] += value


def ffn_back_call(layer, grad, extra, kept, half):
    n, depth = grad.shape
    steps, _, size = layer.bias_up.shape
    per = steps // 2
    has_extra = extra is not None

    def body(grad, *refs):
        extra = refs[0] if has_extra else None
        (
            normed_one, recip_one, normed_two, recip_two, norms, slope, up_one, up_two, down_one, down_two,
            d_final_low, d_pre, d_mid, d_mid_low, sums, bias_sums, total,
        ) = refs[1:] if has_extra else refs
        i = pl.program_id(0)
        gain = lambda at: norms[at : at + 1, :]

        @pl.when(i == 0)
        def _():
            sums[...] = jnp.zeros_like(sums)
            for at in row_tiles(n):
                value = grad[at, :].astype(F32)
                if has_extra and at.start >= 2 * half:
                    value = value + extra[at.start - 2 * half : at.stop - 2 * half, :].astype(F32)
                normed = normed_two[at, :].astype(F32)
                back = normalize_back(value, normed, recip_two[at, :], gain(1))
                total[at, :] = back
                d_final_low[at, :] = back.astype(LOW)
                add_rows(sums, 1, value * normed, at)
                add_rows(sums, 5, value, at)
                add_rows(sums, 4, back, at)

        bias = None
        up, down = joined((up_one, up_two)), joined((down_one, down_two))
        for at in row_tiles(n):
            d_act = dot(d_final_low[at, :], down, 1, 0)
            low = (d_act * slope[0, at, :].astype(F32)).astype(LOW)
            d_pre[0, at, :] = low
            one = jnp.sum(low.astype(F32), axis=0, keepdims=True)
            bias = one if bias is None else bias + one
            total[at, :] += dot(low, up, 1, 1)
        bias_sums[0] = bias

        @pl.when(i == steps - 1)
        def _():
            for at in row_tiles(n):
                value = total[at, :]
                normed = normed_one[at, :].astype(F32)
                back = normalize_back(value, normed, recip_one[at, :], gain(0))
                d_mid[at, :] = back
                d_mid_low[at, :] = back.astype(LOW)
                add_rows(sums, 0, value * normed, at)
                add_rows(sums, 3, value, at)
                add_rows(sums, 2, back, at)

    neurons = per * size
    blocks = ((1, n, size), lambda i: (i // per, 0, i % per))
    return call(
        body, steps,
        [whole(grad)] + ([whole(extra)] if has_extra else []) + [
            whole(kept["normed_one"]), whole(kept["recip_one"]), whole(kept["normed_two"]),
            whole(kept["recip_two"]), whole(layer.norms), (kept["slope"],) + blocks,
        ] + layer.ffn(layer.up) + layer.ffn(layer.down),
        [
            out_whole((n, depth), LOW), ((2, n, neurons), LOW) + blocks, out_whole((n, depth), F32),
            out_whole((n, depth), LOW), out_whole((8, depth), F32), out_group((steps, 1, size), F32),
        ],
        [pltpu.VMEM((n, depth), F32)],
        flops=8 * n * depth * neurons,
    )


def ffn_back_first_call(layer, grad, extra, kept, half):
    n, depth = grad.shape
    steps, _, size = layer.bias_up.shape
    per = steps // 2

    def body(
        grad, extra, normed_two, recip_two, norms, slope, down_one, down_two,
        d_final, d_final_low, d_pre, sums, bias_sums,
    ):
        i = pl.program_id(0)

        @pl.when(i == 0)
        def _():
            sums[...] = jnp.zeros_like(sums)
            for at in row_tiles(n):
                value = grad[at, :]
                if at.start >= 2 * half:
                    value = value + extra[at.start - 2 * half : at.stop - 2 * half, :].astype(F32)
                normed = normed_two[at, :].astype(F32)
                back = normalize_back(value, normed, recip_two[at, :], norms[1:2, :])
                d_final[at, :] = back
                d_final_low[at, :] = back.astype(LOW)
                add_rows(sums, 1, value * normed, at)
                add_rows(sums, 5, value, at)
                add_rows(sums, 4, back, at)

        bias = None
        down = joined((down_one, down_two))
        for at in row_tiles(n):
            d_act = dot(d_final_low[at, :], down, 1, 0)
            low = (d_act * slope[0, at, :].astype(F32)).astype(LOW)
            d_pre[0, at, :] = low
            one = jnp.sum(low.astype(F32), axis=0, keepdims=True)
            bias = one if bias is None else bias + one
        bias_sums[0] = bias

    neurons = per * size
    blocks = ((1, n, size), lambda i: (i // per, 0, i % per))
    return call(
        body, steps,
        [
            whole(grad), whole(extra), whole(kept["normed_two"]), whole(kept["recip_two"]),
            whole(layer.norms), (kept["slope"],) + blocks,
        ] + layer.ffn(layer.down),
        [
            out_whole((n, depth), F32), out_whole((n, depth), LOW), ((2, n, neurons), LOW) + blocks,
            out_whole((8, depth), F32), out_group((steps, 1, size), F32),
        ],
        [],
        flops=4 * n * depth * neurons,
    )


def ffn_back_second_call(layer, d_final, d_pre, kept):
    n, depth = d_final.shape
    steps, _, size = layer.bias_up.shape
    per = steps // 2

    def body(d_final, d_pre, normed_one, recip_one, norms, up_one, up_two, d_mid, d_mid_low, sums):
        i = pl.program_id(0)

        @pl.when(i == 0)
        def _():
            d_mid[...] = d_final[...]

        up = joined((up_one, up_two))
        for at in row_tiles(n):
            d_mid[at, :] += dot(d_pre[0, at, :], up, 1, 1)

        @pl.when(i == steps - 1)
        def _():
            sums[...] = jnp.zeros_like(sums)
            for at in row_tiles(n):
                value = d_mid[at, :]
                normed = normed_one[at, :].astype(F32)
                back = normalize_back(value, normed, recip_one[at, :], norms[0:1, :])
                d_mid[at, :] = back
                d_mid_low[at, :] = back.astype(LOW)
                add_rows(sums, 0, value * normed, at)
                add_rows(sums, 3, value, at)
                add_rows(sums, 2, back, at)

    blocks = ((1, n, size), lambda i: (i // per, 0, i % per))
    return call(
        body, steps,
        [
            whole(d_final), (d_pre,) + blocks, whole(kept["normed_one"]), whole(kept["recip_one"]),
            whole(layer.norms),
        ] + layer.ffn(layer.up),
        [out_whole((n, depth), F32), out_whole((n, depth), LOW), out_whole((8, depth), F32)],
        [],
        flops=4 * n * depth * per * size,
    )


def shared_back_call(layer, d_mid_low, kept, segs, half):
    n, depth = d_mid_low.shape
    width, wide, own = layer.width, 3 * layer.width, 2 * half
    count = 2 * len(layer.qkv_blocks)

    def body(d_mid, proj, away, logsum, *refs):
        weights = pairs_of(refs[:count])
        out_one, out_two, segs_q, segs_k, d_proj, d_away, sums, back, mask, total = refs[count:]
        i = pl.program_id(0)
        make_mask(segs_q, segs_k, mask)
        out_cols = joined((out_one, out_two), slice(layer.out_from, layer.out_from + width))
        d_context = dot(d_mid[...], out_cols, 1, 0).astype(LOW)
        attend_back(
            width, [proj.at[0], away.at[0]], mask, logsum.at[0], d_context,
            [d_proj.at[0], d_away.at[0]], sums.at[0],
        )
        part = through_projection(d_away[0], weights, layer.used)

        @pl.when(i == 0)
        def _():
            total[...] = part

        @pl.when(i == 1)
        def _():
            back[...] = (total[...] + part).astype(LOW)

    return call(
        body, 2,
        [
            (d_mid_low, (half, depth), lambda i: (2, 0)), (kept["proj"], (1, half, wide), lambda i: (i, 2, 0)),
            per_group(kept["proj_away"]), per_group(kept["logsum_shared"]),
        ] + layer.qkv() + layer.out() + [whole(segs[None, :half]), whole(segs[:, None])],
        [
            out_group((2, half, wide), LOW), out_group((2, half, wide), LOW), out_group((2, 8, wide), F32),
            out_whole((half, depth), LOW),
        ],
        [pltpu.VMEM((own, half), F32), pltpu.VMEM((half, depth), F32)],
        flops=4 * half * depth * (wide + width) + 20 * own * half * width,
        exps=2 * own * half * width // HEAD_DIM,
    )


def own_back_call(layer, d_mid, d_mid_low, d_shared, kept, segs, half, with_rows):
    n, depth = d_mid_low.shape
    width, wide, own = layer.width, 3 * layer.width, 2 * half
    count = 2 * len(layer.qkv_blocks) if with_rows else 0

    def body(d_mid_low, d_shared, proj, logsum, out_one, out_two, segs_q, segs_k, *refs):
        i = pl.program_id(0)
        if with_rows:
            d_mid, weights = refs[0], pairs_of(refs[1 : count + 1])
            d_proj, sums, d_rows, mask = refs[count + 1 :]
        else:
            d_proj, sums, mask = refs
        make_mask(segs_q, segs_k, mask)
        out_cols = joined((out_one, out_two), slice(layer.out_from, layer.out_from + width))
        d_context = dot(d_mid_low[...], out_cols, 1, 0).astype(LOW)
        attend_back(
            width, [proj.at[0]], mask, logsum.at[0], d_context, [d_proj.at[0, :own]], sums.at[0]
        )
        d_proj[0, own:] = d_shared[0]
        if with_rows:
            part = through_projection(d_proj[0], weights, layer.used)

            @pl.when(i == 0)
            def _():
                d_rows[...] = d_mid[...] + part

            @pl.when(i == 1)
            def _():
                d_rows[...] += part

    return call(
        body, 2,
        [
            (d_mid_low, (own, depth), lambda i: (0, 0)), per_group(d_shared),
            (kept["proj"], (1, own, wide), lambda i: (i, 0, 0)), per_group(kept["logsum_own"]),
        ] + layer.out() + [whole(segs[None, :]), whole(segs[:, None])]
        + ([whole(d_mid)] + layer.qkv() if with_rows else []),
        [out_group((2, n, wide), LOW), out_group((2, 8, wide), F32)]
        + ([out_whole((n, depth), F32)] if with_rows else []),
        [pltpu.VMEM((own, own), F32)],
        flops=4 * depth * (n * wide * with_rows + own * width) + 20 * own * own * width,
        exps=2 * own * own * width // HEAD_DIM,
    )


def rows_back_call(layer, d_mid, d_proj):
    n, depth = d_mid.shape
    wide = 3 * layer.width

    def body(d_mid, d_proj, *refs):
        weights, d_rows = pairs_of(refs[:-1]), refs[-1]

        @pl.when(pl.program_id(0) == 0)
        def _():
            d_rows[...] = d_mid[...]

        d_rows[...] += through_projection(d_proj[0], weights, layer.used)

    return call(
        body, 2, [whole(d_mid), per_group(d_proj)] + layer.qkv(), [out_whole((n, depth), F32)], [],
        flops=4 * depth * n * wide,
    )[0]


class Grads:
    def __init__(self, entries, columns, cut):
        self.entries, self.columns, self.cut = entries, columns, cut
        sizes = [end - start for _, start, end in columns]
        self.size_a, self.size_b = sum(sizes[:cut]), sum(sizes[cut:])

    def inputs(self, at):
        out = []
        for pairs in self.entries:
            for left, right in pairs:
                out += [whole(left), per_group(right, at)]
        return out

    def scratch(self, rows):
        return [pltpu.VMEM((rows, left.shape[0]), LOW) for pairs in self.entries for left, _ in pairs]

    def flops(self, rows):
        depth = self.entries[0][0][0].shape[1]
        return sum(
            2 * rows * left.shape[0] * (2 * right.shape[2] + depth)
            for pairs in self.entries for left, right in pairs
        )

    def turn(self, pick, refs, turned):
        @pl.when(pl.program_id(0) == 0)
        def _():
            for at in range(len(turned)):
                turned[at][...] = dot(pick[...], refs[2 * at][...], 1, 1).astype(LOW)

    def product(self, refs, turned, entry, start, end):
        first = sum(len(pairs) for pairs in self.entries[:entry])
        total = None
        for at in range(first, first + len(self.entries[entry])):
            one = dot(turned[at][...], refs[2 * at + 1][0, :, start:end], 1, 0)
            total = one if total is None else total + one
        return total

    def send(self, pick):
        rows = pick.shape[0]
        size = self.size_a + self.size_b

        def body(pick, *refs):
            count = 2 * sum(len(pairs) for pairs in self.entries)
            out, turned = refs[count], refs[count + 1 :]
            self.turn(pick, refs, turned)
            col = 0
            for entry, start, end in self.columns:
                part = self.product(refs, turned, entry, start, end)
                out[0, :, col : col + end - start] = part.astype(LOW)
                col += end - start

        return call(
            body, 2, [whole(pick)] + self.inputs(lambda i: i), [out_group((2, rows, size), LOW)],
            self.scratch(rows), self.flops(rows),
        )[0]

    def keep(self, pick, got):
        rows = pick.shape[0]
        half = rows // 2
        size = self.size_a + self.size_b

        def body(pick, got, *refs):
            count = 2 * sum(len(pairs) for pairs in self.entries)
            send_a, keep_a, send_b, keep_b = refs[count : count + 4]
            turned = refs[count + 4 :]
            i = pl.program_id(0)
            self.turn(pick, refs, turned)
            col = 0
            for at, (entry, start, end) in enumerate(self.columns):
                part = self.product(refs, turned, entry, start, end)
                part = part + got[0, :, col : col + end - start].astype(F32)
                if at < self.cut:
                    place = slice(col, col + end - start)

                    @pl.when(i == 0)
                    def _():
                        send_a[:, place] = part.astype(LOW)

                    @pl.when(i == 1)
                    def _():
                        keep_a[:, place] = part
                else:
                    place = slice(col - self.size_a, col - self.size_a + end - start)
                    keep_b[0, :, place] = part[:half]
                    send_b[0, :, place] = part[half:].astype(LOW)
                col += end - start

        return call(
            body, 2,
            [whole(pick), per_group(got, lambda i: 1 - i)] + self.inputs(lambda i: 1 - i),
            [
                out_whole((rows, self.size_a), LOW), out_whole((rows, self.size_a), F32),
                out_group((2, half, self.size_b), LOW), out_group((2, half, self.size_b), F32),
            ],
            self.scratch(rows), self.flops(rows),
        )


class Reduce:
    def __init__(self, grads, pick_send, pick_keep):
        self.grads, self.pick_keep = grads, pick_keep
        self.sends = (grads.send(pick_send),)
        self.got = (swap_core(self.sends[0]),)
        self.work = self._run()

    def _run(self):
        count = lax.axis_size("dp") // 4
        send_a, keep_a, send_b, keep_b = self.grads.keep(self.pick_keep, self.got[0])
        fourth = keep_a.shape[0] // 2
        self.sends = (send_a, send_b)
        self.got = (swap_y(send_a), swap_x(send_b))
        yield
        a = keep_a + self.got[0].astype(F32)
        b = keep_b + self.got[1].astype(F32)
        self.sends = (a[fourth:].astype(LOW), b[0].astype(LOW))
        self.got = (swap_x(self.sends[0]), swap_y(self.sends[1]))
        a, b = a[:fourth], b[1]
        yield
        both = jnp.concatenate([a + self.got[0].astype(F32), b + self.got[1].astype(F32)], axis=1)
        both = both.reshape((count, -1) + both.shape[1:])
        self.sends = tuple(both[back].astype(LOW) for back in range(1, count))
        self.got = tuple(ring_shift(send, -back) for back, send in enumerate(self.sends, 1))
        yield
        total = both[0] + sum(got.astype(F32) for got in self.got)
        self.total = total
        self.got = self.sends = ()

    def step(self):
        next(self.work, None)


class Total:
    def __init__(self, value):
        self.total = value
        self.work = self._run()
        self.step()

    def _run(self):
        n = lax.axis_size("dp")
        self.sends = (self.total,)
        self.got = (swap_y(self.total),)
        yield
        self.total = self.total + self.got[0]
        step = 1
        while step < n:
            self.sends = (self.total,)
            self.got = (lax.ppermute(self.total, "dp", [(i, i ^ step) for i in range(n)]),)
            yield
            self.total = self.total + self.got[0]
            step *= 2
        self.got = self.sends = ()

    def step(self):
        next(self.work, None)


def round_of(*works):
    ended = lax.optimization_barrier(tuple(work.got for work in works))
    for work, got in zip(works, ended):
        work.got = got
    for work in works:
        work.step()


def before(value, *works):
    value, ended = lax.optimization_barrier((value, tuple(work.got for work in works)))
    for work, got in zip(works, ended):
        work.got = got
    return value


def forward_attn(layer, rows, proj, context_own, logsum_own, rows_low, away_low, segs, half):
    proj_away, context, logsum_shared, hidden, hidden_low, normed_one, recip_one = shared_call(
        layer, rows, proj, away_low, context_own, segs[1], half
    )
    kept = dict(
        rows_low=rows_low, away_low=away_low, proj=proj, proj_away=proj_away, context=context,
        logsum_own=logsum_own, logsum_shared=logsum_shared, hidden_low=hidden_low,
        normed_one=normed_one, recip_one=recip_one,
    )
    return hidden, kept


def forward_ffn(layer, hidden, kept):
    act, slope, output, output_low, normed_two, recip_two = ffn_call(layer, hidden, kept["hidden_low"])
    kept.update(act=act, slope=slope, normed_two=normed_two, recip_two=recip_two)
    return output, output_low


def backward_ffn(layer, grad, extra, kept, half):
    d_final_low, d_pre, d_mid, d_mid_low, sums, bias_sums = ffn_back_call(layer, grad, extra, kept, half)
    entries = [[(kept["hidden_low"], d_pre)], [(d_final_low, kept["act"])]]
    return d_mid, d_mid_low, sums[:6], bias_sums, entries


def attn_entries(kept, d_proj, d_away, d_mid_low):
    return [[(kept["rows_low"], d_proj), (kept["away_low"], d_away)], [(d_mid_low, kept["context"])]]


def on_device(
    tokens, segment_ids, out_grad,
    t_qkv, t_qv_bias, t_out, t_up, t_up_bias, t_down, t_gains, t_shifts,
    s_qkv, s_qv_bias, s_out, s_up, s_up_bias, s_down, s_gains, s_shifts,
):
    rows, half, width = tokens.shape
    first = lax.axis_index("mp") == 0
    own_row = lambda value: jnp.where(first, value[0], value[2])
    far_row = lambda value: jnp.where(first, value[2], value[0])

    norm_rows = jnp.concatenate([t_gains, t_shifts, s_gains, s_shifts], axis=0)
    norm_rows = jnp.pad(norm_rows, ((0, 128 - norm_rows.shape[0]), (0, 0)))
    t_width, s_width = t_qkv.shape[2], s_qkv.shape[2]
    size = s_up.shape[1]
    per = t_up.shape[1] // size
    count, block = lax.axis_size("dp") // 4, t_up.shape[0]
    together = lambda *values: lax.optimization_barrier(values)
    every = slice(None)

    def columns(start, width):
        return slice(start, start + width)

    t_cut, t_all = 2 * t_width, 4 * t_width + 128
    f_cut = per * size
    s_cut = size + 2 * s_width
    packed_t, packed_f, student_a, student_b = pack(
        [t_qkv, t_up, s_up, s_qkv], [t_out, norm_rows, t_down, s_out, s_down],
        [(block, t_all), (block, 2 * f_cut), (block, s_cut), (block, s_cut)],
        [(0, (i,), 0, (every, columns(i * t_width, t_width))) for i in range(3)]
        + [
            (4, (), 0, (every, columns(3 * t_width, t_width))), (5, (), 0, (every, columns(4 * t_width, 128))),
            (1, (every,), 1, (every, columns(0, f_cut))), (6, (), 1, (every, columns(f_cut, f_cut))),
            (2, (every,), 2, (every, columns(0, size))), (3, (0,), 2, (every, columns(size, s_width))),
            (7, (), 2, (every, columns(size + s_width, s_width))), (8, (), 3, (every, columns(0, size))),
            (3, (1,), 3, (every, columns(size, s_width))), (3, (2,), 3, (every, columns(size + s_width, s_width))),
        ],
    )

    def along_z(value):
        return [value] + [ring_shift(value, at) for at in range(1, count)]

    def of_line(pieces, cut):
        rest = pieces[0].shape[1] - cut
        return moves(
            pieces, [(count, block, cut), (count, block, rest)],
            [(i, (every, columns(start, wide)), at, (i,)) for i in range(count)
             for at, (start, wide) in enumerate(((0, cut), (cut, rest)))],
        )

    def first_plane(a, got_a, b, got_b):
        return moves(
            [a, got_a, b, got_b], [(2,) + a.shape, (2,) + b.shape],
            [(0, (every,), 0, (0,)), (1, (every,), 0, (1,)), (2, (every,), 1, (0,)), (3, (every,), 1, (1,))],
        )

    def both_planes(a, got_a, b, got_b, order):
        copies, col = [], 0
        for of_b, start, wide in order:
            taken, place = (every, every, every, columns(start, wide)), (every, every, columns(col, wide))
            if of_b:
                copies += [(2, taken, 0, (every, 0) + place), (3, taken, 0, (every, 1) + place)]
            else:
                copies += [(0, taken, 0, (0, every) + place), (1, taken, 0, (1, every) + place)]
            col += wide
        out = moves([a, got_a, b, got_b], [(2, 2, count, block, col)], copies)[0]
        return out.reshape(2, width // 2, col)

    def with_core(own):
        return own, swap_core(own)

    bias_parts = [t_qv_bias[0], t_qv_bias[1], t_up_bias, s_qv_bias[0], s_qv_bias[1], s_up_bias]
    line_t, got_own = along_z(packed_t), swap_y(far_row(tokens))
    line_f = along_z(packed_f)
    *line_t, line_f[1], got_own = together(*line_t, line_f[1], got_own)
    attn_a, attn_b = of_line(line_t, t_cut)
    got_a, got_b, student_x, student_y = swap_x(attn_a), swap_y(attn_b), swap_x(student_a), swap_y(student_b)
    got_a, got_b, student_x, student_y, *line_f[2:-1] = together(
        got_a, got_b, student_x, student_y, *line_f[2:-1]
    )
    attn_a, attn_b = first_plane(attn_a, got_a, attn_b, got_b)
    got_a, got_b = swap_y(attn_a), swap_x(attn_b)
    line_s = along_z(moves(
        [student_a, student_x, student_b, student_y], [(2, block, 2 * s_cut)],
        [(i, (every,), 0, (i % 2, every, columns(i // 2 * s_cut, s_cut))) for i in range(4)],
    )[0])
    got_a, got_b, line_f[-1] = together(got_a, got_b, line_f[-1])
    attn = both_planes(
        attn_a, got_a, attn_b, got_b, [(False, 0, t_cut), (True, 0, t_all - t_cut)]
    )
    attn = with_core(attn)
    ffn_a, ffn_b = of_line(line_f, f_cut)
    got_a, got_b = swap_x(ffn_a), swap_y(ffn_b)
    bias_own = jnp.concatenate(bias_parts)
    bias_far = swap_y(bias_own)
    attn, got_a, got_b, bias_far, line_s[1] = together(attn, got_a, got_b, bias_far, line_s[1])
    ffn_a, ffn_b = first_plane(ffn_a, got_a, ffn_b, got_b)
    got_a, got_b = swap_y(ffn_a), swap_x(ffn_b)
    got_shared = swap_y(tokens[1])
    norms = jnp.concatenate([half[0, :, -128:-116] for half in attn], axis=0).T.astype(F32)
    norms_of = lambda at: jnp.pad(norms[at : at + 6], ((0, 2), (0, 0)))
    bias_all = jnp.stack([bias_own, bias_far]).astype(F32)
    cuts = [0]
    for part in bias_parts:
        cuts.append(cuts[-1] + part.shape[0])
    pick = [bias_all[:, cuts[i] : cuts[i + 1]] for i in range(6)]
    bias_qkv = lambda q, v: jnp.concatenate([q, jnp.zeros_like(q), v], axis=1)[:, None, :]
    teacher = Layer(
        t_width, None, None, [(attn, t_width, i, t_width) for i in range(3)], (attn, t_width, 3, t_width), 0,
        norms_of(0), bias_qkv(pick[0], pick[1]), pick[2].reshape(2 * per, 1, size),
    )

    to_own = feature_order(width)
    into = (lax.iota(jnp.int32, width)[:, None] == to_own[None, :]).astype(LOW)
    reorder = lambda value: jnp.dot(value, into, preferred_element_type=F32).astype(LOW)
    pick_all = jnp.eye(width, dtype=LOW)
    pick_keep, pick_send = pick_all[: width // 2], pick_all[width // 2 :]

    inputs = reorder(jnp.concatenate([own_row(tokens), got_own, tokens[1]], axis=0))
    spin = lambda segs: jnp.where(first, segs, jnp.roll(segs, half))
    segs = (spin(own_row(segment_ids)), spin(segment_ids[1]))
    grad_in = jnp.concatenate([own_row(out_grad), swap_y(far_row(out_grad)), out_grad[1]], axis=0)

    inputs, ffn_a, ffn_b = together(inputs, ffn_a, ffn_b)
    proj, context_own, logsum_own = project_call(teacher, inputs, segs[0], half)
    proj, got_shared, *line_s[2:-1] = together(proj, got_shared, *line_s[2:-1])
    away_low = reorder(got_shared)
    hidden, t_kept = forward_attn(
        teacher, inputs, proj, context_own, logsum_own, inputs, away_low, segs, half
    )
    hidden, got_a, got_b, line_s[-1] = together(hidden, got_a, got_b, line_s[-1])
    ffn = both_planes(ffn_a, got_a, ffn_b, got_b, [(False, 0, f_cut), (True, 0, f_cut)])
    ffn = with_core(ffn)
    student_a, student_b = moves(
        line_s, [(2, count, block, s_cut)] * 2,
        [(i, (every, every, columns(at * s_cut, s_cut)), at, (every, i)) for i in range(count) for at in range(2)],
    )
    got_a, got_b = swap_y(student_a), swap_x(student_b)
    hidden, ffn = together(hidden, ffn)
    teacher.up, teacher.down = (ffn, 0), (ffn, per)
    middle, middle_low = forward_ffn(teacher, hidden, t_kept)
    away_low = swap_y(middle_low[2 * half :])
    middle_low, got_a, got_b, grad_in = together(middle_low, got_a, got_b, grad_in)
    grad_in = reorder(grad_in)
    student_w = with_core(both_planes(
        student_a, got_a, student_b, got_b,
        [(False, 0, size), (True, 0, size), (False, size, 2 * s_width), (True, size, 2 * s_width)],
    ))
    narrow = 2 * s_width
    place = 2 * size // narrow
    student = Layer(
        s_width, (student_w, 0), (student_w, 1),
        [(student_w, narrow, place, s_width), (student_w, narrow, place + 1, narrow)],
        (student_w, narrow, place, s_width), s_width, norms_of(6), bias_qkv(pick[3], pick[4]),
        pick[5].reshape(2, 1, size),
    )
    proj, context_own, logsum_own = project_call(student, middle_low, segs[0], half)
    proj, away_low = together(proj, away_low)
    hidden, s_kept = forward_attn(
        student, middle, proj, context_own, logsum_own, middle_low, away_low, segs, half
    )
    last, _ = forward_ffn(student, hidden, s_kept)

    def far_half(value):
        return swap_y(value[half : 2 * half].astype(LOW))

    def to_rows(value, far):
        near = jnp.concatenate([value[:half], value[2 * half :]], axis=0)
        high = near.astype(LOW)
        low = (near - high.astype(F32)).astype(LOW)
        back = lambda part: jnp.einsum("nr,dr->nd", part, into, preferred_element_type=F32)
        near, far = back(high) + back(low), back(far)
        return jnp.stack([jnp.where(first, near[:half], far), near[half:], jnp.where(first, far, near[:half])])

    far_last = far_half(last)

    d_mid, d_mid_low, s_norm_grads, s_up_grad, s_entries = backward_ffn(student, grad_in, None, s_kept, half)
    d_shared, d_away, s_sums_b, back = shared_back_call(student, d_mid_low, s_kept, segs[1], half)
    extra = swap_y(back)
    d_shared, far_last = together(d_shared, far_last)
    d_proj, s_sums_a, d_rows = own_back_call(
        student, d_mid, d_mid_low, d_shared, s_kept, segs[0], half, True
    )
    d_proj, extra = lax.optimization_barrier((d_proj, extra))
    s_entries += attn_entries(s_kept, d_proj, d_away, d_mid_low)
    s_columns = [(0, 0, size), (2, 0, s_width), (3, 0, s_width), (1, 0, size), (2, s_width, 3 * s_width)]
    reduce_s = Reduce(Grads(s_entries, s_columns, 3), pick_send, pick_keep)

    d_rows = after(d_rows, reduce_s.sends)
    d_final, d_final_low, d_pre, t_sums_two, t_up_grad = ffn_back_first_call(
        teacher, d_rows, extra, t_kept, half
    )
    d_pre = before(d_pre, reduce_s)
    reduce_s.step()
    d_pre = after(d_pre, reduce_s.sends)
    f_entries = [[(t_kept["hidden_low"], d_pre)], [(d_final_low, t_kept["act"])]]
    reduce_f = Reduce(
        Grads(f_entries, [(0, 0, per * size), (1, 0, per * size)], 1), pick_send, pick_keep
    )
    d_pre = after(d_pre, reduce_f.sends)
    d_mid, d_mid_low, t_sums_one = ffn_back_second_call(teacher, d_final, d_pre, t_kept)
    t_norm_grads = (t_sums_one + t_sums_two)[:6]
    d_mid_low = before(d_mid_low, reduce_f)
    reduce_f.step()
    reduce_s.got = after(reduce_s.got, reduce_f.sends)
    d_mid_low = before(d_mid_low, reduce_s)
    reduce_s.step()
    d_mid_low = after(d_mid_low, reduce_s.sends)
    d_shared, d_away, t_sums_b, back = shared_back_call(teacher, d_mid_low, t_kept, segs[1], half)
    extra = swap_y(back)
    d_shared = before(d_shared, reduce_s)
    reduce_s.step()
    d_shared = after(d_shared, reduce_s.sends)
    d_proj, t_sums_a = own_back_call(teacher, None, d_mid_low, d_shared, t_kept, segs[0], half, False)
    t_entries = attn_entries(t_kept, d_proj, d_away, d_mid_low)
    reduce_t = Reduce(
        Grads(t_entries, [(0, 0, 2 * t_width), (0, 2 * t_width, 3 * t_width), (1, 0, t_width)], 1),
        pick_send, pick_keep,
    )

    def qv_grad(one, two, wide):
        sums = one[:, 0] + two[:, 0]
        sums = jnp.concatenate([sums[:, :wide], sums[:, 2 * wide :]], axis=1)
        return jnp.pad(sums, ((0, 0), (0, width - 2 * wide)))

    norm_grads = jnp.concatenate([t_norm_grads, s_norm_grads], axis=0)
    norm_grads = jnp.einsum("nr,dr->nd", norm_grads, into.astype(F32), precision=lax.Precision.HIGHEST)
    qv_t, qv_s = qv_grad(t_sums_a, t_sums_b, t_width), qv_grad(s_sums_a, s_sums_b, s_width)
    mine = jnp.concatenate([t_up_grad[:per, 0], s_up_grad[:1, 0], qv_t[:1], qv_s[:1]], axis=0)
    other = jnp.concatenate([t_up_grad[per:, 0], s_up_grad[1:, 0], qv_t[1:], qv_s[1:]], axis=0)
    small = Total(jnp.concatenate(
        [norm_grads, jnp.where(first, mine, other), jnp.where(first, other, mine)], axis=0
    ))
    reduce_f.got = after(reduce_f.got, reduce_t.sends)
    round_of(reduce_f, small)
    reduce_t.got = after(reduce_t.got, reduce_f.sends)
    reduce_t.step()
    reduce_f.got = after(reduce_f.got, reduce_t.sends)
    round_of(reduce_f, reduce_s)
    d_rows = rows_back_call(teacher, *after((d_mid, d_proj), reduce_t.sends))
    reduce_t.got = after(reduce_t.got, d_rows)
    far_rows = far_half(d_rows)
    round_of(reduce_t, small)
    d_rows, last = after((d_rows, last), reduce_t.sends)
    d_rows = jnp.concatenate([d_rows[: 2 * half], d_rows[2 * half :] + extra.astype(F32)], axis=0)
    input_grad, output = to_rows(d_rows, far_rows), to_rows(last, far_last)
    round_of(reduce_t, reduce_f, small)
    round_of(reduce_t, small)
    for work in (reduce_t, reduce_f, reduce_s, small):
        while work.got:
            work.step()
    s_sum, f_sum, t_sum, small = reduce_s.total, reduce_f.total, reduce_t.total, small.total

    piece = width // lax.axis_size("dp")
    norm_sum = lax.dynamic_slice_in_dim(small[:12], lax.axis_index("dp") * piece, piece, 1)
    bias_sum = small[12:].reshape(2, -1, width)
    bias_sum = jnp.where(first, bias_sum[0], bias_sum[1])
    t_qv_sum, s_qv_sum = bias_sum[per + 1], bias_sum[per + 2, : 2 * s_width]

    def cut(value, *sizes):
        out = []
        for one in sizes:
            out.append(value[:, :one])
            value = value[:, one:]
        return out

    tq, tk, tv, to = cut(t_sum, t_width, t_width, t_width, t_width)
    t_up_sum, t_down_sum = cut(f_sum, per * size, per * size)
    s_up_sum, sq, so, s_down_sum, sk, sv = cut(s_sum, size, s_width, s_width, size, s_width, s_width)
    return (
        output, input_grad,
        jnp.stack([tq, tk, tv]), t_qv_sum.reshape(2, -1), to.T, t_up_sum, bias_sum[:per].reshape(-1),
        t_down_sum.T,
        norm_sum[0:2], norm_sum[2:6],
        jnp.stack([sq, sk, sv]), s_qv_sum.reshape(2, -1), so.T, s_up_sum, bias_sum[per], s_down_sum.T,
        norm_sum[6:8], norm_sum[8:12],
    )


def solution(mesh):
    layer = (
        P(None, "dp", "mp"), P(None, "mp"), P("mp", "dp"), P("dp", "mp"), P("mp"), P("mp", "dp"),
        P(None, "dp"), P(None, "dp"),
    )
    rows = P("dp", "mp", None)
    return jax.shard_map(
        on_device,
        mesh=mesh,
        in_specs=(rows, P("dp", None), rows) + layer + layer,
        out_specs=(rows, rows) + layer + layer,
        check_vma=False,
    )
```

```python
import functools
import math

import jax
import jax.numpy as jnp
from jax import lax
from jax.experimental import pallas as pl
from jax.experimental.pallas import tpu as pltpu
from jax.sharding import PartitionSpec as P

HEAD_DIM = 64
LOW = jnp.bfloat16
F32 = jnp.float32


def ring_of(count):
    return list(range(0, count, 2)) + list(range(1, count, 2))[::-1]


def swap_y(value):
    return lax.ppermute(value, "mp", [(0, 1), (1, 0)])


def swap_x(value):
    n = lax.axis_size("dp")
    return lax.ppermute(value, "dp", [(i, i ^ 2) for i in range(n)])


def swap_core(value):
    n = lax.axis_size("dp")
    return lax.ppermute(value, "dp", [(i, i ^ 1) for i in range(n)])


def ring_shift(value, step):
    count = lax.axis_size("dp") // 4
    ring = ring_of(count)
    pairs = []
    for place in range(count):
        for low in range(4):
            pairs.append((ring[place] * 4 + low, ring[(place + step) % count] * 4 + low))
    return lax.ppermute(value, "dp", pairs)


def feature_order(width):
    n = lax.axis_size("dp")
    count, rows = n // 4, width // n
    me = lax.axis_index("dp")
    z, x, core = me // 4, (me // 2) % 2, me % 2
    place = jnp.where(z % 2 == 0, z // 2, count - 1 - z // 2)
    at = lax.iota(jnp.int32, width)
    row = at % rows
    back = (at // rows) % count
    x_rel = (at // (rows * count)) % 2
    core_rel = at // (rows * count * 2)
    from_place = (place - back + count) % count
    half = (count + 1) // 2
    z_abs = jnp.where(from_place < half, 2 * from_place, 2 * (count - 1 - from_place) + 1)
    block = z_abs * 4 + (x ^ x_rel) * 2 + (core ^ core_rel)
    return block * rows + row


def after(value, *others):
    return lax.optimization_barrier((value, others))[0]


VMEM_BYTES = 48 << 20
TILE = 256


def dot(left, right, left_at, right_at):
    return lax.dot_general(
        left, right, (((left_at,), (right_at,)), ((), ())), preferred_element_type=F32
    )


def call(body, steps, inputs, outputs, scratch, flops, exps=0):
    size = lambda shape, dtype: math.prod(shape) * jnp.dtype(dtype).itemsize
    moved = sum(size(array.shape, array.dtype) for array, _, _ in inputs)
    moved += sum(size(shape, dtype) for shape, dtype, _, _ in outputs)
    return pl.pallas_call(
        body,
        grid=(steps,),
        in_specs=[pl.BlockSpec(block, index) for _, block, index in inputs],
        out_specs=[pl.BlockSpec(block, index) for _, _, block, index in outputs],
        out_shape=[jax.ShapeDtypeStruct(shape, dtype) for shape, dtype, _, _ in outputs],
        scratch_shapes=scratch,
        compiler_params=pltpu.CompilerParams(
            dimension_semantics=("arbitrary",), vmem_limit_bytes=VMEM_BYTES
        ),
        cost_estimate=pl.CostEstimate(
            flops=flops // 2, bytes_accessed=moved // 2, transcendentals=exps // 2
        ),
    )(*[array for array, _, _ in inputs])


def moves(arrays, shapes, copies):
    def body(*refs):
        for source, taken, target, place in copies:
            refs[len(arrays) + target][place] = refs[source][taken]

    moved = 2 * sum(math.prod(shape) for shape in shapes)
    return pl.pallas_call(
        body,
        out_shape=[jax.ShapeDtypeStruct(shape, LOW) for shape in shapes],
        compiler_params=pltpu.CompilerParams(vmem_limit_bytes=VMEM_BYTES),
        cost_estimate=pl.CostEstimate(flops=0, bytes_accessed=moved, transcendentals=0),
    )(*arrays)


def pack(straight, turned, shapes, copies):
    count = len(straight)

    def body(*refs):
        outs = refs[count + len(turned) :]
        rows = turned[0].shape[1]
        at = lambda axis: lax.broadcasted_iota(jnp.int32, (rows, rows), axis)
        same = jnp.where(at(0) == at(1), 1.0, 0.0).astype(LOW)
        for source, taken, target, place in copies:
            if source < count:
                outs[target][place] = refs[source][taken]
            else:
                outs[target][place] = dot(same, refs[source][...], 1, 1).astype(LOW)

    moved = 2 * sum(math.prod(shape) for shape in shapes)
    return pl.pallas_call(
        body,
        out_shape=[jax.ShapeDtypeStruct(shape, LOW) for shape in shapes],
        compiler_params=pltpu.CompilerParams(vmem_limit_bytes=VMEM_BYTES),
        cost_estimate=pl.CostEstimate(flops=0, bytes_accessed=moved, transcendentals=0),
    )(*straight, *turned)


def whole(array):
    rank = array.ndim
    return (array, array.shape, lambda i: (0,) * rank)


def per_group(array, at=lambda i: i):
    return (array, (1,) + array.shape[1:], lambda i: (at(i),) + (0,) * (array.ndim - 1))


def out_whole(shape, dtype):
    return (shape, dtype, shape, lambda i: (0,) * len(shape))


def out_group(shape, dtype, at=lambda i: i):
    return (shape, dtype, (1,) + shape[1:], lambda i: (at(i),) + (0,) * (len(shape) - 1))


class Layer:
    def __init__(self, width, up, down, qkv, out, out_from, norms, bias_qkv, bias_up):
        self.width, self.up, self.down = width, up, down
        self.qkv_blocks, self.out_block, self.out_from = qkv, out, out_from
        self.norms, self.bias_qkv, self.bias_up = norms, bias_qkv, bias_up
        self.used = [block[3] for block in qkv]

    def columns(self, block, at):
        pair, size, place, _ = block
        return [(half, (1, half.shape[1], size), lambda i: (at(i), 0, place)) for half in pair]

    def qkv(self, at=lambda i: i):
        return [one for block in self.qkv_blocks for one in self.columns(block, at)]

    def out(self, at=lambda i: i):
        return self.columns(self.out_block, at)

    def ffn(self, where):
        pair, base = where
        size, per = self.bias_up.shape[2], self.bias_up.shape[0] // 2
        return [(half, (1, half.shape[1], size), lambda i: (i // per, 0, base + i % per)) for half in pair]


def joined(pair, cols=slice(None)):
    return jnp.concatenate([half[0, :, cols] for half in pair], axis=0)


def pairs_of(refs):
    return [refs[at : at + 2] for at in range(0, len(refs), 2)]


def put_projection(rows, weights, used, bias, target):
    start = 0
    for weight, cols in zip(weights, used):
        part = dot(rows, joined(weight, slice(0, cols)), 1, 0) + bias[0, :, start : start + cols]
        target[:, start : start + cols] = part.astype(LOW)
        start += cols


def through_projection(grads, weights, used):
    start = 0
    total = None
    for weight, cols in zip(weights, used):
        part = dot(grads[:, start : start + cols], joined(weight, slice(0, cols)), 1, 1)
        total = part if total is None else total + part
        start += cols
    return total


def head_at(width, part, head):
    return slice(part * width + head * HEAD_DIM, part * width + (head + 1) * HEAD_DIM)


def join(parts, cols):
    picked = [part[:, cols] for part in parts]
    return picked[0] if len(picked) == 1 else jnp.concatenate(picked, axis=0)


def attend(width, kept, mask, logsum):
    scale = jnp.asarray(HEAD_DIM**-0.5, LOW)
    out = []
    for head in range(width // HEAD_DIM):
        query = kept[0][:, head_at(width, 0, head)] * scale
        scores = dot(join(kept, head_at(width, 1, head)), query, 1, 1) + mask[...]
        top = jnp.max(scores, axis=0, keepdims=True)
        expo = jnp.exp(scores - top)
        total = jnp.sum(expo, axis=0, keepdims=True)
        out.append(dot(join(kept, head_at(width, 2, head)), expo.astype(LOW), 0, 0) * (1.0 / total))
        logsum[head : head + 1, :] = top + jnp.log(total)
    return jnp.concatenate(out, axis=0).T.astype(LOW)


def attend_back(width, kept, mask, logsum, d_context, grads, sums):
    scale = jnp.asarray(HEAD_DIM**-0.5, LOW)
    for head in range(width // HEAD_DIM):
        at_q, at_k, at_v = (head_at(width, part, head) for part in range(3))
        query = kept[0][:, at_q] * scale
        keys = join(kept, at_k)
        d_ctx = d_context[:, head * HEAD_DIM : (head + 1) * HEAD_DIM]
        probs = jnp.exp(dot(keys, query, 1, 1) + mask[...] - logsum[head : head + 1, :])
        d_probs = dot(join(kept, at_v), d_ctx, 1, 1)
        both = probs * d_probs
        inner = jnp.sum(both, axis=0, keepdims=True)
        d_scores = (both - probs * inner).astype(LOW)
        d_values = dot(probs.astype(LOW), d_ctx, 1, 0).astype(LOW)
        d_keys = dot(d_scores, query, 1, 0).astype(LOW)
        d_query = dot(keys * scale, d_scores, 0, 0).T.astype(LOW)
        grads[0][:, at_q] = d_query
        start = 0
        for grad in grads:
            rows = grad.shape[0]
            grad[:, at_k] = d_keys[start : start + rows]
            grad[:, at_v] = d_values[start : start + rows]
            start += rows
        for grad in grads[1:]:
            grad[:, at_q] = jnp.zeros((grad.shape[0], HEAD_DIM), LOW)
        sums[0:1, at_q] = jnp.sum(d_query.astype(F32), axis=0, keepdims=True)
        sums[0:1, at_k] = jnp.zeros((1, HEAD_DIM), F32)
        sums[0:1, at_v] = jnp.sum(d_values.astype(F32), axis=0, keepdims=True)


def make_mask(segs_q, segs_k, mask):
    @pl.when(pl.program_id(0) == 0)
    def _():
        mask[...] = jnp.where(segs_k[...] == segs_q[...], 0.0, -1e9)


def normalize(value, gain, shift):
    center = value - jnp.mean(value, axis=-1, keepdims=True)
    recip = lax.rsqrt(jnp.mean(center * center, axis=-1, keepdims=True) + 1e-06)
    normed = center * recip
    return normed * gain + shift, normed, recip


def normalize_back(grad, normed, recip, gain):
    scaled = grad * gain
    mean_one = jnp.mean(scaled, axis=-1, keepdims=True)
    mean_two = jnp.mean(scaled * normed, axis=-1, keepdims=True)
    return recip * (scaled - mean_one - normed * mean_two)


def row_tiles(rows):
    return [slice(start, start + TILE) for start in range(0, rows, TILE)]


def project_call(layer, rows_low, segs, half):
    n, depth = rows_low.shape
    width, wide, own = layer.width, 3 * layer.width, 2 * half
    count = 2 * len(layer.qkv_blocks)

    def body(rows, *refs):
        weights = pairs_of(refs[:count])
        bias, segs_q, segs_k, proj, context, logsum, mask = refs[count:]
        make_mask(segs_q, segs_k, mask)
        put_projection(rows[...], weights, layer.used, bias, proj.at[0])
        context[0] = attend(width, [proj.at[0, :own]], mask, logsum.at[0])

    return call(
        body, 2,
        [whole(rows_low)] + layer.qkv() + [
            per_group(layer.bias_qkv), whole(segs[None, :]), whole(segs[:, None])
        ],
        [
            out_group((2, n, wide), LOW), out_group((2, own, width), LOW), out_group((2, 8, own), F32),
        ],
        [pltpu.VMEM((own, own), F32)],
        flops=4 * n * depth * wide + 8 * own * own * width,
        exps=2 * own * own * width // HEAD_DIM,
    )


def shared_call(layer, rows, proj, away_low, context_own, segs, half):
    n, depth = rows.shape
    width, wide, own = layer.width, 3 * layer.width, 2 * half
    count = 2 * len(layer.qkv_blocks)

    def body(rows, proj, away, *refs):
        weights = pairs_of(refs[:count])
        (
            out_one, out_two, bias, segs_q, segs_k, context_own, norms,
            proj_away, context, logsum, hidden, hidden_low, normed_one, recip_one, mask, total,
        ) = refs[count:]
        i = pl.program_id(0)
        make_mask(segs_q, segs_k, mask)
        put_projection(away[...], weights, layer.used, bias, proj_away.at[0])
        context[0, :own] = context_own[0]
        context[0, own:] = attend(width, [proj.at[0], proj_away.at[0]], mask, logsum.at[0])
        out_cols = joined((out_one, out_two), slice(layer.out_from, layer.out_from + width))

        @pl.when(i == 0)
        def _():
            total[...] = dot(context[0], out_cols, 1, 1)

        @pl.when(i == 1)
        def _():
            for at in row_tiles(n):
                value = rows[at, :].astype(F32) + norms[2:3, :]
                value = value + (total[at, :] + dot(context[0, at], out_cols, 1, 1))
                value, normed, recip = normalize(value, norms[0:1, :], norms[3:4, :])
                hidden[at, :] = value
                hidden_low[at, :] = value.astype(LOW)
                normed_one[at, :] = normed.astype(LOW)
                recip_one[at, :] = recip

    return call(
        body, 2,
        [
            whole(rows), (proj, (1, half, wide), lambda i: (i, 2, 0)), whole(away_low),
        ] + layer.qkv() + layer.out() + [
            per_group(layer.bias_qkv), whole(segs[None, :half]),
            whole(segs[:, None]), per_group(context_own), whole(layer.norms),
        ],
        [
            out_group((2, half, wide), LOW), out_group((2, n, width), LOW), out_group((2, 8, half), F32),
            out_whole((n, depth), F32), out_whole((n, depth), LOW), out_whole((n, depth), LOW),
            out_whole((n, 1), F32),
        ],
        [pltpu.VMEM((own, half), F32), pltpu.VMEM((n, depth), F32)],
        flops=4 * depth * (n * width + half * wide) + 8 * own * half * width,
        exps=2 * own * half * width // HEAD_DIM,
    )


def ffn_call(layer, hidden, hidden_low):
    n, depth = hidden.shape
    steps, _, size = layer.bias_up.shape
    per = steps // 2

    def body(
        hidden, hidden_low, norms, bias_up, up_one, up_two, down_one, down_two,
        act, slope, output, output_low, normed_two, recip_two,
    ):
        i = pl.program_id(0)

        @pl.when(i == 0)
        def _():
            output[...] = hidden[...] + norms[4:5, :]

        up, down = joined((up_one, up_two)), joined((down_one, down_two))
        for at in row_tiles(n):
            pre = dot(hidden_low[at, :], up, 1, 0) + bias_up[0]
            bell = 0.5 + 0.5 * lax.erf(pre * math.sqrt(0.5))
            low = (pre * bell).astype(LOW)
            act[0, at, :] = low
            slope[0, at, :] = (
                bell + pre * (jnp.exp(-0.5 * pre * pre) * (1.0 / math.sqrt(2.0 * math.pi)))
            ).astype(LOW)
            output[at, :] += dot(low, down, 1, 1)

        @pl.when(i == steps - 1)
        def _():
            for at in row_tiles(n):
                value, normed, recip = normalize(output[at, :], norms[1:2, :], norms[5:6, :])
                output[at, :] = value
                output_low[at, :] = value.astype(LOW)
                normed_two[at, :] = normed.astype(LOW)
                recip_two[at, :] = recip

    neurons = per * size
    ffn_out = ((2, n, neurons), LOW, (1, n, size), lambda i: (i // per, 0, i % per))
    return call(
        body, steps,
        [
            whole(hidden), whole(hidden_low), whole(layer.norms), per_group(layer.bias_up),
        ] + layer.ffn(layer.up) + layer.ffn(layer.down),
        [
            ffn_out, ffn_out, out_whole((n, depth), F32), out_whole((n, depth), LOW),
            out_whole((n, depth), LOW), out_whole((n, 1), F32),
        ],
        [],
        flops=8 * n * depth * neurons,
        exps=4 * n * neurons,
    )


def add_rows(sums, row, value, at):
    value = jnp.sum(value, axis=0, keepdims=True)
    if at.start == 0:
        sums[row : row + 1, :] = value
    else:
        sums[row : row + 1, :] += value


def ffn_back_call(layer, grad, extra, kept, half):
    n, depth = grad.shape
    steps, _, size = layer.bias_up.shape
    per = steps // 2
    has_extra = extra is not None

    def body(grad, *refs):
        extra = refs[0] if has_extra else None
        (
            normed_one, recip_one, normed_two, recip_two, norms, slope, up_one, up_two, down_one, down_two,
            d_final_low, d_pre, d_mid, d_mid_low, sums, bias_sums, total,
        ) = refs[1:] if has_extra else refs
        i = pl.program_id(0)
        gain = lambda at: norms[at : at + 1, :]

        @pl.when(i == 0)
        def _():
            sums[...] = jnp.zeros_like(sums)
            for at in row_tiles(n):
                value = grad[at, :].astype(F32)
                if has_extra and at.start >= 2 * half:
                    value = value + extra[at.start - 2 * half : at.stop - 2 * half, :].astype(F32)
                normed = normed_two[at, :].astype(F32)
                back = normalize_back(value, normed, recip_two[at, :], gain(1))
                total[at, :] = back
                d_final_low[at, :] = back.astype(LOW)
                add_rows(sums, 1, value * normed, at)
                add_rows(sums, 5, value, at)
                add_rows(sums, 4, back, at)

        bias = None
        up, down = joined((up_one, up_two)), joined((down_one, down_two))
        for at in row_tiles(n):
            d_act = dot(d_final_low[at, :], down, 1, 0)
            low = (d_act * slope[0, at, :].astype(F32)).astype(LOW)
            d_pre[0, at, :] = low
            one = jnp.sum(low.astype(F32), axis=0, keepdims=True)
            bias = one if bias is None else bias + one
            total[at, :] += dot(low, up, 1, 1)
        bias_sums[0] = bias

        @pl.when(i == steps - 1)
        def _():
            for at in row_tiles(n):
                value = total[at, :]
                normed = normed_one[at, :].astype(F32)
                back = normalize_back(value, normed, recip_one[at, :], gain(0))
                d_mid[at, :] = back
                d_mid_low[at, :] = back.astype(LOW)
                add_rows(sums, 0, value * normed, at)
                add_rows(sums, 3, value, at)
                add_rows(sums, 2, back, at)

    neurons = per * size
    blocks = ((1, n, size), lambda i: (i // per, 0, i % per))
    return call(
        body, steps,
        [whole(grad)] + ([whole(extra)] if has_extra else []) + [
            whole(kept["normed_one"]), whole(kept["recip_one"]), whole(kept["normed_two"]),
            whole(kept["recip_two"]), whole(layer.norms), (kept["slope"],) + blocks,
        ] + layer.ffn(layer.up) + layer.ffn(layer.down),
        [
            out_whole((n, depth), LOW), ((2, n, neurons), LOW) + blocks, out_whole((n, depth), F32),
            out_whole((n, depth), LOW), out_whole((8, depth), F32), out_group((steps, 1, size), F32),
        ],
        [pltpu.VMEM((n, depth), F32)],
        flops=8 * n * depth * neurons,
    )


def ffn_back_first_call(layer, grad, extra, kept, half):
    n, depth = grad.shape
    steps, _, size = layer.bias_up.shape
    per = steps // 2

    def body(
        grad, extra, normed_two, recip_two, norms, slope, down_one, down_two,
        d_final, d_final_low, d_pre, sums, bias_sums,
    ):
        i = pl.program_id(0)

        @pl.when(i == 0)
        def _():
            sums[...] = jnp.zeros_like(sums)
            for at in row_tiles(n):
                value = grad[at, :]
                if at.start >= 2 * half:
                    value = value + extra[at.start - 2 * half : at.stop - 2 * half, :].astype(F32)
                normed = normed_two[at, :].astype(F32)
                back = normalize_back(value, normed, recip_two[at, :], norms[1:2, :])
                d_final[at, :] = back
                d_final_low[at, :] = back.astype(LOW)
                add_rows(sums, 1, value * normed, at)
                add_rows(sums, 5, value, at)
                add_rows(sums, 4, back, at)

        bias = None
        down = joined((down_one, down_two))
        for at in row_tiles(n):
            d_act = dot(d_final_low[at, :], down, 1, 0)
            low = (d_act * slope[0, at, :].astype(F32)).astype(LOW)
            d_pre[0, at, :] = low
            one = jnp.sum(low.astype(F32), axis=0, keepdims=True)
            bias = one if bias is None else bias + one
        bias_sums[0] = bias

    neurons = per * size
    blocks = ((1, n, size), lambda i: (i // per, 0, i % per))
    return call(
        body, steps,
        [
            whole(grad), whole(extra), whole(kept["normed_two"]), whole(kept["recip_two"]),
            whole(layer.norms), (kept["slope"],) + blocks,
        ] + layer.ffn(layer.down),
        [
            out_whole((n, depth), F32), out_whole((n, depth), LOW), ((2, n, neurons), LOW) + blocks,
            out_whole((8, depth), F32), out_group((steps, 1, size), F32),
        ],
        [],
        flops=4 * n * depth * neurons,
    )


def ffn_back_second_call(layer, d_final, d_pre, kept):
    n, depth = d_final.shape
    steps, _, size = layer.bias_up.shape
    per = steps // 2

    def body(d_final, d_pre, normed_one, recip_one, norms, up_one, up_two, d_mid, d_mid_low, sums):
        i = pl.program_id(0)

        @pl.when(i == 0)
        def _():
            d_mid[...] = d_final[...]

        up = joined((up_one, up_two))
        for at in row_tiles(n):
            d_mid[at, :] += dot(d_pre[0, at, :], up, 1, 1)

        @pl.when(i == steps - 1)
        def _():
            sums[...] = jnp.zeros_like(sums)
            for at in row_tiles(n):
                value = d_mid[at, :]
                normed = normed_one[at, :].astype(F32)
                back = normalize_back(value, normed, recip_one[at, :], norms[0:1, :])
                d_mid[at, :] = back
                d_mid_low[at, :] = back.astype(LOW)
                add_rows(sums, 0, value * normed, at)
                add_rows(sums, 3, value, at)
                add_rows(sums, 2, back, at)

    blocks = ((1, n, size), lambda i: (i // per, 0, i % per))
    return call(
        body, steps,
        [
            whole(d_final), (d_pre,) + blocks, whole(kept["normed_one"]), whole(kept["recip_one"]),
            whole(layer.norms),
        ] + layer.ffn(layer.up),
        [out_whole((n, depth), F32), out_whole((n, depth), LOW), out_whole((8, depth), F32)],
        [],
        flops=4 * n * depth * per * size,
    )


def shared_back_call(layer, d_mid_low, kept, segs, half):
    n, depth = d_mid_low.shape
    width, wide, own = layer.width, 3 * layer.width, 2 * half
    count = 2 * len(layer.qkv_blocks)

    def body(d_mid, proj, away, logsum, *refs):
        weights = pairs_of(refs[:count])
        out_one, out_two, segs_q, segs_k, d_proj, d_away, sums, back, mask, total = refs[count:]
        i = pl.program_id(0)
        make_mask(segs_q, segs_k, mask)
        out_cols = joined((out_one, out_two), slice(layer.out_from, layer.out_from + width))
        d_context = dot(d_mid[...], out_cols, 1, 0).astype(LOW)
        attend_back(
            width, [proj.at[0], away.at[0]], mask, logsum.at[0], d_context,
            [d_proj.at[0], d_away.at[0]], sums.at[0],
        )
        part = through_projection(d_away[0], weights, layer.used)

        @pl.when(i == 0)
        def _():
            total[...] = part

        @pl.when(i == 1)
        def _():
            back[...] = (total[...] + part).astype(LOW)

    return call(
        body, 2,
        [
            (d_mid_low, (half, depth), lambda i: (2, 0)), (kept["proj"], (1, half, wide), lambda i: (i, 2, 0)),
            per_group(kept["proj_away"]), per_group(kept["logsum_shared"]),
        ] + layer.qkv() + layer.out() + [whole(segs[None, :half]), whole(segs[:, None])],
        [
            out_group((2, half, wide), LOW), out_group((2, half, wide), LOW), out_group((2, 8, wide), F32),
            out_whole((half, depth), LOW),
        ],
        [pltpu.VMEM((own, half), F32), pltpu.VMEM((half, depth), F32)],
        flops=4 * half * depth * (wide + width) + 20 * own * half * width,
        exps=2 * own * half * width // HEAD_DIM,
    )


def own_back_call(layer, d_mid, d_mid_low, d_shared, kept, segs, half, with_rows):
    n, depth = d_mid_low.shape
    width, wide, own = layer.width, 3 * layer.width, 2 * half
    count = 2 * len(layer.qkv_blocks) if with_rows else 0

    def body(d_mid_low, d_shared, proj, logsum, out_one, out_two, segs_q, segs_k, *refs):
        i = pl.program_id(0)
        if with_rows:
            d_mid, weights = refs[0], pairs_of(refs[1 : count + 1])
            d_proj, sums, d_rows, mask = refs[count + 1 :]
        else:
            d_proj, sums, mask = refs
        make_mask(segs_q, segs_k, mask)
        out_cols = joined((out_one, out_two), slice(layer.out_from, layer.out_from + width))
        d_context = dot(d_mid_low[...], out_cols, 1, 0).astype(LOW)
        attend_back(
            width, [proj.at[0]], mask, logsum.at[0], d_context, [d_proj.at[0, :own]], sums.at[0]
        )
        d_proj[0, own:] = d_shared[0]
        if with_rows:
            part = through_projection(d_proj[0], weights, layer.used)

            @pl.when(i == 0)
            def _():
                d_rows[...] = d_mid[...] + part

            @pl.when(i == 1)
            def _():
                d_rows[...] += part

    return call(
        body, 2,
        [
            (d_mid_low, (own, depth), lambda i: (0, 0)), per_group(d_shared),
            (kept["proj"], (1, own, wide), lambda i: (i, 0, 0)), per_group(kept["logsum_own"]),
        ] + layer.out() + [whole(segs[None, :]), whole(segs[:, None])]
        + ([whole(d_mid)] + layer.qkv() if with_rows else []),
        [out_group((2, n, wide), LOW), out_group((2, 8, wide), F32)]
        + ([out_whole((n, depth), F32)] if with_rows else []),
        [pltpu.VMEM((own, own), F32)],
        flops=4 * depth * (n * wide * with_rows + own * width) + 20 * own * own * width,
        exps=2 * own * own * width // HEAD_DIM,
    )


def rows_back_call(layer, d_mid, d_proj):
    n, depth = d_mid.shape
    wide = 3 * layer.width

    def body(d_mid, d_proj, *refs):
        weights, d_rows = pairs_of(refs[:-1]), refs[-1]

        @pl.when(pl.program_id(0) == 0)
        def _():
            d_rows[...] = d_mid[...]

        d_rows[...] += through_projection(d_proj[0], weights, layer.used)

    return call(
        body, 2, [whole(d_mid), per_group(d_proj)] + layer.qkv(), [out_whole((n, depth), F32)], [],
        flops=4 * depth * n * wide,
    )[0]


class Grads:
    def __init__(self, entries, columns, cut):
        self.entries, self.columns, self.cut = entries, columns, cut
        sizes = [end - start for _, start, end in columns]
        self.size_a, self.size_b = sum(sizes[:cut]), sum(sizes[cut:])

    def inputs(self, at, side):
        out = []
        for pairs in self.entries:
            for left, right in pairs:
                half = (left.shape[0], left.shape[1] // 2)
                out += [(left, half, lambda i: (0, side)), per_group(right, at)]
        return out

    def flops(self, rows):
        return sum(
            4 * rows * left.shape[0] * right.shape[2] for pairs in self.entries for left, right in pairs
        )

    def product(self, refs, entry, start, end):
        first = sum(len(pairs) for pairs in self.entries[:entry])
        total = None
        for at in range(first, first + len(self.entries[entry])):
            one = dot(refs[2 * at][...], refs[2 * at + 1][0, :, start:end], 0, 0)
            total = one if total is None else total + one
        return total

    def send(self):
        rows = self.entries[0][0][0].shape[1] // 2
        size = self.size_a + self.size_b

        def body(*refs):
            col = 0
            for entry, start, end in self.columns:
                part = self.product(refs, entry, start, end)
                refs[-1][0, :, col : col + end - start] = part.astype(LOW)
                col += end - start

        return call(
            body, 2, self.inputs(lambda i: i, 1), [out_group((2, rows, size), LOW)], [], self.flops(rows)
        )[0]

    def keep(self, got):
        rows = self.entries[0][0][0].shape[1] // 2
        half = rows // 2

        def body(got, *refs):
            send_a, keep_a, send_b, keep_b = refs[-4:]
            i = pl.program_id(0)
            col = 0
            for at, (entry, start, end) in enumerate(self.columns):
                part = self.product(refs, entry, start, end)
                part = part + got[0, :, col : col + end - start].astype(F32)
                if at < self.cut:
                    place = slice(col, col + end - start)

                    @pl.when(i == 0)
                    def _():
                        send_a[:, place] = part.astype(LOW)

                    @pl.when(i == 1)
                    def _():
                        keep_a[:, place] = part
                else:
                    place = slice(col - self.size_a, col - self.size_a + end - start)
                    keep_b[0, :, place] = part[:half]
                    send_b[0, :, place] = part[half:].astype(LOW)
                col += end - start

        return call(
            body, 2,
            [per_group(got, lambda i: 1 - i)] + self.inputs(lambda i: 1 - i, 0),
            [
                out_whole((rows, self.size_a), LOW), out_whole((rows, self.size_a), F32),
                out_group((2, half, self.size_b), LOW), out_group((2, half, self.size_b), F32),
            ],
            [], self.flops(rows),
        )


class Reduce:
    def __init__(self, grads):
        self.grads = grads
        self.sends = (grads.send(),)
        self.got = (swap_core(self.sends[0]),)
        self.work = self._run()

    def _run(self):
        count = lax.axis_size("dp") // 4
        send_a, keep_a, send_b, keep_b = self.grads.keep(self.got[0])
        fourth = keep_a.shape[0] // 2
        self.sends = (send_a, send_b)
        self.got = (swap_y(send_a), swap_x(send_b))
        yield
        a = keep_a + self.got[0].astype(F32)
        b = keep_b + self.got[1].astype(F32)
        self.sends = (a[fourth:].astype(LOW), b[0].astype(LOW))
        self.got = (swap_x(self.sends[0]), swap_y(self.sends[1]))
        a, b = a[:fourth], b[1]
        yield
        both = jnp.concatenate([a + self.got[0].astype(F32), b + self.got[1].astype(F32)], axis=1)
        both = both.reshape((count, -1) + both.shape[1:])
        self.sends = tuple(both[back].astype(LOW) for back in range(1, count))
        self.got = tuple(ring_shift(send, -back) for back, send in enumerate(self.sends, 1))
        yield
        total = both[0] + sum(got.astype(F32) for got in self.got)
        self.total = total
        self.got = self.sends = ()

    def step(self):
        next(self.work, None)


class Total:
    def __init__(self, value):
        self.total = value
        self.work = self._run()
        self.step()

    def _run(self):
        n = lax.axis_size("dp")
        self.sends = (self.total,)
        self.got = (swap_y(self.total),)
        yield
        self.total = self.total + self.got[0]
        step = 1
        while step < n:
            self.sends = (self.total,)
            self.got = (lax.ppermute(self.total, "dp", [(i, i ^ step) for i in range(n)]),)
            yield
            self.total = self.total + self.got[0]
            step *= 2
        self.got = self.sends = ()

    def step(self):
        next(self.work, None)


def round_of(*works):
    ended = lax.optimization_barrier(tuple(work.got for work in works))
    for work, got in zip(works, ended):
        work.got = got
    for work in works:
        work.step()


def before(value, *works):
    value, ended = lax.optimization_barrier((value, tuple(work.got for work in works)))
    for work, got in zip(works, ended):
        work.got = got
    return value


def forward_attn(layer, rows, proj, context_own, logsum_own, rows_low, away_low, segs, half):
    proj_away, context, logsum_shared, hidden, hidden_low, normed_one, recip_one = shared_call(
        layer, rows, proj, away_low, context_own, segs[1], half
    )
    kept = dict(
        rows_low=rows_low, away_low=away_low, proj=proj, proj_away=proj_away, context=context,
        logsum_own=logsum_own, logsum_shared=logsum_shared, hidden_low=hidden_low,
        normed_one=normed_one, recip_one=recip_one,
    )
    return hidden, kept


def forward_ffn(layer, hidden, kept):
    act, slope, output, output_low, normed_two, recip_two = ffn_call(layer, hidden, kept["hidden_low"])
    kept.update(act=act, slope=slope, normed_two=normed_two, recip_two=recip_two)
    return output, output_low


def backward_ffn(layer, grad, extra, kept, half):
    d_final_low, d_pre, d_mid, d_mid_low, sums, bias_sums = ffn_back_call(layer, grad, extra, kept, half)
    entries = [[(kept["hidden_low"], d_pre)], [(d_final_low, kept["act"])]]
    return d_mid, d_mid_low, sums[:6], bias_sums, entries


def attn_entries(kept, d_proj, d_away, d_mid_low):
    return [[(kept["rows_low"], d_proj), (kept["away_low"], d_away)], [(d_mid_low, kept["context"])]]


def on_device(
    tokens, segment_ids, out_grad,
    t_qkv, t_qv_bias, t_out, t_up, t_up_bias, t_down, t_gains, t_shifts,
    s_qkv, s_qv_bias, s_out, s_up, s_up_bias, s_down, s_gains, s_shifts,
):
    rows, half, width = tokens.shape
    first = lax.axis_index("mp") == 0
    own_row = lambda value: jnp.where(first, value[0], value[2])
    far_row = lambda value: jnp.where(first, value[2], value[0])

    norm_rows = jnp.concatenate([t_gains, t_shifts, s_gains, s_shifts], axis=0)
    norm_rows = jnp.pad(norm_rows, ((0, 128 - norm_rows.shape[0]), (0, 0)))
    t_width, s_width = t_qkv.shape[2], s_qkv.shape[2]
    size = s_up.shape[1]
    per = t_up.shape[1] // size
    count, block = lax.axis_size("dp") // 4, t_up.shape[0]
    together = lambda *values: lax.optimization_barrier(values)
    every = slice(None)

    def columns(start, width):
        return slice(start, start + width)

    t_cut, t_all = 2 * t_width, 4 * t_width + 128
    f_cut = per * size
    s_cut = size + 2 * s_width
    packed_t, packed_f, student_a, student_b = pack(
        [t_qkv, t_up, s_up, s_qkv], [t_out, norm_rows, t_down, s_out, s_down],
        [(block, t_all), (block, 2 * f_cut), (block, s_cut), (block, s_cut)],
        [(0, (i,), 0, (every, columns(i * t_width, t_width))) for i in range(3)]
        + [
            (4, (), 0, (every, columns(3 * t_width, t_width))), (5, (), 0, (every, columns(4 * t_width, 128))),
            (1, (every,), 1, (every, columns(0, f_cut))), (6, (), 1, (every, columns(f_cut, f_cut))),
            (2, (every,), 2, (every, columns(0, size))), (3, (0,), 2, (every, columns(size, s_width))),
            (7, (), 2, (every, columns(size + s_width, s_width))), (8, (), 3, (every, columns(0, size))),
            (3, (1,), 3, (every, columns(size, s_width))), (3, (2,), 3, (every, columns(size + s_width, s_width))),
        ],
    )

    def along_z(value):
        return [value] + [ring_shift(value, at) for at in range(1, count)]

    def of_line(pieces, cut):
        rest = pieces[0].shape[1] - cut
        return moves(
            pieces, [(count, block, cut), (count, block, rest)],
            [(i, (every, columns(start, wide)), at, (i,)) for i in range(count)
             for at, (start, wide) in enumerate(((0, cut), (cut, rest)))],
        )

    def first_plane(a, got_a, b, got_b):
        return moves(
            [a, got_a, b, got_b], [(2,) + a.shape, (2,) + b.shape],
            [(0, (every,), 0, (0,)), (1, (every,), 0, (1,)), (2, (every,), 1, (0,)), (3, (every,), 1, (1,))],
        )

    def both_planes(a, got_a, b, got_b, order):
        copies, col = [], 0
        for of_b, start, wide in order:
            taken, place = (every, every, every, columns(start, wide)), (every, every, columns(col, wide))
            if of_b:
                copies += [(2, taken, 0, (every, 0) + place), (3, taken, 0, (every, 1) + place)]
            else:
                copies += [(0, taken, 0, (0, every) + place), (1, taken, 0, (1, every) + place)]
            col += wide
        out = moves([a, got_a, b, got_b], [(2, 2, count, block, col)], copies)[0]
        return out.reshape(2, width // 2, col)

    def with_core(own):
        return own, swap_core(own)

    bias_parts = [t_qv_bias[0], t_qv_bias[1], t_up_bias, s_qv_bias[0], s_qv_bias[1], s_up_bias]
    to_own = feature_order(width)
    into = (lax.iota(jnp.int32, width)[:, None] == to_own[None, :]).astype(LOW)
    def reorder(value):
        return jnp.dot(value, into, preferred_element_type=F32).astype(LOW)


    spin = lambda segs: jnp.where(first, segs, jnp.roll(segs, half))
    segs = (spin(own_row(segment_ids)), spin(segment_ids[1]))

    line_t, got_own = along_z(packed_t), swap_y(far_row(tokens))
    *line_t, got_own, into, segs, packed_f, student_a, student_b = together(
        *line_t, got_own, into, segs, packed_f, student_a, student_b
    )
    attn_a, attn_b = of_line(line_t, t_cut)
    got_a, got_b = swap_x(attn_a), swap_y(attn_b)
    line_f = along_z(packed_f)
    student_x, student_y = swap_x(student_a), swap_y(student_b)
    got_a, got_b, student_x, student_y, line_f[1] = together(got_a, got_b, student_x, student_y, line_f[1])
    inputs = reorder(jnp.concatenate([own_row(tokens), got_own, tokens[1]], axis=0))
    attn_a, attn_b = first_plane(attn_a, got_a, attn_b, got_b)
    got_a, got_b = swap_y(attn_a), swap_x(attn_b)
    line_s = along_z(moves(
        [student_a, student_x, student_b, student_y], [(2, block, 2 * s_cut)],
        [(i, (every,), 0, (i % 2, every, columns(i // 2 * s_cut, s_cut))) for i in range(4)],
    )[0])
    got_a, got_b, inputs, *line_f[2:] = together(got_a, got_b, inputs, *line_f[2:])
    attn = both_planes(
        attn_a, got_a, attn_b, got_b, [(False, 0, t_cut), (True, 0, t_all - t_cut)]
    )
    attn = with_core(attn)
    ffn_a, ffn_b = of_line(list(after(line_f, attn[0])), f_cut)
    got_a, got_b = swap_x(ffn_a), swap_y(ffn_b)
    bias_own = jnp.concatenate(bias_parts)
    bias_far = swap_y(bias_own)
    attn, got_a, got_b, bias_far = together(attn, got_a, got_b, bias_far)
    ffn_a, ffn_b = first_plane(ffn_a, got_a, ffn_b, got_b)
    got_a, got_b = swap_y(ffn_a), swap_x(ffn_b)
    got_shared = swap_y(tokens[1])
    norms = jnp.concatenate([half[0, :, -128:-116] for half in attn], axis=0).T.astype(F32)
    norms_of = lambda at: jnp.pad(norms[at : at + 6], ((0, 2), (0, 0)))
    bias_all = jnp.stack([bias_own, bias_far]).astype(F32)
    cuts = [0]
    for part in bias_parts:
        cuts.append(cuts[-1] + part.shape[0])
    pick = [bias_all[:, cuts[i] : cuts[i + 1]] for i in range(6)]
    bias_qkv = lambda q, v: jnp.concatenate([q, jnp.zeros_like(q), v], axis=1)[:, None, :]
    teacher = Layer(
        t_width, None, None, [(attn, t_width, i, t_width) for i in range(3)], (attn, t_width, 3, t_width), 0,
        norms_of(0), bias_qkv(pick[0], pick[1]), pick[2].reshape(2 * per, 1, size),
    )

    grad_in = jnp.concatenate([own_row(out_grad), swap_y(far_row(out_grad)), out_grad[1]], axis=0)

    inputs, ffn_a, ffn_b = together(inputs, ffn_a, ffn_b)
    proj, context_own, logsum_own = project_call(teacher, inputs, segs[0], half)
    proj, got_shared, *line_s[1:-1] = together(proj, got_shared, *line_s[1:-1])
    away_low = reorder(got_shared)
    hidden, t_kept = forward_attn(
        teacher, inputs, proj, context_own, logsum_own, inputs, away_low, segs, half
    )
    hidden, got_a, got_b, line_s[-1] = together(hidden, got_a, got_b, line_s[-1])
    ffn = both_planes(ffn_a, got_a, ffn_b, got_b, [(False, 0, f_cut), (True, 0, f_cut)])
    ffn = with_core(ffn)
    student_a, student_b = moves(
        line_s, [(2, count, block, s_cut)] * 2,
        [(i, (every, every, columns(at * s_cut, s_cut)), at, (every, i)) for i in range(count) for at in range(2)],
    )
    got_a, got_b = swap_y(student_a), swap_x(student_b)
    hidden, ffn = together(hidden, ffn)
    teacher.up, teacher.down = (ffn, 0), (ffn, per)
    middle, middle_low = forward_ffn(teacher, hidden, t_kept)
    away_low = swap_y(middle_low[2 * half :])
    middle_low, got_a, got_b, grad_in = together(middle_low, got_a, got_b, grad_in)
    grad_in = reorder(grad_in)
    student_w = with_core(both_planes(
        student_a, got_a, student_b, got_b,
        [(False, 0, size), (True, 0, size), (False, size, 2 * s_width), (True, size, 2 * s_width)],
    ))
    narrow = 2 * s_width
    place = 2 * size // narrow
    student = Layer(
        s_width, (student_w, 0), (student_w, 1),
        [(student_w, narrow, place, s_width), (student_w, narrow, place + 1, narrow)],
        (student_w, narrow, place, s_width), s_width, norms_of(6), bias_qkv(pick[3], pick[4]),
        pick[5].reshape(2, 1, size),
    )
    proj, context_own, logsum_own = project_call(student, middle_low, segs[0], half)
    proj, away_low = together(proj, away_low)
    hidden, s_kept = forward_attn(
        student, middle, proj, context_own, logsum_own, middle_low, away_low, segs, half
    )
    last, _ = forward_ffn(student, hidden, s_kept)

    def far_half(value):
        return swap_y(value[half : 2 * half].astype(LOW))

    def to_rows(value, far):
        near = jnp.concatenate([value[:half], value[2 * half :]], axis=0)
        high = near.astype(LOW)
        low = (near - high.astype(F32)).astype(LOW)
        back = lambda part: jnp.einsum("nr,dr->nd", part, into, preferred_element_type=F32)
        near, far = back(high) + back(low), back(far)
        return jnp.stack([jnp.where(first, near[:half], far), near[half:], jnp.where(first, far, near[:half])])

    far_last = far_half(last)

    d_mid, d_mid_low, s_norm_grads, s_up_grad, s_entries = backward_ffn(student, grad_in, None, s_kept, half)
    d_shared, d_away, s_sums_b, back = shared_back_call(student, d_mid_low, s_kept, segs[1], half)
    extra = swap_y(back)
    d_shared, far_last = together(d_shared, far_last)
    d_proj, s_sums_a, d_rows = own_back_call(
        student, d_mid, d_mid_low, d_shared, s_kept, segs[0], half, True
    )
    d_proj, extra = lax.optimization_barrier((d_proj, extra))
    s_entries += attn_entries(s_kept, d_proj, d_away, d_mid_low)
    s_columns = [(0, 0, size), (2, 0, s_width), (3, 0, s_width), (1, 0, size), (2, s_width, 3 * s_width)]
    reduce_s = Reduce(Grads(s_entries, s_columns, 3))

    d_rows = after(d_rows, reduce_s.sends)
    d_final, d_final_low, d_pre, t_sums_two, t_up_grad = ffn_back_first_call(
        teacher, d_rows, extra, t_kept, half
    )
    d_pre = before(d_pre, reduce_s)
    reduce_s.step()
    d_pre = after(d_pre, reduce_s.sends)
    f_entries = [[(t_kept["hidden_low"], d_pre)], [(d_final_low, t_kept["act"])]]
    reduce_f = Reduce(Grads(f_entries, [(0, 0, per * size), (1, 0, per * size)], 1))
    d_pre = after(d_pre, reduce_f.sends)
    d_mid, d_mid_low, t_sums_one = ffn_back_second_call(teacher, d_final, d_pre, t_kept)
    t_norm_grads = (t_sums_one + t_sums_two)[:6]
    d_mid_low = before(d_mid_low, reduce_f)
    reduce_f.step()
    reduce_s.got = after(reduce_s.got, reduce_f.sends)
    d_mid_low = before(d_mid_low, reduce_s)
    reduce_s.step()
    d_mid_low = after(d_mid_low, reduce_s.sends)
    d_shared, d_away, t_sums_b, back = shared_back_call(teacher, d_mid_low, t_kept, segs[1], half)
    extra = swap_y(back)
    d_shared = before(d_shared, reduce_s)
    reduce_s.step()
    d_shared = after(d_shared, reduce_s.sends)
    d_proj, t_sums_a = own_back_call(teacher, None, d_mid_low, d_shared, t_kept, segs[0], half, False)
    t_entries = attn_entries(t_kept, d_proj, d_away, d_mid_low)
    reduce_t = Reduce(
        Grads(t_entries, [(0, 0, 2 * t_width), (0, 2 * t_width, 3 * t_width), (1, 0, t_width)], 1)
    )

    def qv_grad(one, two, wide):
        sums = one[:, 0] + two[:, 0]
        sums = jnp.concatenate([sums[:, :wide], sums[:, 2 * wide :]], axis=1)
        return jnp.pad(sums, ((0, 0), (0, width - 2 * wide)))

    norm_grads = jnp.concatenate([t_norm_grads, s_norm_grads], axis=0)
    norm_grads = jnp.einsum("nr,dr->nd", norm_grads, into.astype(F32), precision=lax.Precision.HIGHEST)
    qv_t, qv_s = qv_grad(t_sums_a, t_sums_b, t_width), qv_grad(s_sums_a, s_sums_b, s_width)
    mine = jnp.concatenate([t_up_grad[:per, 0], s_up_grad[:1, 0], qv_t[:1], qv_s[:1]], axis=0)
    other = jnp.concatenate([t_up_grad[per:, 0], s_up_grad[1:, 0], qv_t[1:], qv_s[1:]], axis=0)
    small = Total(jnp.concatenate(
        [norm_grads, jnp.where(first, mine, other), jnp.where(first, other, mine)], axis=0
    ))
    reduce_f.got = after(reduce_f.got, reduce_t.sends)
    round_of(reduce_f, small)
    reduce_t.got = after(reduce_t.got, reduce_f.sends)
    reduce_t.step()
    reduce_f.got = after(reduce_f.got, reduce_t.sends)
    round_of(reduce_f, reduce_s)
    d_rows = rows_back_call(teacher, *after((d_mid, d_proj), reduce_t.sends))
    reduce_t.got = after(reduce_t.got, d_rows)
    far_rows = far_half(d_rows)
    round_of(reduce_t, small)
    d_rows, last = after((d_rows, last), reduce_t.sends)
    d_rows = jnp.concatenate([d_rows[: 2 * half], d_rows[2 * half :] + extra.astype(F32)], axis=0)
    input_grad, output = to_rows(d_rows, far_rows), to_rows(last, far_last)
    round_of(reduce_t, reduce_f, small)
    round_of(reduce_t, small)
    for work in (reduce_t, reduce_f, reduce_s, small):
        while work.got:
            work.step()
    s_sum, f_sum, t_sum, small = reduce_s.total, reduce_f.total, reduce_t.total, small.total

    piece = width // lax.axis_size("dp")
    norm_sum = lax.dynamic_slice_in_dim(small[:12], lax.axis_index("dp") * piece, piece, 1)
    bias_sum = small[12:].reshape(2, -1, width)
    bias_sum = jnp.where(first, bias_sum[0], bias_sum[1])
    t_qv_sum, s_qv_sum = bias_sum[per + 1], bias_sum[per + 2, : 2 * s_width]

    def cut(value, *sizes):
        out = []
        for one in sizes:
            out.append(value[:, :one])
            value = value[:, one:]
        return out

    tq, tk, tv, to = cut(t_sum, t_width, t_width, t_width, t_width)
    t_up_sum, t_down_sum = cut(f_sum, per * size, per * size)
    s_up_sum, sq, so, s_down_sum, sk, sv = cut(s_sum, size, s_width, s_width, size, s_width, s_width)
    return (
        output, input_grad,
        jnp.stack([tq, tk, tv]), t_qv_sum.reshape(2, -1), to.T, t_up_sum, bias_sum[:per].reshape(-1),
        t_down_sum.T,
        norm_sum[0:2], norm_sum[2:6],
        jnp.stack([sq, sk, sv]), s_qv_sum.reshape(2, -1), so.T, s_up_sum, bias_sum[per], s_down_sum.T,
        norm_sum[6:8], norm_sum[8:12],
    )


def solution(mesh):
    layer = (
        P(None, "dp", "mp"), P(None, "mp"), P("mp", "dp"), P("dp", "mp"), P("mp"), P("mp", "dp"),
        P(None, "dp"), P(None, "dp"),
    )
    rows = P("dp", "mp", None)
    return jax.shard_map(
        on_device,
        mesh=mesh,
        in_specs=(rows, P("dp", None), rows) + layer + layer,
        out_specs=(rows, rows) + layer + layer,
        check_vma=False,
    )
```

```python
import functools
import math

import jax
import jax.numpy as jnp
from jax import lax
from jax.experimental import pallas as pl
from jax.experimental.pallas import tpu as pltpu
from jax.sharding import PartitionSpec as P

HEAD_DIM = 64
LOW = jnp.bfloat16
F32 = jnp.float32


def ring_of(count):
    return list(range(0, count, 2)) + list(range(1, count, 2))[::-1]


def swap_y(value):
    return lax.ppermute(value, "mp", [(0, 1), (1, 0)])


def swap_x(value):
    n = lax.axis_size("dp")
    return lax.ppermute(value, "dp", [(i, i ^ 2) for i in range(n)])


def swap_core(value):
    n = lax.axis_size("dp")
    return lax.ppermute(value, "dp", [(i, i ^ 1) for i in range(n)])


def ring_shift(value, step):
    count = lax.axis_size("dp") // 4
    ring = ring_of(count)
    pairs = []
    for place in range(count):
        for low in range(4):
            pairs.append((ring[place] * 4 + low, ring[(place + step) % count] * 4 + low))
    return lax.ppermute(value, "dp", pairs)


def feature_order(width):
    n = lax.axis_size("dp")
    count, rows = n // 4, width // n
    me = lax.axis_index("dp")
    z, x, core = me // 4, (me // 2) % 2, me % 2
    place = jnp.where(z % 2 == 0, z // 2, count - 1 - z // 2)
    at = lax.iota(jnp.int32, width)
    row = at % rows
    back = (at // rows) % count
    x_rel = (at // (rows * count)) % 2
    core_rel = at // (rows * count * 2)
    from_place = (place - back + count) % count
    half = (count + 1) // 2
    z_abs = jnp.where(from_place < half, 2 * from_place, 2 * (count - 1 - from_place) + 1)
    block = z_abs * 4 + (x ^ x_rel) * 2 + (core ^ core_rel)
    return block * rows + row


def after(value, *others):
    return lax.optimization_barrier((value, others))[0]


VMEM_BYTES = 48 << 20
TILE = 256


def dot(left, right, left_at, right_at):
    return lax.dot_general(
        left, right, (((left_at,), (right_at,)), ((), ())), preferred_element_type=F32
    )


def call(body, steps, inputs, outputs, scratch, flops, exps=0):
    size = lambda shape, dtype: math.prod(shape) * jnp.dtype(dtype).itemsize
    moved = sum(size(array.shape, array.dtype) for array, _, _ in inputs)
    moved += sum(size(shape, dtype) for shape, dtype, _, _ in outputs)
    return pl.pallas_call(
        body,
        grid=(steps,),
        in_specs=[pl.BlockSpec(block, index) for _, block, index in inputs],
        out_specs=[pl.BlockSpec(block, index) for _, _, block, index in outputs],
        out_shape=[jax.ShapeDtypeStruct(shape, dtype) for shape, dtype, _, _ in outputs],
        scratch_shapes=scratch,
        compiler_params=pltpu.CompilerParams(
            dimension_semantics=("arbitrary",), vmem_limit_bytes=VMEM_BYTES
        ),
        cost_estimate=pl.CostEstimate(
            flops=flops // 2, bytes_accessed=moved // 2, transcendentals=exps // 2
        ),
    )(*[array for array, _, _ in inputs])


def moves(arrays, shapes, copies):
    def body(*refs):
        for source, taken, target, place in copies:
            refs[len(arrays) + target][place] = refs[source][taken]

    moved = 2 * sum(math.prod(shape) for shape in shapes)
    return pl.pallas_call(
        body,
        out_shape=[jax.ShapeDtypeStruct(shape, LOW) for shape in shapes],
        compiler_params=pltpu.CompilerParams(vmem_limit_bytes=VMEM_BYTES),
        cost_estimate=pl.CostEstimate(flops=0, bytes_accessed=moved, transcendentals=0),
    )(*arrays)


def whole(array):
    rank = array.ndim
    return (array, array.shape, lambda i: (0,) * rank)


def per_group(array, at=lambda i: i):
    return (array, (1,) + array.shape[1:], lambda i: (at(i),) + (0,) * (array.ndim - 1))


def out_whole(shape, dtype):
    return (shape, dtype, shape, lambda i: (0,) * len(shape))


def out_group(shape, dtype, at=lambda i: i):
    return (shape, dtype, (1,) + shape[1:], lambda i: (at(i),) + (0,) * (len(shape) - 1))


class Layer:
    def __init__(self, width, up, down, qkv, out, out_from, norms, bias_qkv, bias_up):
        self.width, self.up, self.down = width, up, down
        self.qkv_blocks, self.out_block, self.out_from = qkv, out, out_from
        self.norms, self.bias_qkv, self.bias_up = norms, bias_qkv, bias_up
        self.used = [block[3] for block in qkv]

    def columns(self, block, at):
        pair, size, place, _ = block
        return [(half, (1, half.shape[1], size), lambda i: (at(i), 0, place)) for half in pair]

    def qkv(self, at=lambda i: i):
        return [one for block in self.qkv_blocks for one in self.columns(block, at)]

    def out(self, at=lambda i: i):
        return self.columns(self.out_block, at)

    def ffn(self, where):
        pair, base = where
        size, per = self.bias_up.shape[2], self.bias_up.shape[0] // 2
        return [(half, (1, half.shape[1], size), lambda i: (i // per, 0, base + i % per)) for half in pair]


def joined(pair, cols=slice(None)):
    return jnp.concatenate([half[0, :, cols] for half in pair], axis=0)


def pairs_of(refs):
    return [refs[at : at + 2] for at in range(0, len(refs), 2)]


def put_projection(rows, weights, used, bias, target):
    start = 0
    for weight, cols in zip(weights, used):
        part = dot(rows, joined(weight, slice(0, cols)), 1, 0) + bias[0, :, start : start + cols]
        target[:, start : start + cols] = part.astype(LOW)
        start += cols


def through_projection(grads, weights, used):
    start = 0
    total = None
    for weight, cols in zip(weights, used):
        part = dot(grads[:, start : start + cols], joined(weight, slice(0, cols)), 1, 1)
        total = part if total is None else total + part
        start += cols
    return total


def head_at(width, part, head):
    return slice(part * width + head * HEAD_DIM, part * width + (head + 1) * HEAD_DIM)


def join(parts, cols):
    picked = [part[:, cols] for part in parts]
    return picked[0] if len(picked) == 1 else jnp.concatenate(picked, axis=0)


def attend(width, kept, mask, logsum):
    scale = jnp.asarray(HEAD_DIM**-0.5, LOW)
    out = []
    for head in range(width // HEAD_DIM):
        query = kept[0][:, head_at(width, 0, head)] * scale
        scores = dot(join(kept, head_at(width, 1, head)), query, 1, 1) + mask[...]
        top = jnp.max(scores, axis=0, keepdims=True)
        expo = jnp.exp(scores - top)
        total = jnp.sum(expo, axis=0, keepdims=True)
        out.append(dot(join(kept, head_at(width, 2, head)), expo.astype(LOW), 0, 0) * (1.0 / total))
        logsum[head : head + 1, :] = top + jnp.log(total)
    return jnp.concatenate(out, axis=0).T.astype(LOW)


def attend_back(width, kept, mask, logsum, d_context, grads, sums):
    scale = jnp.asarray(HEAD_DIM**-0.5, LOW)
    for head in range(width // HEAD_DIM):
        at_q, at_k, at_v = (head_at(width, part, head) for part in range(3))
        query = kept[0][:, at_q] * scale
        keys = join(kept, at_k)
        d_ctx = d_context[:, head * HEAD_DIM : (head + 1) * HEAD_DIM]
        probs = jnp.exp(dot(keys, query, 1, 1) + mask[...] - logsum[head : head + 1, :])
        d_probs = dot(join(kept, at_v), d_ctx, 1, 1)
        both = probs * d_probs
        inner = jnp.sum(both, axis=0, keepdims=True)
        d_scores = (both - probs * inner).astype(LOW)
        d_values = dot(probs.astype(LOW), d_ctx, 1, 0).astype(LOW)
        d_keys = dot(d_scores, query, 1, 0).astype(LOW)
        d_query = dot(keys * scale, d_scores, 0, 0).T.astype(LOW)
        grads[0][:, at_q] = d_query
        start = 0
        for grad in grads:
            rows = grad.shape[0]
            grad[:, at_k] = d_keys[start : start + rows]
            grad[:, at_v] = d_values[start : start + rows]
            start += rows
        for grad in grads[1:]:
            grad[:, at_q] = jnp.zeros((grad.shape[0], HEAD_DIM), LOW)
        sums[0:1, at_q] = jnp.sum(d_query.astype(F32), axis=0, keepdims=True)
        sums[0:1, at_k] = jnp.zeros((1, HEAD_DIM), F32)
        sums[0:1, at_v] = jnp.sum(d_values.astype(F32), axis=0, keepdims=True)


def make_mask(segs_q, segs_k, mask):
    @pl.when(pl.program_id(0) == 0)
    def _():
        mask[...] = jnp.where(segs_k[...] == segs_q[...], 0.0, -1e9)


def normalize(value, gain, shift):
    center = value - jnp.mean(value, axis=-1, keepdims=True)
    recip = lax.rsqrt(jnp.mean(center * center, axis=-1, keepdims=True) + 1e-06)
    normed = center * recip
    return normed * gain + shift, normed, recip


def normalize_back(grad, normed, recip, gain):
    scaled = grad * gain
    mean_one = jnp.mean(scaled, axis=-1, keepdims=True)
    mean_two = jnp.mean(scaled * normed, axis=-1, keepdims=True)
    return recip * (scaled - mean_one - normed * mean_two)


def row_tiles(rows):
    return [slice(start, start + TILE) for start in range(0, rows, TILE)]


def project_call(layer, rows_low, segs, half):
    n, depth = rows_low.shape
    width, wide, own = layer.width, 3 * layer.width, 2 * half
    count = 2 * len(layer.qkv_blocks)

    def body(rows, *refs):
        weights = pairs_of(refs[:count])
        bias, segs_q, segs_k, proj, context, logsum, mask = refs[count:]
        make_mask(segs_q, segs_k, mask)
        put_projection(rows[...], weights, layer.used, bias, proj.at[0])
        context[0] = attend(width, [proj.at[0, :own]], mask, logsum.at[0])

    return call(
        body, 2,
        [whole(rows_low)] + layer.qkv() + [
            per_group(layer.bias_qkv), whole(segs[None, :]), whole(segs[:, None])
        ],
        [
            out_group((2, n, wide), LOW), out_group((2, own, width), LOW), out_group((2, 8, own), F32),
        ],
        [pltpu.VMEM((own, own), F32)],
        flops=4 * n * depth * wide + 8 * own * own * width,
        exps=2 * own * own * width // HEAD_DIM,
    )


def shared_call(layer, rows, proj, away_low, context_own, segs, half):
    n, depth = rows.shape
    width, wide, own = layer.width, 3 * layer.width, 2 * half
    count = 2 * len(layer.qkv_blocks)

    def body(rows, proj, away, *refs):
        weights = pairs_of(refs[:count])
        (
            out_one, out_two, bias, segs_q, segs_k, context_own, norms,
            proj_away, context, logsum, hidden_low, normed_one, recip_one, mask, total,
        ) = refs[count:]
        i = pl.program_id(0)
        make_mask(segs_q, segs_k, mask)
        put_projection(away[...], weights, layer.used, bias, proj_away.at[0])
        context[0, :own] = context_own[0]
        context[0, own:] = attend(width, [proj.at[0], proj_away.at[0]], mask, logsum.at[0])
        out_cols = joined((out_one, out_two), slice(layer.out_from, layer.out_from + width))

        @pl.when(i == 0)
        def _():
            total[...] = dot(context[0], out_cols, 1, 1)

        @pl.when(i == 1)
        def _():
            for at in row_tiles(n):
                value = rows[at, :].astype(F32) + norms[2:3, :]
                value = value + (total[at, :] + dot(context[0, at], out_cols, 1, 1))
                value, normed, recip = normalize(value, norms[0:1, :], norms[3:4, :])
                hidden_low[at, :] = value.astype(LOW)
                normed_one[at, :] = normed.astype(LOW)
                recip_one[at, :] = recip

    return call(
        body, 2,
        [
            whole(rows), (proj, (1, half, wide), lambda i: (i, 2, 0)), whole(away_low),
        ] + layer.qkv() + layer.out() + [
            per_group(layer.bias_qkv), whole(segs[None, :half]),
            whole(segs[:, None]), per_group(context_own), whole(layer.norms),
        ],
        [
            out_group((2, half, wide), LOW), out_group((2, n, width), LOW), out_group((2, 8, half), F32),
            out_whole((n, depth), LOW), out_whole((n, depth), LOW), out_whole((n, 1), F32),
        ],
        [pltpu.VMEM((own, half), F32), pltpu.VMEM((n, depth), F32)],
        flops=4 * depth * (n * width + half * wide) + 8 * own * half * width,
        exps=2 * own * half * width // HEAD_DIM,
    )


def ffn_call(layer, hidden_low, wide):
    n, depth = hidden_low.shape
    steps, _, size = layer.bias_up.shape
    per = steps // 2

    def body(
        hidden_low, norms, bias_up, up_one, up_two, down_one, down_two,
        act, slope, output, normed_two, recip_two, total,
    ):
        i = pl.program_id(0)

        @pl.when(i == 0)
        def _():
            total[...] = hidden_low[...].astype(F32) + norms[4:5, :]

        up, down = joined((up_one, up_two)), joined((down_one, down_two))
        for at in row_tiles(n):
            pre = dot(hidden_low[at, :], up, 1, 0) + bias_up[0]
            bell = 0.5 + 0.5 * lax.erf(pre * math.sqrt(0.5))
            low = (pre * bell).astype(LOW)
            act[0, at, :] = low
            slope[0, at, :] = (
                bell + pre * (jnp.exp(-0.5 * pre * pre) * (1.0 / math.sqrt(2.0 * math.pi)))
            ).astype(LOW)
            total[at, :] += dot(low, down, 1, 1)

        @pl.when(i == steps - 1)
        def _():
            for at in row_tiles(n):
                value, normed, recip = normalize(total[at, :], norms[1:2, :], norms[5:6, :])
                output[at, :] = value.astype(output.dtype)
                normed_two[at, :] = normed.astype(LOW)
                recip_two[at, :] = recip

    neurons = per * size
    ffn_out = ((2, n, neurons), LOW, (1, n, size), lambda i: (i // per, 0, i % per))
    return call(
        body, steps,
        [
            whole(hidden_low), whole(layer.norms), per_group(layer.bias_up),
        ] + layer.ffn(layer.up) + layer.ffn(layer.down),
        [
            ffn_out, ffn_out, out_whole((n, depth), F32 if wide else LOW), out_whole((n, depth), LOW),
            out_whole((n, 1), F32),
        ],
        [pltpu.VMEM((n, depth), F32)],
        flops=8 * n * depth * neurons,
        exps=4 * n * neurons,
    )


def add_rows(sums, row, value, at):
    value = jnp.sum(value, axis=0, keepdims=True)
    if at.start == 0:
        sums[row : row + 1, :] = value
    else:
        sums[row : row + 1, :] += value


def ffn_back_call(layer, grad, extra, kept, half):
    n, depth = grad.shape
    steps, _, size = layer.bias_up.shape
    per = steps // 2
    has_extra = extra is not None

    def body(grad, *refs):
        extra = refs[0] if has_extra else None
        (
            normed_one, recip_one, normed_two, recip_two, norms, slope, up_one, up_two, down_one, down_two,
            d_final_low, d_pre, d_mid_low, sums, bias_sums, total,
        ) = refs[1:] if has_extra else refs
        i = pl.program_id(0)
        gain = lambda at: norms[at : at + 1, :]

        @pl.when(i == 0)
        def _():
            sums[...] = jnp.zeros_like(sums)
            for at in row_tiles(n):
                value = grad[at, :].astype(F32)
                if has_extra and at.start >= 2 * half:
                    value = value + extra[at.start - 2 * half : at.stop - 2 * half, :].astype(F32)
                normed = normed_two[at, :].astype(F32)
                back = normalize_back(value, normed, recip_two[at, :], gain(1))
                total[at, :] = back
                d_final_low[at, :] = back.astype(LOW)
                add_rows(sums, 1, value * normed, at)
                add_rows(sums, 5, value, at)
                add_rows(sums, 4, back, at)

        bias = None
        up, down = joined((up_one, up_two)), joined((down_one, down_two))
        for at in row_tiles(n):
            d_act = dot(d_final_low[at, :], down, 1, 0)
            low = (d_act * slope[0, at, :].astype(F32)).astype(LOW)
            d_pre[0, at, :] = low
            one = jnp.sum(low.astype(F32), axis=0, keepdims=True)
            bias = one if bias is None else bias + one
            total[at, :] += dot(low, up, 1, 1)
        bias_sums[0] = bias

        @pl.when(i == steps - 1)
        def _():
            for at in row_tiles(n):
                value = total[at, :]
                normed = normed_one[at, :].astype(F32)
                back = normalize_back(value, normed, recip_one[at, :], gain(0))
                d_mid_low[at, :] = back.astype(LOW)
                add_rows(sums, 0, value * normed, at)
                add_rows(sums, 3, value, at)
                add_rows(sums, 2, back, at)

    neurons = per * size
    blocks = ((1, n, size), lambda i: (i // per, 0, i % per))
    return call(
        body, steps,
        [whole(grad)] + ([whole(extra)] if has_extra else []) + [
            whole(kept["normed_one"]), whole(kept["recip_one"]), whole(kept["normed_two"]),
            whole(kept["recip_two"]), whole(layer.norms), (kept["slope"],) + blocks,
        ] + layer.ffn(layer.up) + layer.ffn(layer.down),
        [
            out_whole((n, depth), LOW), ((2, n, neurons), LOW) + blocks, out_whole((n, depth), LOW),
            out_whole((8, depth), F32), out_group((steps, 1, size), F32),
        ],
        [pltpu.VMEM((n, depth), F32)],
        flops=8 * n * depth * neurons,
    )


def ffn_back_first_call(layer, grad, extra, kept, half):
    n, depth = grad.shape
    steps, _, size = layer.bias_up.shape
    per = steps // 2

    def body(
        grad, extra, normed_two, recip_two, norms, slope, down_one, down_two,
        d_final_low, d_pre, sums, bias_sums,
    ):
        i = pl.program_id(0)

        @pl.when(i == 0)
        def _():
            sums[...] = jnp.zeros_like(sums)
            for at in row_tiles(n):
                value = grad[at, :].astype(F32)
                if at.start >= 2 * half:
                    value = value + extra[at.start - 2 * half : at.stop - 2 * half, :].astype(F32)
                normed = normed_two[at, :].astype(F32)
                back = normalize_back(value, normed, recip_two[at, :], norms[1:2, :])
                d_final_low[at, :] = back.astype(LOW)
                add_rows(sums, 1, value * normed, at)
                add_rows(sums, 5, value, at)
                add_rows(sums, 4, back, at)

        bias = None
        down = joined((down_one, down_two))
        for at in row_tiles(n):
            d_act = dot(d_final_low[at, :], down, 1, 0)
            low = (d_act * slope[0, at, :].astype(F32)).astype(LOW)
            d_pre[0, at, :] = low
            one = jnp.sum(low.astype(F32), axis=0, keepdims=True)
            bias = one if bias is None else bias + one
        bias_sums[0] = bias

    neurons = per * size
    blocks = ((1, n, size), lambda i: (i // per, 0, i % per))
    return call(
        body, steps,
        [
            whole(grad), whole(extra), whole(kept["normed_two"]), whole(kept["recip_two"]),
            whole(layer.norms), (kept["slope"],) + blocks,
        ] + layer.ffn(layer.down),
        [
            out_whole((n, depth), LOW), ((2, n, neurons), LOW) + blocks,
            out_whole((8, depth), F32), out_group((steps, 1, size), F32),
        ],
        [],
        flops=4 * n * depth * neurons,
    )


def ffn_back_second_call(layer, d_final_low, d_pre, kept):
    n, depth = d_final_low.shape
    steps, _, size = layer.bias_up.shape
    per = steps // 2

    def body(d_final, d_pre, normed_one, recip_one, norms, up_one, up_two, d_mid_low, sums, total):
        i = pl.program_id(0)

        @pl.when(i == 0)
        def _():
            total[...] = d_final[...].astype(F32)

        up = joined((up_one, up_two))
        for at in row_tiles(n):
            total[at, :] += dot(d_pre[0, at, :], up, 1, 1)

        @pl.when(i == steps - 1)
        def _():
            sums[...] = jnp.zeros_like(sums)
            for at in row_tiles(n):
                value = total[at, :]
                normed = normed_one[at, :].astype(F32)
                back = normalize_back(value, normed, recip_one[at, :], norms[0:1, :])
                d_mid_low[at, :] = back.astype(LOW)
                add_rows(sums, 0, value * normed, at)
                add_rows(sums, 3, value, at)
                add_rows(sums, 2, back, at)

    blocks = ((1, n, size), lambda i: (i // per, 0, i % per))
    return call(
        body, steps,
        [
            whole(d_final_low), (d_pre,) + blocks, whole(kept["normed_one"]), whole(kept["recip_one"]),
            whole(layer.norms),
        ] + layer.ffn(layer.up),
        [out_whole((n, depth), LOW), out_whole((8, depth), F32)],
        [pltpu.VMEM((n, depth), F32)],
        flops=4 * n * depth * per * size,
    )


def shared_back_call(layer, d_mid_low, kept, segs, half):
    n, depth = d_mid_low.shape
    width, wide, own = layer.width, 3 * layer.width, 2 * half
    count = 2 * len(layer.qkv_blocks)

    def body(d_mid, proj, away, logsum, *refs):
        weights = pairs_of(refs[:count])
        out_one, out_two, segs_q, segs_k, d_proj, d_away, sums, back, mask, total = refs[count:]
        i = pl.program_id(0)
        make_mask(segs_q, segs_k, mask)
        out_cols = joined((out_one, out_two), slice(layer.out_from, layer.out_from + width))
        d_context = dot(d_mid[...], out_cols, 1, 0).astype(LOW)
        attend_back(
            width, [proj.at[0], away.at[0]], mask, logsum.at[0], d_context,
            [d_proj.at[0], d_away.at[0]], sums.at[0],
        )
        part = through_projection(d_away[0], weights, layer.used)

        @pl.when(i == 0)
        def _():
            total[...] = part

        @pl.when(i == 1)
        def _():
            back[...] = (total[...] + part).astype(LOW)

    return call(
        body, 2,
        [
            (d_mid_low, (half, depth), lambda i: (2, 0)), (kept["proj"], (1, half, wide), lambda i: (i, 2, 0)),
            per_group(kept["proj_away"]), per_group(kept["logsum_shared"]),
        ] + layer.qkv() + layer.out() + [whole(segs[None, :half]), whole(segs[:, None])],
        [
            out_group((2, half, wide), LOW), out_group((2, half, wide), LOW), out_group((2, 8, wide), F32),
            out_whole((half, depth), LOW),
        ],
        [pltpu.VMEM((own, half), F32), pltpu.VMEM((half, depth), F32)],
        flops=4 * half * depth * (wide + width) + 20 * own * half * width,
        exps=2 * own * half * width // HEAD_DIM,
    )


def own_back_call(layer, d_mid_low, d_shared, kept, segs, half, with_rows):
    n, depth = d_mid_low.shape
    width, wide, own = layer.width, 3 * layer.width, 2 * half
    count = 2 * len(layer.qkv_blocks) if with_rows else 0

    def body(d_mid_low, d_shared, proj, logsum, out_one, out_two, segs_q, segs_k, *refs):
        i = pl.program_id(0)
        if with_rows:
            d_mid, weights = refs[0], pairs_of(refs[1 : count + 1])
            d_proj, sums, d_rows, mask, total = refs[count + 1 :]
        else:
            d_proj, sums, mask = refs
        make_mask(segs_q, segs_k, mask)
        out_cols = joined((out_one, out_two), slice(layer.out_from, layer.out_from + width))
        d_context = dot(d_mid_low[...], out_cols, 1, 0).astype(LOW)
        attend_back(
            width, [proj.at[0]], mask, logsum.at[0], d_context, [d_proj.at[0, :own]], sums.at[0]
        )
        d_proj[0, own:] = d_shared[0]
        if with_rows:
            part = through_projection(d_proj[0], weights, layer.used)

            @pl.when(i == 0)
            def _():
                total[...] = d_mid[...].astype(F32) + part

            @pl.when(i == 1)
            def _():
                d_rows[...] = (total[...] + part).astype(LOW)

    return call(
        body, 2,
        [
            (d_mid_low, (own, depth), lambda i: (0, 0)), per_group(d_shared),
            (kept["proj"], (1, own, wide), lambda i: (i, 0, 0)), per_group(kept["logsum_own"]),
        ] + layer.out() + [whole(segs[None, :]), whole(segs[:, None])]
        + ([whole(d_mid_low)] + layer.qkv() if with_rows else []),
        [out_group((2, n, wide), LOW), out_group((2, 8, wide), F32)]
        + ([out_whole((n, depth), LOW)] if with_rows else []),
        [pltpu.VMEM((own, own), F32)] + ([pltpu.VMEM((n, depth), F32)] if with_rows else []),
        flops=4 * depth * (n * wide * with_rows + own * width) + 20 * own * own * width,
        exps=2 * own * own * width // HEAD_DIM,
    )


def rows_back_call(layer, d_mid_low, d_proj):
    n, depth = d_mid_low.shape
    wide = 3 * layer.width

    def body(d_mid, d_proj, *refs):
        weights, d_rows = pairs_of(refs[:-1]), refs[-1]

        @pl.when(pl.program_id(0) == 0)
        def _():
            d_rows[...] = d_mid[...].astype(F32)

        d_rows[...] += through_projection(d_proj[0], weights, layer.used)

    return call(
        body, 2, [whole(d_mid_low), per_group(d_proj)] + layer.qkv(), [out_whole((n, depth), F32)], [],
        flops=4 * depth * n * wide,
    )[0]


class Grads:
    def __init__(self, entries, columns, cut):
        self.entries, self.columns, self.cut = entries, columns, cut
        sizes = [end - start for _, start, end in columns]
        self.size_a, self.size_b = sum(sizes[:cut]), sum(sizes[cut:])

    def inputs(self, at, side):
        out = []
        for pairs in self.entries:
            for left, right in pairs:
                half = (left.shape[0], left.shape[1] // 2)
                out += [(left, half, lambda i: (0, side)), per_group(right, at)]
        return out

    def flops(self, rows):
        return sum(
            4 * rows * left.shape[0] * right.shape[2] for pairs in self.entries for left, right in pairs
        )

    def product(self, refs, entry, start, end):
        first = sum(len(pairs) for pairs in self.entries[:entry])
        total = None
        for at in range(first, first + len(self.entries[entry])):
            one = dot(refs[2 * at][...], refs[2 * at + 1][0, :, start:end], 0, 0)
            total = one if total is None else total + one
        return total

    def send(self):
        rows = self.entries[0][0][0].shape[1] // 2
        size = self.size_a + self.size_b

        def body(*refs):
            col = 0
            for entry, start, end in self.columns:
                part = self.product(refs, entry, start, end)
                refs[-1][0, :, col : col + end - start] = part.astype(LOW)
                col += end - start

        return call(
            body, 2, self.inputs(lambda i: i, 1), [out_group((2, rows, size), LOW)], [], self.flops(rows)
        )[0]

    def keep(self, got):
        rows = self.entries[0][0][0].shape[1] // 2
        half = rows // 2

        def body(got, *refs):
            send_a, keep_a, send_b, keep_b = refs[-4:]
            i = pl.program_id(0)
            col = 0
            for at, (entry, start, end) in enumerate(self.columns):
                part = self.product(refs, entry, start, end)
                part = part + got[0, :, col : col + end - start].astype(F32)
                if at < self.cut:
                    place = slice(col, col + end - start)

                    @pl.when(i == 0)
                    def _():
                        send_a[:, place] = part.astype(LOW)

                    @pl.when(i == 1)
                    def _():
                        keep_a[:, place] = part
                else:
                    place = slice(col - self.size_a, col - self.size_a + end - start)
                    keep_b[0, :, place] = part[:half]
                    send_b[0, :, place] = part[half:].astype(LOW)
                col += end - start

        return call(
            body, 2,
            [per_group(got, lambda i: 1 - i)] + self.inputs(lambda i: 1 - i, 0),
            [
                out_whole((rows, self.size_a), LOW), out_whole((rows, self.size_a), F32),
                out_group((2, half, self.size_b), LOW), out_group((2, half, self.size_b), F32),
            ],
            [], self.flops(rows),
        )


class Reduce:
    def __init__(self, grads):
        self.grads = grads
        self.sends = (grads.send(),)
        self.got = (swap_core(self.sends[0]),)
        self.work = self._run()

    def _run(self):
        count = lax.axis_size("dp") // 4
        send_a, keep_a, send_b, keep_b = self.grads.keep(self.got[0])
        fourth = keep_a.shape[0] // 2
        self.sends = (send_a, send_b)
        self.got = (swap_y(send_a), swap_x(send_b))
        yield
        a = keep_a + self.got[0].astype(F32)
        b = keep_b + self.got[1].astype(F32)
        self.sends = (a[fourth:].astype(LOW), b[0].astype(LOW))
        self.got = (swap_x(self.sends[0]), swap_y(self.sends[1]))
        a, b = a[:fourth], b[1]
        yield
        both = jnp.concatenate([a + self.got[0].astype(F32), b + self.got[1].astype(F32)], axis=1)
        both = both.reshape((count, -1) + both.shape[1:])
        self.sends = tuple(both[back].astype(LOW) for back in range(1, count))
        self.got = tuple(ring_shift(send, -back) for back, send in enumerate(self.sends, 1))
        yield
        total = both[0] + sum(got.astype(F32) for got in self.got)
        self.total = total
        self.got = self.sends = ()

    def step(self):
        next(self.work, None)


class Total:
    def __init__(self, value):
        self.total = value
        self.work = self._run()
        self.step()

    def _run(self):
        n = lax.axis_size("dp")
        self.sends = (self.total,)
        self.got = (swap_y(self.total),)
        yield
        self.total = self.total + self.got[0]
        step = 1
        while step < n:
            self.sends = (self.total,)
            self.got = (lax.ppermute(self.total, "dp", [(i, i ^ step) for i in range(n)]),)
            yield
            self.total = self.total + self.got[0]
            step *= 2
        self.got = self.sends = ()

    def step(self):
        next(self.work, None)


def round_of(*works):
    ended = lax.optimization_barrier(tuple(work.got for work in works))
    for work, got in zip(works, ended):
        work.got = got
    for work in works:
        work.step()


def before(value, *works):
    value, ended = lax.optimization_barrier((value, tuple(work.got for work in works)))
    for work, got in zip(works, ended):
        work.got = got
    return value


def forward_attn(layer, rows, proj, context_own, logsum_own, rows_low, away_low, segs, half):
    proj_away, context, logsum_shared, hidden_low, normed_one, recip_one = shared_call(
        layer, rows, proj, away_low, context_own, segs[1], half
    )
    kept = dict(
        rows_low=rows_low, away_low=away_low, proj=proj, proj_away=proj_away, context=context,
        logsum_own=logsum_own, logsum_shared=logsum_shared, hidden_low=hidden_low,
        normed_one=normed_one, recip_one=recip_one,
    )
    return hidden_low, kept


def forward_ffn(layer, hidden_low, kept, wide):
    act, slope, output, normed_two, recip_two = ffn_call(layer, hidden_low, wide)
    kept.update(act=act, slope=slope, normed_two=normed_two, recip_two=recip_two)
    return output


def backward_ffn(layer, grad, extra, kept, half):
    d_final_low, d_pre, d_mid_low, sums, bias_sums = ffn_back_call(layer, grad, extra, kept, half)
    entries = [[(kept["hidden_low"], d_pre)], [(d_final_low, kept["act"])]]
    return d_mid_low, sums[:6], bias_sums, entries


def attn_entries(kept, d_proj, d_away, d_mid_low):
    return [[(kept["rows_low"], d_proj), (kept["away_low"], d_away)], [(d_mid_low, kept["context"])]]


def on_device(
    tokens, segment_ids, out_grad,
    t_qkv, t_qv_bias, t_out, t_up, t_up_bias, t_down, t_gains, t_shifts,
    s_qkv, s_qv_bias, s_out, s_up, s_up_bias, s_down, s_gains, s_shifts,
):
    rows, half, width = tokens.shape
    first = lax.axis_index("mp") == 0
    own_row = lambda value: jnp.where(first, value[0], value[2])
    far_row = lambda value: jnp.where(first, value[2], value[0])

    norm_rows = jnp.concatenate([t_gains, t_shifts, s_gains, s_shifts], axis=0)
    norm_rows = jnp.pad(norm_rows, ((0, 128 - norm_rows.shape[0]), (0, 0)))
    t_width, s_width = t_qkv.shape[2], s_qkv.shape[2]
    size = s_up.shape[1]
    per = t_up.shape[1] // size
    count, block = lax.axis_size("dp") // 4, t_up.shape[0]
    together = lambda *values: lax.optimization_barrier(values)
    every = slice(None)

    def columns(start, width):
        return slice(start, start + width)

    t_cut, t_all = 2 * t_width, 4 * t_width + 128
    f_cut = per * size
    s_cut = size + 2 * s_width
    packed_t = moves(
        [t_qkv, t_out.T, norm_rows.T], [(block, t_all)],
        [(0, (i,), 0, (every, columns(i * t_width, t_width))) for i in range(3)]
        + [
            (1, (every,), 0, (every, columns(3 * t_width, t_width))),
            (2, (every,), 0, (every, columns(4 * t_width, 128))),
        ],
    )[0]
    packed_f, student_a, student_b = moves(
        [t_up, t_down.T, s_up, s_qkv, s_out.T, s_down.T],
        [(block, 2 * f_cut), (block, s_cut), (block, s_cut)],
        [
            (0, (every,), 0, (every, columns(0, f_cut))), (1, (every,), 0, (every, columns(f_cut, f_cut))),
            (2, (every,), 1, (every, columns(0, size))), (3, (0,), 1, (every, columns(size, s_width))),
            (4, (every,), 1, (every, columns(size + s_width, s_width))),
            (5, (every,), 2, (every, columns(0, size))), (3, (1,), 2, (every, columns(size, s_width))),
            (3, (2,), 2, (every, columns(size + s_width, s_width))),
        ],
    )

    def along_z(value):
        return [value] + [ring_shift(value, at) for at in range(1, count)]

    def of_line(pieces, cut):
        rest = pieces[0].shape[1] - cut
        return moves(
            pieces, [(count, block, cut), (count, block, rest)],
            [(i, (every, columns(start, wide)), at, (i,)) for i in range(count)
             for at, (start, wide) in enumerate(((0, cut), (cut, rest)))],
        )

    def first_plane(a, got_a, b, got_b):
        return moves(
            [a, got_a, b, got_b], [(2,) + a.shape, (2,) + b.shape],
            [(0, (every,), 0, (0,)), (1, (every,), 0, (1,)), (2, (every,), 1, (0,)), (3, (every,), 1, (1,))],
        )

    def both_planes(a, got_a, b, got_b, order):
        copies, col = [], 0
        for of_b, start, wide in order:
            taken, place = (every, every, every, columns(start, wide)), (every, every, columns(col, wide))
            if of_b:
                copies += [(2, taken, 0, (every, 0) + place), (3, taken, 0, (every, 1) + place)]
            else:
                copies += [(0, taken, 0, (0, every) + place), (1, taken, 0, (1, every) + place)]
            col += wide
        out = moves([a, got_a, b, got_b], [(2, 2, count, block, col)], copies)[0]
        return out.reshape(2, width // 2, col)

    def with_core(own):
        return own, swap_core(own)

    bias_parts = [t_qv_bias[0], t_qv_bias[1], t_up_bias, s_qv_bias[0], s_qv_bias[1], s_up_bias]
    to_own = feature_order(width)
    into = (lax.iota(jnp.int32, width)[:, None] == to_own[None, :]).astype(LOW)
    def reorder(value):
        return jnp.dot(value, into, preferred_element_type=F32).astype(LOW)


    spin = lambda segs: jnp.where(first, segs, jnp.roll(segs, half))
    segs = (spin(own_row(segment_ids)), spin(segment_ids[1]))

    line_t, got_own = along_z(packed_t), swap_y(far_row(tokens))
    *line_t, got_own, into, segs, packed_f, student_a, student_b = together(
        *line_t, got_own, into, segs, packed_f, student_a, student_b
    )
    attn_a, attn_b = of_line(line_t, t_cut)
    got_a, got_b = swap_x(attn_a), swap_y(attn_b)
    line_f = along_z(packed_f)
    student_x, student_y = swap_x(student_a), swap_y(student_b)
    got_a, got_b, student_x, student_y, line_f[1] = together(got_a, got_b, student_x, student_y, line_f[1])
    inputs = reorder(jnp.concatenate([own_row(tokens), got_own, tokens[1]], axis=0))
    attn_a, attn_b = first_plane(attn_a, got_a, attn_b, got_b)
    got_a, got_b = swap_y(attn_a), swap_x(attn_b)
    line_s = along_z(moves(
        [student_a, student_x, student_b, student_y], [(2, block, 2 * s_cut)],
        [(i, (every,), 0, (i % 2, every, columns(i // 2 * s_cut, s_cut))) for i in range(4)],
    )[0])
    got_a, got_b, inputs, *line_f[2:] = together(got_a, got_b, inputs, *line_f[2:])
    attn = both_planes(
        attn_a, got_a, attn_b, got_b, [(False, 0, t_cut), (True, 0, t_all - t_cut)]
    )
    attn = with_core(attn)
    ffn_a, ffn_b = of_line(list(after(line_f, attn[0])), f_cut)
    got_a, got_b = swap_x(ffn_a), swap_y(ffn_b)
    bias_own = jnp.concatenate(bias_parts)
    bias_far = swap_y(bias_own)
    attn, got_a, got_b, bias_far = together(attn, got_a, got_b, bias_far)
    ffn_a, ffn_b = first_plane(ffn_a, got_a, ffn_b, got_b)
    got_a, got_b = swap_y(ffn_a), swap_x(ffn_b)
    got_shared = swap_y(tokens[1])
    norms = jnp.concatenate([half[0, :, -128:-116] for half in attn], axis=0).T.astype(F32)
    norms_of = lambda at: jnp.pad(norms[at : at + 6], ((0, 2), (0, 0)))
    bias_all = jnp.stack([bias_own, bias_far]).astype(F32)
    cuts = [0]
    for part in bias_parts:
        cuts.append(cuts[-1] + part.shape[0])
    pick = [bias_all[:, cuts[i] : cuts[i + 1]] for i in range(6)]
    bias_qkv = lambda q, v: jnp.concatenate([q, jnp.zeros_like(q), v], axis=1)[:, None, :]
    teacher = Layer(
        t_width, None, None, [(attn, t_width, i, t_width) for i in range(3)], (attn, t_width, 3, t_width), 0,
        norms_of(0), bias_qkv(pick[0], pick[1]), pick[2].reshape(2 * per, 1, size),
    )

    grad_in = jnp.concatenate([own_row(out_grad), swap_y(far_row(out_grad)), out_grad[1]], axis=0)

    inputs, ffn_a, ffn_b = together(inputs, ffn_a, ffn_b)
    proj, context_own, logsum_own = project_call(teacher, inputs, segs[0], half)
    proj, got_shared, *line_s[1:-1] = together(proj, got_shared, *line_s[1:-1])
    away_low = reorder(got_shared)
    hidden, t_kept = forward_attn(
        teacher, inputs, proj, context_own, logsum_own, inputs, away_low, segs, half
    )
    hidden, got_a, got_b, line_s[-1] = together(hidden, got_a, got_b, line_s[-1])
    ffn = both_planes(ffn_a, got_a, ffn_b, got_b, [(False, 0, f_cut), (True, 0, f_cut)])
    ffn = with_core(ffn)
    student_a, student_b = moves(
        line_s, [(2, count, block, s_cut)] * 2,
        [(i, (every, every, columns(at * s_cut, s_cut)), at, (every, i)) for i in range(count) for at in range(2)],
    )
    got_a, got_b = swap_y(student_a), swap_x(student_b)
    hidden, ffn = together(hidden, ffn)
    teacher.up, teacher.down = (ffn, 0), (ffn, per)
    middle_low = forward_ffn(teacher, hidden, t_kept, False)
    away_low = swap_y(middle_low[2 * half :])
    middle_low, got_a, got_b, grad_in = together(middle_low, got_a, got_b, grad_in)
    grad_in = reorder(grad_in)
    student_w = with_core(both_planes(
        student_a, got_a, student_b, got_b,
        [(False, 0, size), (True, 0, size), (False, size, 2 * s_width), (True, size, 2 * s_width)],
    ))
    narrow = 2 * s_width
    place = 2 * size // narrow
    student = Layer(
        s_width, (student_w, 0), (student_w, 1),
        [(student_w, narrow, place, s_width), (student_w, narrow, place + 1, narrow)],
        (student_w, narrow, place, s_width), s_width, norms_of(6), bias_qkv(pick[3], pick[4]),
        pick[5].reshape(2, 1, size),
    )
    proj, context_own, logsum_own = project_call(student, middle_low, segs[0], half)
    proj, away_low = together(proj, away_low)
    hidden, s_kept = forward_attn(
        student, middle_low, proj, context_own, logsum_own, middle_low, away_low, segs, half
    )
    last = forward_ffn(student, hidden, s_kept, True)

    def far_half(value):
        return swap_y(value[half : 2 * half].astype(LOW))

    def to_rows(value, far):
        near = jnp.concatenate([value[:half], value[2 * half :]], axis=0)
        high = near.astype(LOW)
        low = (near - high.astype(F32)).astype(LOW)
        back = lambda part: jnp.einsum("nr,dr->nd", part, into, preferred_element_type=F32)
        near, far = back(high) + back(low), back(far)
        return jnp.stack([jnp.where(first, near[:half], far), near[half:], jnp.where(first, far, near[:half])])

    far_last = far_half(last)

    d_mid_low, s_norm_grads, s_up_grad, s_entries = backward_ffn(student, grad_in, None, s_kept, half)
    d_shared, d_away, s_sums_b, back = shared_back_call(student, d_mid_low, s_kept, segs[1], half)
    extra = swap_y(back)
    d_shared, far_last = together(d_shared, far_last)
    d_proj, s_sums_a, d_rows = own_back_call(
        student, d_mid_low, d_shared, s_kept, segs[0], half, True
    )
    d_proj, extra = lax.optimization_barrier((d_proj, extra))
    s_entries += attn_entries(s_kept, d_proj, d_away, d_mid_low)
    s_columns = [(0, 0, size), (2, 0, s_width), (3, 0, s_width), (1, 0, size), (2, s_width, 3 * s_width)]
    reduce_s = Reduce(Grads(s_entries, s_columns, 3))

    d_rows = after(d_rows, reduce_s.sends)
    d_final_low, d_pre, t_sums_two, t_up_grad = ffn_back_first_call(
        teacher, d_rows, extra, t_kept, half
    )
    d_pre = before(d_pre, reduce_s)
    reduce_s.step()
    d_pre = after(d_pre, reduce_s.sends)
    f_entries = [[(t_kept["hidden_low"], d_pre)], [(d_final_low, t_kept["act"])]]
    reduce_f = Reduce(Grads(f_entries, [(0, 0, per * size), (1, 0, per * size)], 1))
    d_pre = after(d_pre, reduce_f.sends)
    d_mid_low, t_sums_one = ffn_back_second_call(teacher, d_final_low, d_pre, t_kept)
    t_norm_grads = (t_sums_one + t_sums_two)[:6]
    d_mid_low = before(d_mid_low, reduce_f)
    reduce_f.step()
    reduce_s.got = after(reduce_s.got, reduce_f.sends)
    d_mid_low = before(d_mid_low, reduce_s)
    reduce_s.step()
    d_mid_low = after(d_mid_low, reduce_s.sends)
    d_shared, d_away, t_sums_b, back = shared_back_call(teacher, d_mid_low, t_kept, segs[1], half)
    extra = swap_y(back)
    d_shared = before(d_shared, reduce_s)
    reduce_s.step()
    d_shared = after(d_shared, reduce_s.sends)
    d_proj, t_sums_a = own_back_call(teacher, d_mid_low, d_shared, t_kept, segs[0], half, False)
    t_entries = attn_entries(t_kept, d_proj, d_away, d_mid_low)
    reduce_t = Reduce(
        Grads(t_entries, [(0, 0, 2 * t_width), (0, 2 * t_width, 3 * t_width), (1, 0, t_width)], 1)
    )

    def qv_grad(one, two, wide):
        sums = one[:, 0] + two[:, 0]
        sums = jnp.concatenate([sums[:, :wide], sums[:, 2 * wide :]], axis=1)
        return jnp.pad(sums, ((0, 0), (0, width - 2 * wide)))

    norm_grads = jnp.concatenate([t_norm_grads, s_norm_grads], axis=0)
    norm_grads = jnp.einsum("nr,dr->nd", norm_grads, into.astype(F32), precision=lax.Precision.HIGHEST)
    qv_t, qv_s = qv_grad(t_sums_a, t_sums_b, t_width), qv_grad(s_sums_a, s_sums_b, s_width)
    mine = jnp.concatenate([t_up_grad[:per, 0], s_up_grad[:1, 0], qv_t[:1], qv_s[:1]], axis=0)
    other = jnp.concatenate([t_up_grad[per:, 0], s_up_grad[1:, 0], qv_t[1:], qv_s[1:]], axis=0)
    small = Total(jnp.concatenate(
        [norm_grads, jnp.where(first, mine, other), jnp.where(first, other, mine)], axis=0
    ))
    reduce_f.got = after(reduce_f.got, reduce_t.sends)
    round_of(reduce_f, small)
    reduce_t.got = after(reduce_t.got, reduce_f.sends)
    reduce_t.step()
    reduce_f.got = after(reduce_f.got, reduce_t.sends)
    round_of(reduce_f, reduce_s, small)
    d_rows = rows_back_call(teacher, *after((d_mid_low, d_proj), reduce_t.sends))
    reduce_t.got = after(reduce_t.got, d_rows)
    far_rows = far_half(d_rows)
    round_of(reduce_t, small)
    d_rows, last = after((d_rows, last), reduce_t.sends)
    d_rows = jnp.concatenate([d_rows[: 2 * half], d_rows[2 * half :] + extra.astype(F32)], axis=0)
    input_grad, output = to_rows(d_rows, far_rows), to_rows(last, far_last)
    round_of(reduce_t, reduce_f, small)
    round_of(reduce_t, small)
    for work in (reduce_f, reduce_s, small):
        while work.got:
            work.step()
    s_sum, f_sum, small = reduce_s.total, reduce_f.total, small.total

    piece = width // lax.axis_size("dp")
    norm_sum = lax.dynamic_slice_in_dim(small[:12], lax.axis_index("dp") * piece, piece, 1)
    bias_sum = small[12:].reshape(2, -1, width)
    bias_sum = jnp.where(first, bias_sum[0], bias_sum[1])
    t_qv_sum, s_qv_sum = bias_sum[per + 1], bias_sum[per + 2, : 2 * s_width]

    def cut(value, *sizes):
        out = []
        for one in sizes:
            out.append(value[:, :one])
            value = value[:, one:]
        return out

    t_up_sum, t_down_sum = cut(f_sum, per * size, per * size)
    s_up_sum, sq, so, s_down_sum, sk, sv = cut(s_sum, size, s_width, s_width, size, s_width, s_width)
    done = (
        output, input_grad, t_qv_sum.reshape(2, -1), t_up_sum, bias_sum[:per].reshape(-1), t_down_sum.T,
        norm_sum[0:2], norm_sum[2:6], jnp.stack([sq, sk, sv]), s_qv_sum.reshape(2, -1), so.T, s_up_sum,
        bias_sum[per], s_down_sum.T, norm_sum[6:8], norm_sum[8:12],
    )
    done, reduce_t.got = together(done, reduce_t.got)
    while reduce_t.got:
        reduce_t.step()
    tq, tk, tv, to = cut(reduce_t.total, t_width, t_width, t_width, t_width)
    return done[:2] + (jnp.stack([tq, tk, tv]), done[2], to.T) + done[3:]


def solution(mesh):
    layer = (
        P(None, "dp", "mp"), P(None, "mp"), P("mp", "dp"), P("dp", "mp"), P("mp"), P("mp", "dp"),
        P(None, "dp"), P(None, "dp"),
    )
    rows = P("dp", "mp", None)
    return jax.shard_map(
        on_device,
        mesh=mesh,
        in_specs=(rows, P("dp", None), rows) + layer + layer,
        out_specs=(rows, rows) + layer + layer,
        check_vma=False,
    )
```

```python
import functools
import math

import jax
import jax.numpy as jnp
from jax import lax
from jax.experimental import pallas as pl
from jax.experimental.pallas import tpu as pltpu
from jax.sharding import PartitionSpec as P

HEAD_DIM = 64
LOW = jnp.bfloat16
F32 = jnp.float32


def ring_of(count):
    return list(range(0, count, 2)) + list(range(1, count, 2))[::-1]


def swap_y(value):
    return lax.ppermute(value, "mp", [(0, 1), (1, 0)])


def swap_x(value):
    n = lax.axis_size("dp")
    return lax.ppermute(value, "dp", [(i, i ^ 2) for i in range(n)])


def swap_core(value):
    n = lax.axis_size("dp")
    return lax.ppermute(value, "dp", [(i, i ^ 1) for i in range(n)])


def ring_shift(value, step):
    count = lax.axis_size("dp") // 4
    ring = ring_of(count)
    pairs = []
    for place in range(count):
        for low in range(4):
            pairs.append((ring[place] * 4 + low, ring[(place + step) % count] * 4 + low))
    return lax.ppermute(value, "dp", pairs)


def feature_order(width):
    n = lax.axis_size("dp")
    count, rows = n // 4, width // n
    me = lax.axis_index("dp")
    z, x, core = me // 4, (me // 2) % 2, me % 2
    place = jnp.where(z % 2 == 0, z // 2, count - 1 - z // 2)
    at = lax.iota(jnp.int32, width)
    row = at % rows
    back = (at // rows) % count
    x_rel = (at // (rows * count)) % 2
    core_rel = at // (rows * count * 2)
    from_place = (place - back + count) % count
    half = (count + 1) // 2
    z_abs = jnp.where(from_place < half, 2 * from_place, 2 * (count - 1 - from_place) + 1)
    block = z_abs * 4 + (x ^ x_rel) * 2 + (core ^ core_rel)
    return block * rows + row


def after(value, *others):
    return lax.optimization_barrier((value, others))[0]


VMEM_BYTES = 26 << 20
TILE = 256


def dot(left, right, left_at, right_at):
    return lax.dot_general(
        left, right, (((left_at,), (right_at,)), ((), ())), preferred_element_type=F32
    )


def call(body, steps, inputs, outputs, scratch, flops, exps=0):
    size = lambda shape, dtype: math.prod(shape) * jnp.dtype(dtype).itemsize
    moved = sum(size(array.shape, array.dtype) for array, _, _ in inputs)
    moved += sum(size(shape, dtype) for shape, dtype, _, _ in outputs)
    return pl.pallas_call(
        body,
        grid=(steps,),
        in_specs=[pl.BlockSpec(block, index) for _, block, index in inputs],
        out_specs=[pl.BlockSpec(block, index) for _, _, block, index in outputs],
        out_shape=[jax.ShapeDtypeStruct(shape, dtype) for shape, dtype, _, _ in outputs],
        scratch_shapes=scratch,
        compiler_params=pltpu.CompilerParams(
            dimension_semantics=("arbitrary",), vmem_limit_bytes=VMEM_BYTES
        ),
        cost_estimate=pl.CostEstimate(
            flops=flops // 2, bytes_accessed=moved // 2, transcendentals=exps // 2
        ),
    )(*[array for array, _, _ in inputs])


def moves(arrays, shapes, copies):
    def body(*refs):
        for source, taken, target, place in copies:
            refs[len(arrays) + target][place] = refs[source][taken]

    moved = 2 * sum(math.prod(shape) for shape in shapes)
    return pl.pallas_call(
        body,
        out_shape=[jax.ShapeDtypeStruct(shape, LOW) for shape in shapes],
        compiler_params=pltpu.CompilerParams(vmem_limit_bytes=VMEM_BYTES),
        cost_estimate=pl.CostEstimate(flops=0, bytes_accessed=moved, transcendentals=0),
    )(*arrays)


def whole(array):
    rank = array.ndim
    return (array, array.shape, lambda i: (0,) * rank)


def per_group(array, at=lambda i: i):
    return (array, (1,) + array.shape[1:], lambda i: (at(i),) + (0,) * (array.ndim - 1))


def out_whole(shape, dtype):
    return (shape, dtype, shape, lambda i: (0,) * len(shape))


def out_group(shape, dtype, at=lambda i: i):
    return (shape, dtype, (1,) + shape[1:], lambda i: (at(i),) + (0,) * (len(shape) - 1))


class Layer:
    def __init__(self, width, up, down, qkv, out, out_from, norms, bias_qkv, bias_up):
        self.width, self.up, self.down = width, up, down
        self.qkv_blocks, self.out_block, self.out_from = qkv, out, out_from
        self.norms, self.bias_qkv, self.bias_up = norms, bias_qkv, bias_up
        self.used = [block[3] for block in qkv]

    def columns(self, block, at):
        pair, size, place, _ = block
        return [(half, (1, half.shape[1], size), lambda i: (at(i), 0, place)) for half in pair]

    def qkv(self, at=lambda i: i):
        return [one for block in self.qkv_blocks for one in self.columns(block, at)]

    def out(self, at=lambda i: i):
        return self.columns(self.out_block, at)

    def ffn(self, where):
        pair, base = where
        size, per = self.bias_up.shape[2], self.bias_up.shape[0] // 2
        return [(half, (1, half.shape[1], size), lambda i: (i // per, 0, base + i % per)) for half in pair]


def joined(pair, cols=slice(None)):
    return jnp.concatenate([half[0, :, cols] for half in pair], axis=0)


def pairs_of(refs):
    return [refs[at : at + 2] for at in range(0, len(refs), 2)]


def put_projection(rows, weights, used, bias, target):
    start = 0
    for weight, cols in zip(weights, used):
        part = dot(rows, joined(weight, slice(0, cols)), 1, 0) + bias[0, :, start : start + cols]
        target[:, start : start + cols] = part.astype(LOW)
        start += cols


def through_projection(grads, weights, used):
    start = 0
    total = None
    for weight, cols in zip(weights, used):
        part = dot(grads[:, start : start + cols], joined(weight, slice(0, cols)), 1, 1)
        total = part if total is None else total + part
        start += cols
    return total


def head_at(width, part, head):
    return slice(part * width + head * HEAD_DIM, part * width + (head + 1) * HEAD_DIM)


def join(parts, cols):
    picked = [part[:, cols] for part in parts]
    return picked[0] if len(picked) == 1 else jnp.concatenate(picked, axis=0)


def attend(width, kept, mask, logsum):
    scale = jnp.asarray(HEAD_DIM**-0.5, LOW)
    out = []
    for head in range(width // HEAD_DIM):
        query = kept[0][:, head_at(width, 0, head)] * scale
        scores = dot(join(kept, head_at(width, 1, head)), query, 1, 1) + mask[...]
        top = jnp.max(scores, axis=0, keepdims=True)
        expo = jnp.exp(scores - top)
        total = jnp.sum(expo, axis=0, keepdims=True)
        out.append(dot(join(kept, head_at(width, 2, head)), expo.astype(LOW), 0, 0) * (1.0 / total))
        logsum[head : head + 1, :] = top + jnp.log(total)
    return jnp.concatenate(out, axis=0).T.astype(LOW)


def attend_back(width, kept, mask, logsum, d_context, grads, sums):
    scale = jnp.asarray(HEAD_DIM**-0.5, LOW)
    for head in range(width // HEAD_DIM):
        at_q, at_k, at_v = (head_at(width, part, head) for part in range(3))
        query = kept[0][:, at_q] * scale
        keys = join(kept, at_k)
        d_ctx = d_context[:, head * HEAD_DIM : (head + 1) * HEAD_DIM]
        probs = jnp.exp(dot(keys, query, 1, 1) + mask[...] - logsum[head : head + 1, :])
        d_probs = dot(join(kept, at_v), d_ctx, 1, 1)
        both = probs * d_probs
        inner = jnp.sum(both, axis=0, keepdims=True)
        d_scores = (both - probs * inner).astype(LOW)
        d_values = dot(probs.astype(LOW), d_ctx, 1, 0).astype(LOW)
        d_keys = dot(d_scores, query, 1, 0).astype(LOW)
        d_query = dot(keys * scale, d_scores, 0, 0).T.astype(LOW)
        grads[0][:, at_q] = d_query
        start = 0
        for grad in grads:
            rows = grad.shape[0]
            grad[:, at_k] = d_keys[start : start + rows]
            grad[:, at_v] = d_values[start : start + rows]
            start += rows
        for grad in grads[1:]:
            grad[:, at_q] = jnp.zeros((grad.shape[0], HEAD_DIM), LOW)
        sums[0:1, at_q] = jnp.sum(d_query.astype(F32), axis=0, keepdims=True)
        sums[0:1, at_k] = jnp.zeros((1, HEAD_DIM), F32)
        sums[0:1, at_v] = jnp.sum(d_values.astype(F32), axis=0, keepdims=True)


def make_mask(segs_q, segs_k, mask):
    @pl.when(pl.program_id(0) == 0)
    def _():
        mask[...] = jnp.where(segs_k[...] == segs_q[...], 0.0, -1e9)


def normalize(value, gain, shift):
    center = value - jnp.mean(value, axis=-1, keepdims=True)
    recip = lax.rsqrt(jnp.mean(center * center, axis=-1, keepdims=True) + 1e-06)
    normed = center * recip
    return normed * gain + shift, normed, recip


def normalize_back(grad, normed, recip, gain):
    scaled = grad * gain
    mean_one = jnp.mean(scaled, axis=-1, keepdims=True)
    mean_two = jnp.mean(scaled * normed, axis=-1, keepdims=True)
    return recip * (scaled - mean_one - normed * mean_two)


def row_tiles(rows):
    return [slice(start, start + TILE) for start in range(0, rows, TILE)]


def project_call(layer, rows_low, segs, half):
    n, depth = rows_low.shape
    width, wide, own = layer.width, 3 * layer.width, 2 * half
    count = 2 * len(layer.qkv_blocks)

    def body(rows, *refs):
        weights = pairs_of(refs[:count])
        bias, segs_q, segs_k, proj, context, logsum, mask = refs[count:]
        make_mask(segs_q, segs_k, mask)
        put_projection(rows[...], weights, layer.used, bias, proj.at[0])
        context[0] = attend(width, [proj.at[0, :own]], mask, logsum.at[0])

    return call(
        body, 2,
        [whole(rows_low)] + layer.qkv() + [
            per_group(layer.bias_qkv), whole(segs[None, :]), whole(segs[:, None])
        ],
        [
            out_group((2, n, wide), LOW), out_group((2, own, width), LOW), out_group((2, 8, own), F32),
        ],
        [pltpu.VMEM((own, own), F32)],
        flops=4 * n * depth * wide + 8 * own * own * width,
        exps=2 * own * own * width // HEAD_DIM,
    )


def shared_call(layer, rows, proj, away_low, context_own, segs, half):
    n, depth = rows.shape
    width, wide, own = layer.width, 3 * layer.width, 2 * half
    count = 2 * len(layer.qkv_blocks)

    def body(rows, proj, away, *refs):
        weights = pairs_of(refs[:count])
        (
            out_one, out_two, bias, segs_q, segs_k, context_own, norms,
            proj_away, context, logsum, hidden_low, normed_one, recip_one, mask, total,
        ) = refs[count:]
        i = pl.program_id(0)
        make_mask(segs_q, segs_k, mask)
        put_projection(away[...], weights, layer.used, bias, proj_away.at[0])
        context[0, :own] = context_own[0]
        context[0, own:] = attend(width, [proj.at[0], proj_away.at[0]], mask, logsum.at[0])
        out_cols = joined((out_one, out_two), slice(layer.out_from, layer.out_from + width))

        @pl.when(i == 0)
        def _():
            total[...] = dot(context[0], out_cols, 1, 1)

        @pl.when(i == 1)
        def _():
            for at in row_tiles(n):
                value = rows[at, :].astype(F32) + norms[2:3, :]
                value = value + (total[at, :] + dot(context[0, at], out_cols, 1, 1))
                value, normed, recip = normalize(value, norms[0:1, :], norms[3:4, :])
                hidden_low[at, :] = value.astype(LOW)
                normed_one[at, :] = normed.astype(LOW)
                recip_one[at, :] = recip

    return call(
        body, 2,
        [
            whole(rows), (proj, (1, half, wide), lambda i: (i, 2, 0)), whole(away_low),
        ] + layer.qkv() + layer.out() + [
            per_group(layer.bias_qkv), whole(segs[None, :half]),
            whole(segs[:, None]), per_group(context_own), whole(layer.norms),
        ],
        [
            out_group((2, half, wide), LOW), out_group((2, n, width), LOW), out_group((2, 8, half), F32),
            out_whole((n, depth), LOW), out_whole((n, depth), LOW), out_whole((n, 1), F32),
        ],
        [pltpu.VMEM((own, half), F32), pltpu.VMEM((n, depth), F32)],
        flops=4 * depth * (n * width + half * wide) + 8 * own * half * width,
        exps=2 * own * half * width // HEAD_DIM,
    )


def ffn_call(layer, hidden_low, wide):
    n, depth = hidden_low.shape
    steps, _, size = layer.bias_up.shape
    per = steps // 2

    def body(
        hidden_low, norms, bias_up, up_one, up_two, down_one, down_two,
        act, slope, output, normed_two, recip_two, total,
    ):
        i = pl.program_id(0)

        @pl.when(i == 0)
        def _():
            total[...] = hidden_low[...].astype(F32) + norms[4:5, :]

        up, down = joined((up_one, up_two)), joined((down_one, down_two))
        for at in row_tiles(n):
            pre = dot(hidden_low[at, :], up, 1, 0) + bias_up[0]
            bell = 0.5 + 0.5 * lax.erf(pre * math.sqrt(0.5))
            low = (pre * bell).astype(LOW)
            act[0, at, :] = low
            slope[0, at, :] = (
                bell + pre * (jnp.exp(-0.5 * pre * pre) * (1.0 / math.sqrt(2.0 * math.pi)))
            ).astype(LOW)
            total[at, :] += dot(low, down, 1, 1)

        @pl.when(i == steps - 1)
        def _():
            for at in row_tiles(n):
                value, normed, recip = normalize(total[at, :], norms[1:2, :], norms[5:6, :])
                output[at, :] = value.astype(output.dtype)
                normed_two[at, :] = normed.astype(LOW)
                recip_two[at, :] = recip

    neurons = per * size
    ffn_out = ((2, n, neurons), LOW, (1, n, size), lambda i: (i // per, 0, i % per))
    return call(
        body, steps,
        [
            whole(hidden_low), whole(layer.norms), per_group(layer.bias_up),
        ] + layer.ffn(layer.up) + layer.ffn(layer.down),
        [
            ffn_out, ffn_out, out_whole((n, depth), F32 if wide else LOW), out_whole((n, depth), LOW),
            out_whole((n, 1), F32),
        ],
        [pltpu.VMEM((n, depth), F32)],
        flops=8 * n * depth * neurons,
        exps=4 * n * neurons,
    )


def add_rows(sums, row, value, at):
    value = jnp.sum(value, axis=0, keepdims=True)
    if at.start == 0:
        sums[row : row + 1, :] = value
    else:
        sums[row : row + 1, :] += value


def ffn_back_call(layer, grad, extra, kept, half):
    n, depth = grad.shape
    steps, _, size = layer.bias_up.shape
    per = steps // 2
    has_extra = extra is not None

    def body(grad, *refs):
        extra = refs[0] if has_extra else None
        (
            normed_one, recip_one, normed_two, recip_two, norms, slope, up_one, up_two, down_one, down_two,
            d_final_low, d_pre, d_mid_low, sums, bias_sums, total,
        ) = refs[1:] if has_extra else refs
        i = pl.program_id(0)
        gain = lambda at: norms[at : at + 1, :]

        @pl.when(i == 0)
        def _():
            sums[...] = jnp.zeros_like(sums)
            for at in row_tiles(n):
                value = grad[at, :].astype(F32)
                if has_extra and at.start >= 2 * half:
                    value = value + extra[at.start - 2 * half : at.stop - 2 * half, :].astype(F32)
                normed = normed_two[at, :].astype(F32)
                back = normalize_back(value, normed, recip_two[at, :], gain(1))
                total[at, :] = back
                d_final_low[at, :] = back.astype(LOW)
                add_rows(sums, 1, value * normed, at)
                add_rows(sums, 5, value, at)
                add_rows(sums, 4, back, at)

        bias = None
        up, down = joined((up_one, up_two)), joined((down_one, down_two))
        for at in row_tiles(n):
            d_act = dot(d_final_low[at, :], down, 1, 0)
            low = (d_act * slope[0, at, :].astype(F32)).astype(LOW)
            d_pre[0, at, :] = low
            one = jnp.sum(low.astype(F32), axis=0, keepdims=True)
            bias = one if bias is None else bias + one
            total[at, :] += dot(low, up, 1, 1)
        bias_sums[0] = bias

        @pl.when(i == steps - 1)
        def _():
            for at in row_tiles(n):
                value = total[at, :]
                normed = normed_one[at, :].astype(F32)
                back = normalize_back(value, normed, recip_one[at, :], gain(0))
                d_mid_low[at, :] = back.astype(LOW)
                add_rows(sums, 0, value * normed, at)
                add_rows(sums, 3, value, at)
                add_rows(sums, 2, back, at)

    neurons = per * size
    blocks = ((1, n, size), lambda i: (i // per, 0, i % per))
    return call(
        body, steps,
        [whole(grad)] + ([whole(extra)] if has_extra else []) + [
            whole(kept["normed_one"]), whole(kept["recip_one"]), whole(kept["normed_two"]),
            whole(kept["recip_two"]), whole(layer.norms), (kept["slope"],) + blocks,
        ] + layer.ffn(layer.up) + layer.ffn(layer.down),
        [
            out_whole((n, depth), LOW), ((2, n, neurons), LOW) + blocks, out_whole((n, depth), LOW),
            out_whole((8, depth), F32), out_group((steps, 1, size), F32),
        ],
        [pltpu.VMEM((n, depth), F32)],
        flops=8 * n * depth * neurons,
    )


def ffn_back_first_call(layer, grad, extra, kept, half):
    n, depth = grad.shape
    steps, _, size = layer.bias_up.shape
    per = steps // 2

    def body(
        grad, extra, normed_two, recip_two, norms, slope, down_one, down_two,
        d_final_low, d_pre, sums, bias_sums,
    ):
        i = pl.program_id(0)

        @pl.when(i == 0)
        def _():
            sums[...] = jnp.zeros_like(sums)
            for at in row_tiles(n):
                value = grad[at, :].astype(F32)
                if at.start >= 2 * half:
                    value = value + extra[at.start - 2 * half : at.stop - 2 * half, :].astype(F32)
                normed = normed_two[at, :].astype(F32)
                back = normalize_back(value, normed, recip_two[at, :], norms[1:2, :])
                d_final_low[at, :] = back.astype(LOW)
                add_rows(sums, 1, value * normed, at)
                add_rows(sums, 5, value, at)
                add_rows(sums, 4, back, at)

        bias = None
        down = joined((down_one, down_two))
        for at in row_tiles(n):
            d_act = dot(d_final_low[at, :], down, 1, 0)
            low = (d_act * slope[0, at, :].astype(F32)).astype(LOW)
            d_pre[0, at, :] = low
            one = jnp.sum(low.astype(F32), axis=0, keepdims=True)
            bias = one if bias is None else bias + one
        bias_sums[0] = bias

    neurons = per * size
    blocks = ((1, n, size), lambda i: (i // per, 0, i % per))
    return call(
        body, steps,
        [
            whole(grad), whole(extra), whole(kept["normed_two"]), whole(kept["recip_two"]),
            whole(layer.norms), (kept["slope"],) + blocks,
        ] + layer.ffn(layer.down),
        [
            out_whole((n, depth), LOW), ((2, n, neurons), LOW) + blocks,
            out_whole((8, depth), F32), out_group((steps, 1, size), F32),
        ],
        [],
        flops=4 * n * depth * neurons,
    )


def ffn_back_second_call(layer, d_final_low, d_pre, kept):
    n, depth = d_final_low.shape
    steps, _, size = layer.bias_up.shape
    per = steps // 2

    def body(d_final, d_pre, normed_one, recip_one, norms, up_one, up_two, d_mid_low, sums, total):
        i = pl.program_id(0)

        @pl.when(i == 0)
        def _():
            total[...] = d_final[...].astype(F32)

        up = joined((up_one, up_two))
        for at in row_tiles(n):
            total[at, :] += dot(d_pre[0, at, :], up, 1, 1)

        @pl.when(i == steps - 1)
        def _():
            sums[...] = jnp.zeros_like(sums)
            for at in row_tiles(n):
                value = total[at, :]
                normed = normed_one[at, :].astype(F32)
                back = normalize_back(value, normed, recip_one[at, :], norms[0:1, :])
                d_mid_low[at, :] = back.astype(LOW)
                add_rows(sums, 0, value * normed, at)
                add_rows(sums, 3, value, at)
                add_rows(sums, 2, back, at)

    blocks = ((1, n, size), lambda i: (i // per, 0, i % per))
    return call(
        body, steps,
        [
            whole(d_final_low), (d_pre,) + blocks, whole(kept["normed_one"]), whole(kept["recip_one"]),
            whole(layer.norms),
        ] + layer.ffn(layer.up),
        [out_whole((n, depth), LOW), out_whole((8, depth), F32)],
        [pltpu.VMEM((n, depth), F32)],
        flops=4 * n * depth * per * size,
    )


def shared_back_call(layer, d_mid_low, kept, segs, half):
    n, depth = d_mid_low.shape
    width, wide, own = layer.width, 3 * layer.width, 2 * half
    count = 2 * len(layer.qkv_blocks)

    def body(d_mid, proj, away, logsum, *refs):
        weights = pairs_of(refs[:count])
        out_one, out_two, segs_q, segs_k, d_proj, d_away, sums, back, mask, total = refs[count:]
        i = pl.program_id(0)
        make_mask(segs_q, segs_k, mask)
        out_cols = joined((out_one, out_two), slice(layer.out_from, layer.out_from + width))
        d_context = dot(d_mid[...], out_cols, 1, 0).astype(LOW)
        attend_back(
            width, [proj.at[0], away.at[0]], mask, logsum.at[0], d_context,
            [d_proj.at[0], d_away.at[0]], sums.at[0],
        )
        part = through_projection(d_away[0], weights, layer.used)

        @pl.when(i == 0)
        def _():
            total[...] = part

        @pl.when(i == 1)
        def _():
            back[...] = (total[...] + part).astype(LOW)

    return call(
        body, 2,
        [
            (d_mid_low, (half, depth), lambda i: (2, 0)), (kept["proj"], (1, half, wide), lambda i: (i, 2, 0)),
            per_group(kept["proj_away"]), per_group(kept["logsum_shared"]),
        ] + layer.qkv() + layer.out() + [whole(segs[None, :half]), whole(segs[:, None])],
        [
            out_group((2, half, wide), LOW), out_group((2, half, wide), LOW), out_group((2, 8, wide), F32),
            out_whole((half, depth), LOW),
        ],
        [pltpu.VMEM((own, half), F32), pltpu.VMEM((half, depth), F32)],
        flops=4 * half * depth * (wide + width) + 20 * own * half * width,
        exps=2 * own * half * width // HEAD_DIM,
    )


def own_back_call(layer, d_mid_low, d_shared, kept, segs, half, with_rows):
    n, depth = d_mid_low.shape
    width, wide, own = layer.width, 3 * layer.width, 2 * half
    count = 2 * len(layer.qkv_blocks) if with_rows else 0

    def body(d_mid_low, d_shared, proj, logsum, out_one, out_two, segs_q, segs_k, *refs):
        i = pl.program_id(0)
        if with_rows:
            d_mid, weights = refs[0], pairs_of(refs[1 : count + 1])
            d_proj, sums, d_rows, mask, total = refs[count + 1 :]
        else:
            d_proj, sums, mask = refs
        make_mask(segs_q, segs_k, mask)
        out_cols = joined((out_one, out_two), slice(layer.out_from, layer.out_from + width))
        d_context = dot(d_mid_low[...], out_cols, 1, 0).astype(LOW)
        attend_back(
            width, [proj.at[0]], mask, logsum.at[0], d_context, [d_proj.at[0, :own]], sums.at[0]
        )
        d_proj[0, own:] = d_shared[0]
        if with_rows:
            part = through_projection(d_proj[0], weights, layer.used)

            @pl.when(i == 0)
            def _():
                total[...] = d_mid[...].astype(F32) + part

            @pl.when(i == 1)
            def _():
                d_rows[...] = (total[...] + part).astype(LOW)

    return call(
        body, 2,
        [
            (d_mid_low, (own, depth), lambda i: (0, 0)), per_group(d_shared),
            (kept["proj"], (1, own, wide), lambda i: (i, 0, 0)), per_group(kept["logsum_own"]),
        ] + layer.out() + [whole(segs[None, :]), whole(segs[:, None])]
        + ([whole(d_mid_low)] + layer.qkv() if with_rows else []),
        [out_group((2, n, wide), LOW), out_group((2, 8, wide), F32)]
        + ([out_whole((n, depth), LOW)] if with_rows else []),
        [pltpu.VMEM((own, own), F32)] + ([pltpu.VMEM((n, depth), F32)] if with_rows else []),
        flops=4 * depth * (n * wide * with_rows + own * width) + 20 * own * own * width,
        exps=2 * own * own * width // HEAD_DIM,
    )


def rows_back_call(layer, d_mid_low, d_proj):
    n, depth = d_mid_low.shape
    wide = 3 * layer.width

    def body(d_mid, d_proj, *refs):
        weights, d_rows = pairs_of(refs[:-1]), refs[-1]

        @pl.when(pl.program_id(0) == 0)
        def _():
            d_rows[...] = d_mid[...].astype(F32)

        d_rows[...] += through_projection(d_proj[0], weights, layer.used)

    return call(
        body, 2, [whole(d_mid_low), per_group(d_proj)] + layer.qkv(), [out_whole((n, depth), F32)], [],
        flops=4 * depth * n * wide,
    )[0]


class Grads:
    def __init__(self, entries, columns, cut):
        self.entries, self.columns, self.cut = entries, columns, cut
        sizes = [end - start for _, start, end in columns]
        self.size_a, self.size_b = sum(sizes[:cut]), sum(sizes[cut:])

    def inputs(self, at, side):
        out = []
        for pairs in self.entries:
            for left, right in pairs:
                half = (left.shape[0], left.shape[1] // 2)
                out += [(left, half, lambda i: (0, side)), per_group(right, at)]
        return out

    def flops(self, rows):
        return sum(
            4 * rows * left.shape[0] * right.shape[2] for pairs in self.entries for left, right in pairs
        )

    def product(self, refs, entry, start, end):
        first = sum(len(pairs) for pairs in self.entries[:entry])
        total = None
        for at in range(first, first + len(self.entries[entry])):
            one = dot(refs[2 * at][...], refs[2 * at + 1][0, :, start:end], 0, 0)
            total = one if total is None else total + one
        return total

    def send(self):
        rows = self.entries[0][0][0].shape[1] // 2
        size = self.size_a + self.size_b

        def body(*refs):
            col = 0
            for entry, start, end in self.columns:
                part = self.product(refs, entry, start, end)
                refs[-1][0, :, col : col + end - start] = part.astype(LOW)
                col += end - start

        return call(
            body, 2, self.inputs(lambda i: i, 1), [out_group((2, rows, size), LOW)], [], self.flops(rows)
        )[0]

    def keep(self, got):
        rows = self.entries[0][0][0].shape[1] // 2
        half = rows // 2

        def body(got, *refs):
            send_a, keep_a, send_b, keep_b = refs[-4:]
            i = pl.program_id(0)
            col = 0
            for at, (entry, start, end) in enumerate(self.columns):
                part = self.product(refs, entry, start, end)
                part = part + got[0, :, col : col + end - start].astype(F32)
                if at < self.cut:
                    place = slice(col, col + end - start)

                    @pl.when(i == 0)
                    def _():
                        send_a[:, place] = part.astype(LOW)

                    @pl.when(i == 1)
                    def _():
                        keep_a[:, place] = part
                else:
                    place = slice(col - self.size_a, col - self.size_a + end - start)
                    keep_b[0, :, place] = part[:half]
                    send_b[0, :, place] = part[half:].astype(LOW)
                col += end - start

        return call(
            body, 2,
            [per_group(got, lambda i: 1 - i)] + self.inputs(lambda i: 1 - i, 0),
            [
                out_whole((rows, self.size_a), LOW), out_whole((rows, self.size_a), F32),
                out_group((2, half, self.size_b), LOW), out_group((2, half, self.size_b), F32),
            ],
            [], self.flops(rows),
        )


class Reduce:
    def __init__(self, grads):
        self.grads = grads
        self.sends = (grads.send(),)
        self.got = (swap_core(self.sends[0]),)
        self.work = self._run()

    def _run(self):
        count = lax.axis_size("dp") // 4
        send_a, keep_a, send_b, keep_b = self.grads.keep(self.got[0])
        fourth = keep_a.shape[0] // 2
        self.sends = (send_a, send_b)
        self.got = (swap_y(send_a), swap_x(send_b))
        yield
        a = keep_a + self.got[0].astype(F32)
        b = keep_b + self.got[1].astype(F32)
        self.sends = (a[fourth:].astype(LOW), b[0].astype(LOW))
        self.got = (swap_x(self.sends[0]), swap_y(self.sends[1]))
        a, b = a[:fourth], b[1]
        yield
        both = jnp.concatenate([a + self.got[0].astype(F32), b + self.got[1].astype(F32)], axis=1)
        both = both.reshape((count, -1) + both.shape[1:])
        self.sends = tuple(both[back].astype(LOW) for back in range(1, count))
        self.got = tuple(ring_shift(send, -back) for back, send in enumerate(self.sends, 1))
        yield
        total = both[0] + sum(got.astype(F32) for got in self.got)
        self.total = total
        self.got = self.sends = ()

    def step(self):
        next(self.work, None)


class Total:
    def __init__(self, value):
        self.total = value
        self.work = self._run()
        self.step()

    def _run(self):
        n = lax.axis_size("dp")
        self.sends = (self.total,)
        self.got = (swap_y(self.total),)
        yield
        self.total = self.total + self.got[0]
        step = 1
        while step < n:
            self.sends = (self.total,)
            self.got = (lax.ppermute(self.total, "dp", [(i, i ^ step) for i in range(n)]),)
            yield
            self.total = self.total + self.got[0]
            step *= 2
        self.got = self.sends = ()

    def step(self):
        next(self.work, None)


def round_of(*works):
    ended = lax.optimization_barrier(tuple(work.got for work in works))
    for work, got in zip(works, ended):
        work.got = got
    for work in works:
        work.step()


def before(value, *works):
    value, ended = lax.optimization_barrier((value, tuple(work.got for work in works)))
    for work, got in zip(works, ended):
        work.got = got
    return value


def forward_attn(layer, rows, proj, context_own, logsum_own, rows_low, away_low, segs, half):
    proj_away, context, logsum_shared, hidden_low, normed_one, recip_one = shared_call(
        layer, rows, proj, away_low, context_own, segs[1], half
    )
    kept = dict(
        rows_low=rows_low, away_low=away_low, proj=proj, proj_away=proj_away, context=context,
        logsum_own=logsum_own, logsum_shared=logsum_shared, hidden_low=hidden_low,
        normed_one=normed_one, recip_one=recip_one,
    )
    return hidden_low, kept


def forward_ffn(layer, hidden_low, kept, wide):
    act, slope, output, normed_two, recip_two = ffn_call(layer, hidden_low, wide)
    kept.update(act=act, slope=slope, normed_two=normed_two, recip_two=recip_two)
    return output


def backward_ffn(layer, grad, extra, kept, half):
    d_final_low, d_pre, d_mid_low, sums, bias_sums = ffn_back_call(layer, grad, extra, kept, half)
    entries = [[(kept["hidden_low"], d_pre)], [(d_final_low, kept["act"])]]
    return d_mid_low, sums[:6], bias_sums, entries


def attn_entries(kept, d_proj, d_away, d_mid_low):
    return [[(kept["rows_low"], d_proj), (kept["away_low"], d_away)], [(d_mid_low, kept["context"])]]


def on_device(
    tokens, segment_ids, out_grad,
    t_qkv, t_qv_bias, t_out, t_up, t_up_bias, t_down, t_gains, t_shifts,
    s_qkv, s_qv_bias, s_out, s_up, s_up_bias, s_down, s_gains, s_shifts,
):
    rows, half, width = tokens.shape
    first = lax.axis_index("mp") == 0
    own_row = lambda value: jnp.where(first, value[0], value[2])
    far_row = lambda value: jnp.where(first, value[2], value[0])

    norm_rows = jnp.concatenate([t_gains, t_shifts, s_gains, s_shifts], axis=0)
    norm_rows = jnp.pad(norm_rows, ((0, 128 - norm_rows.shape[0]), (0, 0)))
    t_width, s_width = t_qkv.shape[2], s_qkv.shape[2]
    size = s_up.shape[1]
    per = t_up.shape[1] // size
    count, block = lax.axis_size("dp") // 4, t_up.shape[0]
    together = lambda *values: lax.optimization_barrier(values)
    every = slice(None)

    def columns(start, width):
        return slice(start, start + width)

    t_cut, t_all = 2 * t_width, 4 * t_width + 128
    f_cut = per * size
    s_cut = size + 2 * s_width
    packed_t = moves(
        [t_qkv, t_out.T, norm_rows.T], [(block, t_all)],
        [(0, (i,), 0, (every, columns(i * t_width, t_width))) for i in range(3)]
        + [
            (1, (every,), 0, (every, columns(3 * t_width, t_width))),
            (2, (every,), 0, (every, columns(4 * t_width, 128))),
        ],
    )[0]
    packed_f, student_a, student_b = moves(
        [t_up, t_down.T, s_up, s_qkv, s_out.T, s_down.T],
        [(block, 2 * f_cut), (block, s_cut), (block, s_cut)],
        [
            (0, (every,), 0, (every, columns(0, f_cut))), (1, (every,), 0, (every, columns(f_cut, f_cut))),
            (2, (every,), 1, (every, columns(0, size))), (3, (0,), 1, (every, columns(size, s_width))),
            (4, (every,), 1, (every, columns(size + s_width, s_width))),
            (5, (every,), 2, (every, columns(0, size))), (3, (1,), 2, (every, columns(size, s_width))),
            (3, (2,), 2, (every, columns(size + s_width, s_width))),
        ],
    )

    def along_z(value):
        return [value] + [ring_shift(value, at) for at in range(1, count)]

    def of_line(pieces, cut):
        rest = pieces[0].shape[1] - cut
        return moves(
            pieces, [(count, block, cut), (count, block, rest)],
            [(i, (every, columns(start, wide)), at, (i,)) for i in range(count)
             for at, (start, wide) in enumerate(((0, cut), (cut, rest)))],
        )

    def first_plane(a, got_a, b, got_b):
        return moves(
            [a, got_a, b, got_b], [(2,) + a.shape, (2,) + b.shape],
            [(0, (every,), 0, (0,)), (1, (every,), 0, (1,)), (2, (every,), 1, (0,)), (3, (every,), 1, (1,))],
        )

    def both_planes(a, got_a, b, got_b, order):
        copies, col = [], 0
        for of_b, start, wide in order:
            taken, place = (every, every, every, columns(start, wide)), (every, every, columns(col, wide))
            if of_b:
                copies += [(2, taken, 0, (every, 0) + place), (3, taken, 0, (every, 1) + place)]
            else:
                copies += [(0, taken, 0, (0, every) + place), (1, taken, 0, (1, every) + place)]
            col += wide
        out = moves([a, got_a, b, got_b], [(2, 2, count, block, col)], copies)[0]
        return out.reshape(2, width // 2, col)

    def with_core(own):
        return own, swap_core(own)

    bias_parts = [t_qv_bias[0], t_qv_bias[1], t_up_bias, s_qv_bias[0], s_qv_bias[1], s_up_bias]
    to_own = feature_order(width)
    into = (lax.iota(jnp.int32, width)[:, None] == to_own[None, :]).astype(LOW)
    def reorder(value):
        return jnp.dot(value, into, preferred_element_type=F32).astype(LOW)


    spin = lambda segs: jnp.where(first, segs, jnp.roll(segs, half))
    segs = (spin(own_row(segment_ids)), spin(segment_ids[1]))

    line_t, got_own = along_z(packed_t), swap_y(far_row(tokens))
    *line_t, got_own, into, segs, packed_f, student_a, student_b = together(
        *line_t, got_own, into, segs, packed_f, student_a, student_b
    )
    attn_a, attn_b = of_line(line_t, t_cut)
    got_a, got_b = swap_x(attn_a), swap_y(attn_b)
    line_f = along_z(packed_f)
    student_x, student_y = swap_x(student_a), swap_y(student_b)
    got_a, got_b, student_x, student_y, line_f[1] = together(got_a, got_b, student_x, student_y, line_f[1])
    inputs = reorder(jnp.concatenate([own_row(tokens), got_own, tokens[1]], axis=0))
    attn_a, attn_b = first_plane(attn_a, got_a, attn_b, got_b)
    got_a, got_b = swap_y(attn_a), swap_x(attn_b)
    line_s = along_z(moves(
        [student_a, student_x, student_b, student_y], [(2, block, 2 * s_cut)],
        [(i, (every,), 0, (i % 2, every, columns(i // 2 * s_cut, s_cut))) for i in range(4)],
    )[0])
    got_a, got_b, inputs, *line_f[2:] = together(got_a, got_b, inputs, *line_f[2:])
    attn = both_planes(
        attn_a, got_a, attn_b, got_b, [(False, 0, t_cut), (True, 0, t_all - t_cut)]
    )
    attn = with_core(attn)
    ffn_a, ffn_b = of_line(list(after(line_f, attn[0])), f_cut)
    got_a, got_b = swap_x(ffn_a), swap_y(ffn_b)
    bias_own = jnp.concatenate(bias_parts)
    bias_far = swap_y(bias_own)
    attn, got_a, got_b, bias_far = together(attn, got_a, got_b, bias_far)
    ffn_a, ffn_b = first_plane(ffn_a, got_a, ffn_b, got_b)
    got_a, got_b = swap_y(ffn_a), swap_x(ffn_b)
    got_shared = swap_y(tokens[1])
    norms = jnp.concatenate([half[0, :, -128:-116] for half in attn], axis=0).T.astype(F32)
    norms_of = lambda at: jnp.pad(norms[at : at + 6], ((0, 2), (0, 0)))
    bias_all = jnp.stack([bias_own, bias_far]).astype(F32)
    cuts = [0]
    for part in bias_parts:
        cuts.append(cuts[-1] + part.shape[0])
    pick = [bias_all[:, cuts[i] : cuts[i + 1]] for i in range(6)]
    bias_qkv = lambda q, v: jnp.concatenate([q, jnp.zeros_like(q), v], axis=1)[:, None, :]
    teacher = Layer(
        t_width, None, None, [(attn, t_width, i, t_width) for i in range(3)], (attn, t_width, 3, t_width), 0,
        norms_of(0), bias_qkv(pick[0], pick[1]), pick[2].reshape(2 * per, 1, size),
    )

    grad_in = jnp.concatenate([own_row(out_grad), swap_y(far_row(out_grad)), out_grad[1]], axis=0)

    inputs, ffn_a, ffn_b = together(inputs, ffn_a, ffn_b)
    proj, context_own, logsum_own = project_call(teacher, inputs, segs[0], half)
    proj, got_shared, *line_s[1:-1] = together(proj, got_shared, *line_s[1:-1])
    away_low = reorder(got_shared)
    hidden, t_kept = forward_attn(
        teacher, inputs, proj, context_own, logsum_own, inputs, away_low, segs, half
    )
    hidden, got_a, got_b, line_s[-1] = together(hidden, got_a, got_b, line_s[-1])
    ffn = both_planes(ffn_a, got_a, ffn_b, got_b, [(False, 0, f_cut), (True, 0, f_cut)])
    ffn = with_core(ffn)
    student_a, student_b = moves(
        line_s, [(2, count, block, s_cut)] * 2,
        [(i, (every, every, columns(at * s_cut, s_cut)), at, (every, i)) for i in range(count) for at in range(2)],
    )
    got_a, got_b = swap_y(student_a), swap_x(student_b)
    hidden, ffn = together(hidden, ffn)
    teacher.up, teacher.down = (ffn, 0), (ffn, per)
    middle_low = forward_ffn(teacher, hidden, t_kept, False)
    away_low = swap_y(middle_low[2 * half :])
    middle_low, got_a, got_b, grad_in = together(middle_low, got_a, got_b, grad_in)
    grad_in = reorder(grad_in)
    student_w = with_core(both_planes(
        student_a, got_a, student_b, got_b,
        [(False, 0, size), (True, 0, size), (False, size, 2 * s_width), (True, size, 2 * s_width)],
    ))
    narrow = 2 * s_width
    place = 2 * size // narrow
    student = Layer(
        s_width, (student_w, 0), (student_w, 1),
        [(student_w, narrow, place, s_width), (student_w, narrow, place + 1, narrow)],
        (student_w, narrow, place, s_width), s_width, norms_of(6), bias_qkv(pick[3], pick[4]),
        pick[5].reshape(2, 1, size),
    )
    proj, context_own, logsum_own = project_call(student, middle_low, segs[0], half)
    proj, away_low = together(proj, away_low)
    hidden, s_kept = forward_attn(
        student, middle_low, proj, context_own, logsum_own, middle_low, away_low, segs, half
    )
    last = forward_ffn(student, hidden, s_kept, True)

    def far_half(value):
        return swap_y(value[half : 2 * half].astype(LOW))

    def to_rows(value, far):
        near = jnp.concatenate([value[:half], value[2 * half :]], axis=0)
        high = near.astype(LOW)
        low = (near - high.astype(F32)).astype(LOW)
        back = lambda part: jnp.einsum("nr,dr->nd", part, into, preferred_element_type=F32)
        near, far = back(high) + back(low), back(far)
        return jnp.stack([jnp.where(first, near[:half], far), near[half:], jnp.where(first, far, near[:half])])

    far_last = far_half(last)

    d_mid_low, s_norm_grads, s_up_grad, s_entries = backward_ffn(student, grad_in, None, s_kept, half)
    d_shared, d_away, s_sums_b, back = shared_back_call(student, d_mid_low, s_kept, segs[1], half)
    extra = swap_y(back)
    d_shared, far_last = together(d_shared, far_last)
    d_proj, s_sums_a, d_rows = own_back_call(
        student, d_mid_low, d_shared, s_kept, segs[0], half, True
    )
    d_proj, extra = lax.optimization_barrier((d_proj, extra))
    s_entries += attn_entries(s_kept, d_proj, d_away, d_mid_low)
    s_columns = [(0, 0, size), (2, 0, s_width), (3, 0, s_width), (1, 0, size), (2, s_width, 3 * s_width)]
    reduce_s = Reduce(Grads(s_entries, s_columns, 3))

    d_rows = after(d_rows, reduce_s.sends)
    d_final_low, d_pre, t_sums_two, t_up_grad = ffn_back_first_call(
        teacher, d_rows, extra, t_kept, half
    )
    d_pre = before(d_pre, reduce_s)
    reduce_s.step()
    d_pre = after(d_pre, reduce_s.sends)
    f_entries = [[(t_kept["hidden_low"], d_pre)], [(d_final_low, t_kept["act"])]]
    reduce_f = Reduce(Grads(f_entries, [(0, 0, per * size), (1, 0, per * size)], 1))
    d_pre = after(d_pre, reduce_f.sends)
    d_mid_low, t_sums_one = ffn_back_second_call(teacher, d_final_low, d_pre, t_kept)
    t_norm_grads = (t_sums_one + t_sums_two)[:6]
    d_mid_low = before(d_mid_low, reduce_f)
    reduce_f.step()
    reduce_s.got = after(reduce_s.got, reduce_f.sends)
    d_mid_low = before(d_mid_low, reduce_s)
    reduce_s.step()
    d_mid_low = after(d_mid_low, reduce_s.sends)
    d_shared, d_away, t_sums_b, back = shared_back_call(teacher, d_mid_low, t_kept, segs[1], half)
    extra = swap_y(back)
    d_shared = before(d_shared, reduce_s)
    reduce_s.step()
    d_shared = after(d_shared, reduce_s.sends)
    d_proj, t_sums_a = own_back_call(teacher, d_mid_low, d_shared, t_kept, segs[0], half, False)
    t_entries = attn_entries(t_kept, d_proj, d_away, d_mid_low)
    reduce_t = Reduce(
        Grads(t_entries, [(0, 0, 2 * t_width), (0, 2 * t_width, 3 * t_width), (1, 0, t_width)], 1)
    )

    def qv_grad(one, two, wide):
        sums = one[:, 0] + two[:, 0]
        sums = jnp.concatenate([sums[:, :wide], sums[:, 2 * wide :]], axis=1)
        return jnp.pad(sums, ((0, 0), (0, width - 2 * wide)))

    norm_grads = jnp.concatenate([t_norm_grads, s_norm_grads], axis=0)
    norm_grads = jnp.einsum("nr,dr->nd", norm_grads, into.astype(F32), precision=lax.Precision.HIGHEST)
    qv_t, qv_s = qv_grad(t_sums_a, t_sums_b, t_width), qv_grad(s_sums_a, s_sums_b, s_width)
    mine = jnp.concatenate([t_up_grad[:per, 0], s_up_grad[:1, 0], qv_t[:1], qv_s[:1]], axis=0)
    other = jnp.concatenate([t_up_grad[per:, 0], s_up_grad[1:, 0], qv_t[1:], qv_s[1:]], axis=0)
    small = Total(jnp.concatenate(
        [norm_grads, jnp.where(first, mine, other), jnp.where(first, other, mine)], axis=0
    ))
    reduce_f.got = after(reduce_f.got, reduce_t.sends)
    round_of(reduce_f, small)
    reduce_t.got = after(reduce_t.got, reduce_f.sends)
    reduce_t.step()
    reduce_f.got = after(reduce_f.got, reduce_t.sends)
    round_of(reduce_f, reduce_s, small)
    d_rows = rows_back_call(teacher, *after((d_mid_low, d_proj), reduce_t.sends))
    reduce_t.got = after(reduce_t.got, d_rows)
    far_rows = far_half(d_rows)
    round_of(reduce_t, small)
    d_rows, last = after((d_rows, last), reduce_t.sends)
    d_rows = jnp.concatenate([d_rows[: 2 * half], d_rows[2 * half :] + extra.astype(F32)], axis=0)
    input_grad, output = to_rows(d_rows, far_rows), to_rows(last, far_last)
    round_of(reduce_t, reduce_f, small)
    round_of(reduce_t, small)
    for work in (reduce_f, reduce_s, small):
        while work.got:
            work.step()
    s_sum, f_sum, small = reduce_s.total, reduce_f.total, small.total

    piece = width // lax.axis_size("dp")
    norm_sum = lax.dynamic_slice_in_dim(small[:12], lax.axis_index("dp") * piece, piece, 1)
    bias_sum = small[12:].reshape(2, -1, width)
    bias_sum = jnp.where(first, bias_sum[0], bias_sum[1])
    t_qv_sum, s_qv_sum = bias_sum[per + 1], bias_sum[per + 2, : 2 * s_width]

    def cut(value, *sizes):
        out = []
        for one in sizes:
            out.append(value[:, :one])
            value = value[:, one:]
        return out

    t_up_sum, t_down_sum = cut(f_sum, per * size, per * size)
    s_up_sum, sq, so, s_down_sum, sk, sv = cut(s_sum, size, s_width, s_width, size, s_width, s_width)
    done = (
        output, input_grad, t_qv_sum.reshape(2, -1), t_up_sum, bias_sum[:per].reshape(-1), t_down_sum.T,
        norm_sum[0:2], norm_sum[2:6], jnp.stack([sq, sk, sv]), s_qv_sum.reshape(2, -1), so.T, s_up_sum,
        bias_sum[per], s_down_sum.T, norm_sum[6:8], norm_sum[8:12],
    )
    done, reduce_t.got = together(done, reduce_t.got)
    while reduce_t.got:
        reduce_t.step()
    tq, tk, tv, to = cut(reduce_t.total, t_width, t_width, t_width, t_width)
    return done[:2] + (jnp.stack([tq, tk, tv]), done[2], to.T) + done[3:]


def solution(mesh):
    layer = (
        P(None, "dp", "mp"), P(None, "mp"), P("mp", "dp"), P("dp", "mp"), P("mp"), P("mp", "dp"),
        P(None, "dp"), P(None, "dp"),
    )
    rows = P("dp", "mp", None)
    return jax.shard_map(
        on_device,
        mesh=mesh,
        in_specs=(rows, P("dp", None), rows) + layer + layer,
        out_specs=(rows, rows) + layer + layer,
        check_vma=False,
    )
```

```python
import functools
import math

import jax
import jax.numpy as jnp
from jax import lax
from jax.experimental import pallas as pl
from jax.experimental.pallas import tpu as pltpu
from jax.sharding import PartitionSpec as P

HEAD_DIM = 64
LOW = jnp.bfloat16
F32 = jnp.float32


def ring_of(count):
    return list(range(0, count, 2)) + list(range(1, count, 2))[::-1]


def swap_y(value):
    return lax.ppermute(value, "mp", [(0, 1), (1, 0)])


def swap_x(value):
    n = lax.axis_size("dp")
    return lax.ppermute(value, "dp", [(i, i ^ 2) for i in range(n)])


def swap_core(value):
    n = lax.axis_size("dp")
    return lax.ppermute(value, "dp", [(i, i ^ 1) for i in range(n)])


def ring_shift(value, step):
    count = lax.axis_size("dp") // 4
    ring = ring_of(count)
    pairs = []
    for place in range(count):
        for low in range(4):
            pairs.append((ring[place] * 4 + low, ring[(place + step) % count] * 4 + low))
    return lax.ppermute(value, "dp", pairs)


def feature_order(width):
    n = lax.axis_size("dp")
    count, rows = n // 4, width // n
    me = lax.axis_index("dp")
    z, x, core = me // 4, (me // 2) % 2, me % 2
    place = jnp.where(z % 2 == 0, z // 2, count - 1 - z // 2)
    at = lax.iota(jnp.int32, width)
    row = at % rows
    back = (at // rows) % count
    x_rel = (at // (rows * count)) % 2
    core_rel = at // (rows * count * 2)
    from_place = (place - back + count) % count
    half = (count + 1) // 2
    z_abs = jnp.where(from_place < half, 2 * from_place, 2 * (count - 1 - from_place) + 1)
    block = z_abs * 4 + (x ^ x_rel) * 2 + (core ^ core_rel)
    return block * rows + row


def after(value, *others):
    return lax.optimization_barrier((value, others))[0]


VMEM_BYTES = 26 << 20
TILE = 256


def dot(left, right, left_at, right_at):
    return lax.dot_general(
        left, right, (((left_at,), (right_at,)), ((), ())), preferred_element_type=F32
    )


def call(body, steps, inputs, outputs, scratch, flops, exps=0):
    size = lambda shape, dtype: math.prod(shape) * jnp.dtype(dtype).itemsize
    moved = sum(size(array.shape, array.dtype) for array, _, _ in inputs)
    moved += sum(size(shape, dtype) for shape, dtype, _, _ in outputs)
    return pl.pallas_call(
        body,
        grid=(steps,),
        in_specs=[pl.BlockSpec(block, index) for _, block, index in inputs],
        out_specs=[pl.BlockSpec(block, index) for _, _, block, index in outputs],
        out_shape=[jax.ShapeDtypeStruct(shape, dtype) for shape, dtype, _, _ in outputs],
        scratch_shapes=scratch,
        compiler_params=pltpu.CompilerParams(
            dimension_semantics=("arbitrary",), vmem_limit_bytes=VMEM_BYTES
        ),
        cost_estimate=pl.CostEstimate(
            flops=flops // 2, bytes_accessed=moved // 2, transcendentals=exps // 2
        ),
    )(*[array for array, _, _ in inputs])


def moves(arrays, shapes, copies):
    def body(*refs):
        for source, taken, target, place in copies:
            refs[len(arrays) + target][place] = refs[source][taken]

    moved = 2 * sum(math.prod(shape) for shape in shapes)
    return pl.pallas_call(
        body,
        out_shape=[jax.ShapeDtypeStruct(shape, LOW) for shape in shapes],
        compiler_params=pltpu.CompilerParams(vmem_limit_bytes=VMEM_BYTES),
        cost_estimate=pl.CostEstimate(flops=0, bytes_accessed=moved, transcendentals=0),
    )(*arrays)


def whole(array):
    rank = array.ndim
    return (array, array.shape, lambda i: (0,) * rank)


def per_group(array, at=lambda i: i):
    return (array, (1,) + array.shape[1:], lambda i: (at(i),) + (0,) * (array.ndim - 1))


def out_whole(shape, dtype):
    return (shape, dtype, shape, lambda i: (0,) * len(shape))


def out_group(shape, dtype, at=lambda i: i):
    return (shape, dtype, (1,) + shape[1:], lambda i: (at(i),) + (0,) * (len(shape) - 1))


class Layer:
    def __init__(self, width, up, down, qkv, out, out_from, norms, bias_qkv, bias_up):
        self.width, self.up, self.down = width, up, down
        self.qkv_blocks, self.out_block, self.out_from = qkv, out, out_from
        self.norms, self.bias_qkv, self.bias_up = norms, bias_qkv, bias_up
        self.used = [block[3] for block in qkv]

    def columns(self, block, at):
        pair, size, place, _ = block
        return [(half, (1, half.shape[1], size), lambda i: (at(i), 0, place)) for half in pair]

    def qkv(self, at=lambda i: i):
        return [one for block in self.qkv_blocks for one in self.columns(block, at)]

    def out(self, at=lambda i: i):
        return self.columns(self.out_block, at)

    def ffn(self, where):
        pair, base = where
        size, per = self.bias_up.shape[2], self.bias_up.shape[0] // 2
        return [(half, (1, half.shape[1], size), lambda i: (i // per, 0, base + i % per)) for half in pair]


def joined(pair, cols=slice(None)):
    return jnp.concatenate([half[0, :, cols] for half in pair], axis=0)


def pairs_of(refs):
    return [refs[at : at + 2] for at in range(0, len(refs), 2)]


def put_projection(rows, weights, used, bias, target):
    start = 0
    for weight, cols in zip(weights, used):
        part = dot(rows, joined(weight, slice(0, cols)), 1, 0) + bias[0, :, start : start + cols]
        target[:, start : start + cols] = part.astype(LOW)
        start += cols


def through_projection(grads, weights, used):
    start = 0
    total = None
    for weight, cols in zip(weights, used):
        part = dot(grads[:, start : start + cols], joined(weight, slice(0, cols)), 1, 1)
        total = part if total is None else total + part
        start += cols
    return total


def head_at(width, part, head):
    return slice(part * width + head * HEAD_DIM, part * width + (head + 1) * HEAD_DIM)


def join(parts, cols):
    picked = [part[:, cols] for part in parts]
    return picked[0] if len(picked) == 1 else jnp.concatenate(picked, axis=0)


def attend(width, kept, mask, logsum):
    scale = jnp.asarray(HEAD_DIM**-0.5, LOW)
    out = []
    for head in range(width // HEAD_DIM):
        query = kept[0][:, head_at(width, 0, head)] * scale
        scores = dot(join(kept, head_at(width, 1, head)), query, 1, 1) + mask[...]
        top = jnp.max(scores, axis=0, keepdims=True)
        expo = jnp.exp(scores - top)
        total = jnp.sum(expo, axis=0, keepdims=True)
        out.append(dot(join(kept, head_at(width, 2, head)), expo.astype(LOW), 0, 0) * (1.0 / total))
        logsum[head : head + 1, :] = top + jnp.log(total)
    return jnp.concatenate(out, axis=0).T.astype(LOW)


def attend_back(width, kept, mask, logsum, d_context, grads, sums):
    scale = jnp.asarray(HEAD_DIM**-0.5, LOW)
    for head in range(width // HEAD_DIM):
        at_q, at_k, at_v = (head_at(width, part, head) for part in range(3))
        query = kept[0][:, at_q] * scale
        keys = join(kept, at_k)
        d_ctx = d_context[:, head * HEAD_DIM : (head + 1) * HEAD_DIM]
        probs = jnp.exp(dot(keys, query, 1, 1) + mask[...] - logsum[head : head + 1, :])
        d_probs = dot(join(kept, at_v), d_ctx, 1, 1)
        both = probs * d_probs
        inner = jnp.sum(both, axis=0, keepdims=True)
        d_scores = (both - probs * inner).astype(LOW)
        d_values = dot(probs.astype(LOW), d_ctx, 1, 0).astype(LOW)
        d_keys = dot(d_scores, query, 1, 0).astype(LOW)
        d_query = dot(keys * scale, d_scores, 0, 0).T.astype(LOW)
        grads[0][:, at_q] = d_query
        start = 0
        for grad in grads:
            rows = grad.shape[0]
            grad[:, at_k] = d_keys[start : start + rows]
            grad[:, at_v] = d_values[start : start + rows]
            start += rows
        for grad in grads[1:]:
            grad[:, at_q] = jnp.zeros((grad.shape[0], HEAD_DIM), LOW)
        sums[0:1, at_q] = jnp.sum(d_query.astype(F32), axis=0, keepdims=True)
        sums[0:1, at_k] = jnp.zeros((1, HEAD_DIM), F32)
        sums[0:1, at_v] = jnp.sum(d_values.astype(F32), axis=0, keepdims=True)


def make_mask(segs_q, segs_k, mask):
    @pl.when(pl.program_id(0) == 0)
    def _():
        mask[...] = jnp.where(segs_k[...] == segs_q[...], 0.0, -1e9)


def normalize(value, gain, shift):
    center = value - jnp.mean(value, axis=-1, keepdims=True)
    recip = lax.rsqrt(jnp.mean(center * center, axis=-1, keepdims=True) + 1e-06)
    normed = center * recip
    return normed * gain + shift, normed, recip


def normalize_back(grad, normed, recip, gain):
    scaled = grad * gain
    mean_one = jnp.mean(scaled, axis=-1, keepdims=True)
    mean_two = jnp.mean(scaled * normed, axis=-1, keepdims=True)
    return recip * (scaled - mean_one - normed * mean_two)


def row_tiles(rows):
    return [slice(start, start + TILE) for start in range(0, rows, TILE)]


def project_call(layer, rows_low, segs, half):
    n, depth = rows_low.shape
    width, wide, own = layer.width, 3 * layer.width, 2 * half
    count = 2 * len(layer.qkv_blocks)

    def body(rows, *refs):
        weights = pairs_of(refs[:count])
        bias, segs_q, segs_k, proj, context, logsum, mask = refs[count:]
        make_mask(segs_q, segs_k, mask)
        put_projection(rows[...], weights, layer.used, bias, proj.at[0])
        context[0] = attend(width, [proj.at[0, :own]], mask, logsum.at[0])

    return call(
        body, 2,
        [whole(rows_low)] + layer.qkv() + [
            per_group(layer.bias_qkv), whole(segs[None, :]), whole(segs[:, None])
        ],
        [
            out_group((2, n, wide), LOW), out_group((2, own, width), LOW), out_group((2, 8, own), F32),
        ],
        [pltpu.VMEM((own, own), F32)],
        flops=4 * n * depth * wide + 8 * own * own * width,
        exps=2 * own * own * width // HEAD_DIM,
    )


def shared_call(layer, rows, proj, away_low, context_own, segs, half):
    n, depth = rows.shape
    width, wide, own = layer.width, 3 * layer.width, 2 * half
    count = 2 * len(layer.qkv_blocks)

    def body(rows, proj, away, *refs):
        weights = pairs_of(refs[:count])
        (
            out_one, out_two, bias, segs_q, segs_k, context_own, norms,
            proj_away, context, logsum, hidden_low, normed_one, recip_one, mask, total,
        ) = refs[count:]
        i = pl.program_id(0)
        make_mask(segs_q, segs_k, mask)
        put_projection(away[...], weights, layer.used, bias, proj_away.at[0])
        context[0, :own] = context_own[0]
        context[0, own:] = attend(width, [proj.at[0], proj_away.at[0]], mask, logsum.at[0])
        out_cols = joined((out_one, out_two), slice(layer.out_from, layer.out_from + width))

        @pl.when(i == 0)
        def _():
            total[...] = dot(context[0], out_cols, 1, 1)

        @pl.when(i == 1)
        def _():
            for at in row_tiles(n):
                value = rows[at, :].astype(F32) + norms[2:3, :]
                value = value + (total[at, :] + dot(context[0, at], out_cols, 1, 1))
                value, normed, recip = normalize(value, norms[0:1, :], norms[3:4, :])
                hidden_low[at, :] = value.astype(LOW)
                normed_one[at, :] = normed.astype(LOW)
                recip_one[at, :] = recip

    return call(
        body, 2,
        [
            whole(rows), (proj, (1, half, wide), lambda i: (i, 2, 0)), whole(away_low),
        ] + layer.qkv() + layer.out() + [
            per_group(layer.bias_qkv), whole(segs[None, :half]),
            whole(segs[:, None]), per_group(context_own), whole(layer.norms),
        ],
        [
            out_group((2, half, wide), LOW), out_group((2, n, width), LOW), out_group((2, 8, half), F32),
            out_whole((n, depth), LOW), out_whole((n, depth), LOW), out_whole((n, 1), F32),
        ],
        [pltpu.VMEM((own, half), F32), pltpu.VMEM((n, depth), F32)],
        flops=4 * depth * (n * width + half * wide) + 8 * own * half * width,
        exps=2 * own * half * width // HEAD_DIM,
    )


def ffn_call(layer, hidden_low, wide):
    n, depth = hidden_low.shape
    steps, _, size = layer.bias_up.shape
    per = steps // 2

    def body(
        hidden_low, norms, bias_up, up_one, up_two, down_one, down_two,
        act, slope, output, normed_two, recip_two, total,
    ):
        i = pl.program_id(0)

        @pl.when(i == 0)
        def _():
            total[...] = hidden_low[...].astype(F32) + norms[4:5, :]

        up, down = joined((up_one, up_two)), joined((down_one, down_two))
        for at in row_tiles(n):
            pre = dot(hidden_low[at, :], up, 1, 0) + bias_up[0]
            bell = 0.5 + 0.5 * lax.erf(pre * math.sqrt(0.5))
            low = (pre * bell).astype(LOW)
            act[0, at, :] = low
            slope[0, at, :] = (
                bell + pre * (jnp.exp(-0.5 * pre * pre) * (1.0 / math.sqrt(2.0 * math.pi)))
            ).astype(LOW)
            total[at, :] += dot(low, down, 1, 1)

        @pl.when(i == steps - 1)
        def _():
            for at in row_tiles(n):
                value, normed, recip = normalize(total[at, :], norms[1:2, :], norms[5:6, :])
                output[at, :] = value.astype(output.dtype)
                normed_two[at, :] = normed.astype(LOW)
                recip_two[at, :] = recip

    neurons = per * size
    ffn_out = ((2, n, neurons), LOW, (1, n, size), lambda i: (i // per, 0, i % per))
    return call(
        body, steps,
        [
            whole(hidden_low), whole(layer.norms), per_group(layer.bias_up),
        ] + layer.ffn(layer.up) + layer.ffn(layer.down),
        [
            ffn_out, ffn_out, out_whole((n, depth), F32 if wide else LOW), out_whole((n, depth), LOW),
            out_whole((n, 1), F32),
        ],
        [pltpu.VMEM((n, depth), F32)],
        flops=8 * n * depth * neurons,
        exps=4 * n * neurons,
    )


def add_rows(sums, row, value, at):
    value = jnp.sum(value, axis=0, keepdims=True)
    if at.start == 0:
        sums[row : row + 1, :] = value
    else:
        sums[row : row + 1, :] += value


def ffn_back_call(layer, grad, extra, kept, half):
    n, depth = grad.shape
    steps, _, size = layer.bias_up.shape
    per = steps // 2
    has_extra = extra is not None

    def body(grad, *refs):
        extra = refs[0] if has_extra else None
        (
            normed_one, recip_one, normed_two, recip_two, norms, slope, up_one, up_two, down_one, down_two,
            d_final_low, d_pre, d_mid_low, sums, bias_sums, total,
        ) = refs[1:] if has_extra else refs
        i = pl.program_id(0)
        gain = lambda at: norms[at : at + 1, :]

        @pl.when(i == 0)
        def _():
            sums[...] = jnp.zeros_like(sums)
            for at in row_tiles(n):
                value = grad[at, :].astype(F32)
                if has_extra and at.start >= 2 * half:
                    value = value + extra[at.start - 2 * half : at.stop - 2 * half, :].astype(F32)
                normed = normed_two[at, :].astype(F32)
                back = normalize_back(value, normed, recip_two[at, :], gain(1))
                total[at, :] = back
                d_final_low[at, :] = back.astype(LOW)
                add_rows(sums, 1, value * normed, at)
                add_rows(sums, 5, value, at)
                add_rows(sums, 4, back, at)

        bias = None
        up, down = joined((up_one, up_two)), joined((down_one, down_two))
        for at in row_tiles(n):
            d_act = dot(d_final_low[at, :], down, 1, 0)
            low = (d_act * slope[0, at, :].astype(F32)).astype(LOW)
            d_pre[0, at, :] = low
            one = jnp.sum(low.astype(F32), axis=0, keepdims=True)
            bias = one if bias is None else bias + one
            total[at, :] += dot(low, up, 1, 1)
        bias_sums[0] = bias

        @pl.when(i == steps - 1)
        def _():
            for at in row_tiles(n):
                value = total[at, :]
                normed = normed_one[at, :].astype(F32)
                back = normalize_back(value, normed, recip_one[at, :], gain(0))
                d_mid_low[at, :] = back.astype(LOW)
                add_rows(sums, 0, value * normed, at)
                add_rows(sums, 3, value, at)
                add_rows(sums, 2, back, at)

    neurons = per * size
    blocks = ((1, n, size), lambda i: (i // per, 0, i % per))
    return call(
        body, steps,
        [whole(grad)] + ([whole(extra)] if has_extra else []) + [
            whole(kept["normed_one"]), whole(kept["recip_one"]), whole(kept["normed_two"]),
            whole(kept["recip_two"]), whole(layer.norms), (kept["slope"],) + blocks,
        ] + layer.ffn(layer.up) + layer.ffn(layer.down),
        [
            out_whole((n, depth), LOW), ((2, n, neurons), LOW) + blocks, out_whole((n, depth), LOW),
            out_whole((8, depth), F32), out_group((steps, 1, size), F32),
        ],
        [pltpu.VMEM((n, depth), F32)],
        flops=8 * n * depth * neurons,
    )


def ffn_back_first_call(layer, grad, extra, kept, half):
    n, depth = grad.shape
    steps, _, size = layer.bias_up.shape
    per = steps // 2

    def body(
        grad, extra, normed_two, recip_two, norms, slope, down_one, down_two,
        d_final_low, d_pre, sums, bias_sums,
    ):
        i = pl.program_id(0)

        @pl.when(i == 0)
        def _():
            sums[...] = jnp.zeros_like(sums)
            for at in row_tiles(n):
                value = grad[at, :].astype(F32)
                if at.start >= 2 * half:
                    value = value + extra[at.start - 2 * half : at.stop - 2 * half, :].astype(F32)
                normed = normed_two[at, :].astype(F32)
                back = normalize_back(value, normed, recip_two[at, :], norms[1:2, :])
                d_final_low[at, :] = back.astype(LOW)
                add_rows(sums, 1, value * normed, at)
                add_rows(sums, 5, value, at)
                add_rows(sums, 4, back, at)

        bias = None
        down = joined((down_one, down_two))
        for at in row_tiles(n):
            d_act = dot(d_final_low[at, :], down, 1, 0)
            low = (d_act * slope[0, at, :].astype(F32)).astype(LOW)
            d_pre[0, at, :] = low
            one = jnp.sum(low.astype(F32), axis=0, keepdims=True)
            bias = one if bias is None else bias + one
        bias_sums[0] = bias

    neurons = per * size
    blocks = ((1, n, size), lambda i: (i // per, 0, i % per))
    return call(
        body, steps,
        [
            whole(grad), whole(extra), whole(kept["normed_two"]), whole(kept["recip_two"]),
            whole(layer.norms), (kept["slope"],) + blocks,
        ] + layer.ffn(layer.down),
        [
            out_whole((n, depth), LOW), ((2, n, neurons), LOW) + blocks,
            out_whole((8, depth), F32), out_group((steps, 1, size), F32),
        ],
        [],
        flops=4 * n * depth * neurons,
    )


def ffn_back_second_call(layer, d_final_low, d_pre, kept):
    n, depth = d_final_low.shape
    steps, _, size = layer.bias_up.shape
    per = steps // 2

    def body(d_final, d_pre, normed_one, recip_one, norms, up_one, up_two, d_mid_low, sums, total):
        i = pl.program_id(0)

        @pl.when(i == 0)
        def _():
            total[...] = d_final[...].astype(F32)

        up = joined((up_one, up_two))
        for at in row_tiles(n):
            total[at, :] += dot(d_pre[0, at, :], up, 1, 1)

        @pl.when(i == steps - 1)
        def _():
            sums[...] = jnp.zeros_like(sums)
            for at in row_tiles(n):
                value = total[at, :]
                normed = normed_one[at, :].astype(F32)
                back = normalize_back(value, normed, recip_one[at, :], norms[0:1, :])
                d_mid_low[at, :] = back.astype(LOW)
                add_rows(sums, 0, value * normed, at)
                add_rows(sums, 3, value, at)
                add_rows(sums, 2, back, at)

    blocks = ((1, n, size), lambda i: (i // per, 0, i % per))
    return call(
        body, steps,
        [
            whole(d_final_low), (d_pre,) + blocks, whole(kept["normed_one"]), whole(kept["recip_one"]),
            whole(layer.norms),
        ] + layer.ffn(layer.up),
        [out_whole((n, depth), LOW), out_whole((8, depth), F32)],
        [pltpu.VMEM((n, depth), F32)],
        flops=4 * n * depth * per * size,
    )


def shared_back_call(layer, d_mid_low, kept, segs, half):
    n, depth = d_mid_low.shape
    width, wide, own = layer.width, 3 * layer.width, 2 * half
    count = 2 * len(layer.qkv_blocks)

    def body(d_mid, proj, away, logsum, *refs):
        weights = pairs_of(refs[:count])
        out_one, out_two, segs_q, segs_k, d_proj, d_away, sums, back, mask, total = refs[count:]
        i = pl.program_id(0)
        make_mask(segs_q, segs_k, mask)
        out_cols = joined((out_one, out_two), slice(layer.out_from, layer.out_from + width))
        d_context = dot(d_mid[...], out_cols, 1, 0).astype(LOW)
        attend_back(
            width, [proj.at[0], away.at[0]], mask, logsum.at[0], d_context,
            [d_proj.at[0], d_away.at[0]], sums.at[0],
        )
        part = through_projection(d_away[0], weights, layer.used)

        @pl.when(i == 0)
        def _():
            total[...] = part

        @pl.when(i == 1)
        def _():
            back[...] = (total[...] + part).astype(LOW)

    return call(
        body, 2,
        [
            (d_mid_low, (half, depth), lambda i: (2, 0)), (kept["proj"], (1, half, wide), lambda i: (i, 2, 0)),
            per_group(kept["proj_away"]), per_group(kept["logsum_shared"]),
        ] + layer.qkv() + layer.out() + [whole(segs[None, :half]), whole(segs[:, None])],
        [
            out_group((2, half, wide), LOW), out_group((2, half, wide), LOW), out_group((2, 8, wide), F32),
            out_whole((half, depth), LOW),
        ],
        [pltpu.VMEM((own, half), F32), pltpu.VMEM((half, depth), F32)],
        flops=4 * half * depth * (wide + width) + 20 * own * half * width,
        exps=2 * own * half * width // HEAD_DIM,
    )


def own_back_call(layer, d_mid_low, d_shared, kept, segs, half, with_rows):
    n, depth = d_mid_low.shape
    width, wide, own = layer.width, 3 * layer.width, 2 * half
    count = 2 * len(layer.qkv_blocks) if with_rows else 0

    def body(d_mid_low, d_shared, proj, logsum, out_one, out_two, segs_q, segs_k, *refs):
        i = pl.program_id(0)
        if with_rows:
            d_mid, weights = refs[0], pairs_of(refs[1 : count + 1])
            d_proj, sums, d_rows, mask, total = refs[count + 1 :]
        else:
            d_proj, sums, mask = refs
        make_mask(segs_q, segs_k, mask)
        out_cols = joined((out_one, out_two), slice(layer.out_from, layer.out_from + width))
        d_context = dot(d_mid_low[...], out_cols, 1, 0).astype(LOW)
        attend_back(
            width, [proj.at[0]], mask, logsum.at[0], d_context, [d_proj.at[0, :own]], sums.at[0]
        )
        d_proj[0, own:] = d_shared[0]
        if with_rows:
            part = through_projection(d_proj[0], weights, layer.used)

            @pl.when(i == 0)
            def _():
                total[...] = d_mid[...].astype(F32) + part

            @pl.when(i == 1)
            def _():
                d_rows[...] = (total[...] + part).astype(LOW)

    return call(
        body, 2,
        [
            (d_mid_low, (own, depth), lambda i: (0, 0)), per_group(d_shared),
            (kept["proj"], (1, own, wide), lambda i: (i, 0, 0)), per_group(kept["logsum_own"]),
        ] + layer.out() + [whole(segs[None, :]), whole(segs[:, None])]
        + ([whole(d_mid_low)] + layer.qkv() if with_rows else []),
        [out_group((2, n, wide), LOW), out_group((2, 8, wide), F32)]
        + ([out_whole((n, depth), LOW)] if with_rows else []),
        [pltpu.VMEM((own, own), F32)] + ([pltpu.VMEM((n, depth), F32)] if with_rows else []),
        flops=4 * depth * (n * wide * with_rows + own * width) + 20 * own * own * width,
        exps=2 * own * own * width // HEAD_DIM,
    )


def rows_back_call(layer, d_mid_low, d_proj):
    n, depth = d_mid_low.shape
    wide = 3 * layer.width

    def body(d_mid, d_proj, *refs):
        weights, d_rows = pairs_of(refs[:-1]), refs[-1]

        @pl.when(pl.program_id(0) == 0)
        def _():
            d_rows[...] = d_mid[...].astype(F32)

        d_rows[...] += through_projection(d_proj[0], weights, layer.used)

    return call(
        body, 2, [whole(d_mid_low), per_group(d_proj)] + layer.qkv(), [out_whole((n, depth), F32)], [],
        flops=4 * depth * n * wide,
    )[0]


class Grads:
    def __init__(self, entries, columns, cut):
        self.entries, self.columns, self.cut = entries, columns, cut
        sizes = [end - start for _, start, end in columns]
        self.size_a, self.size_b = sum(sizes[:cut]), sum(sizes[cut:])

    def inputs(self, at, side):
        out = []
        for pairs in self.entries:
            for left, right in pairs:
                half = (left.shape[0], left.shape[1] // 2)
                out += [(left, half, lambda i: (0, side)), per_group(right, at)]
        return out

    def flops(self, rows):
        return sum(
            4 * rows * left.shape[0] * right.shape[2] for pairs in self.entries for left, right in pairs
        )

    def product(self, refs, entry, start, end):
        first = sum(len(pairs) for pairs in self.entries[:entry])
        total = None
        for at in range(first, first + len(self.entries[entry])):
            one = dot(refs[2 * at][...], refs[2 * at + 1][0, :, start:end], 0, 0)
            total = one if total is None else total + one
        return total

    def send(self):
        rows = self.entries[0][0][0].shape[1] // 2
        size = self.size_a + self.size_b

        def body(*refs):
            col = 0
            for entry, start, end in self.columns:
                part = self.product(refs, entry, start, end)
                refs[-1][0, :, col : col + end - start] = part.astype(LOW)
                col += end - start

        return call(
            body, 2, self.inputs(lambda i: i, 1), [out_group((2, rows, size), LOW)], [], self.flops(rows)
        )[0]

    def keep(self, got):
        rows = self.entries[0][0][0].shape[1] // 2
        half = rows // 2

        def body(got, *refs):
            send_a, keep_a, send_b, keep_b = refs[-4:]
            i = pl.program_id(0)
            col = 0
            for at, (entry, start, end) in enumerate(self.columns):
                part = self.product(refs, entry, start, end)
                part = part + got[0, :, col : col + end - start].astype(F32)
                if at < self.cut:
                    place = slice(col, col + end - start)

                    @pl.when(i == 0)
                    def _():
                        send_a[:, place] = part.astype(LOW)

                    @pl.when(i == 1)
                    def _():
                        keep_a[:, place] = part.astype(LOW)
                else:
                    place = slice(col - self.size_a, col - self.size_a + end - start)
                    keep_b[0, :, place] = part[:half].astype(LOW)
                    send_b[0, :, place] = part[half:].astype(LOW)
                col += end - start

        return call(
            body, 2,
            [per_group(got, lambda i: 1 - i)] + self.inputs(lambda i: 1 - i, 0),
            [
                out_whole((rows, self.size_a), LOW), out_whole((rows, self.size_a), LOW),
                out_group((2, half, self.size_b), LOW), out_group((2, half, self.size_b), LOW),
            ],
            [], self.flops(rows),
        )


class Reduce:
    def __init__(self, grads):
        self.grads = grads
        self.sends = (grads.send(),)
        self.got = (swap_core(self.sends[0]),)
        self.work = self._run()

    def _run(self):
        count = lax.axis_size("dp") // 4
        send_a, keep_a, send_b, keep_b = self.grads.keep(self.got[0])
        fourth = keep_a.shape[0] // 2
        self.sends = (send_a, send_b)
        self.got = (swap_y(send_a), swap_x(send_b))
        yield
        a = keep_a + self.got[0].astype(F32)
        b = keep_b + self.got[1].astype(F32)
        self.sends = (a[fourth:].astype(LOW), b[0].astype(LOW))
        self.got = (swap_x(self.sends[0]), swap_y(self.sends[1]))
        a, b = a[:fourth], b[1]
        yield
        both = jnp.concatenate([a + self.got[0].astype(F32), b + self.got[1].astype(F32)], axis=1)
        both = both.reshape((count, -1) + both.shape[1:])
        self.sends = tuple(both[back].astype(LOW) for back in range(1, count))
        self.got = tuple(ring_shift(send, -back) for back, send in enumerate(self.sends, 1))
        yield
        total = both[0] + sum(got.astype(F32) for got in self.got)
        self.total = total
        self.got = self.sends = ()

    def step(self):
        next(self.work, None)


class Total:
    def __init__(self, value):
        self.total = value
        self.work = self._run()
        self.step()

    def _run(self):
        n = lax.axis_size("dp")
        self.sends = (self.total,)
        self.got = (swap_y(self.total),)
        yield
        self.total = self.total + self.got[0]
        step = 1
        while step < n:
            self.sends = (self.total,)
            self.got = (lax.ppermute(self.total, "dp", [(i, i ^ step) for i in range(n)]),)
            yield
            self.total = self.total + self.got[0]
            step *= 2
        self.got = self.sends = ()

    def step(self):
        next(self.work, None)


def round_of(*works):
    ended = lax.optimization_barrier(tuple(work.got for work in works))
    for work, got in zip(works, ended):
        work.got = got
    for work in works:
        work.step()


def before(value, *works):
    value, ended = lax.optimization_barrier((value, tuple(work.got for work in works)))
    for work, got in zip(works, ended):
        work.got = got
    return value


def forward_attn(layer, rows, proj, context_own, logsum_own, rows_low, away_low, segs, half):
    proj_away, context, logsum_shared, hidden_low, normed_one, recip_one = shared_call(
        layer, rows, proj, away_low, context_own, segs[1], half
    )
    kept = dict(
        rows_low=rows_low, away_low=away_low, proj=proj, proj_away=proj_away, context=context,
        logsum_own=logsum_own, logsum_shared=logsum_shared, hidden_low=hidden_low,
        normed_one=normed_one, recip_one=recip_one,
    )
    return hidden_low, kept


def forward_ffn(layer, hidden_low, kept, wide):
    act, slope, output, normed_two, recip_two = ffn_call(layer, hidden_low, wide)
    kept.update(act=act, slope=slope, normed_two=normed_two, recip_two=recip_two)
    return output


def backward_ffn(layer, grad, extra, kept, half):
    d_final_low, d_pre, d_mid_low, sums, bias_sums = ffn_back_call(layer, grad, extra, kept, half)
    entries = [[(kept["hidden_low"], d_pre)], [(d_final_low, kept["act"])]]
    return d_mid_low, sums[:6], bias_sums, entries


def attn_entries(kept, d_proj, d_away, d_mid_low):
    return [[(kept["rows_low"], d_proj), (kept["away_low"], d_away)], [(d_mid_low, kept["context"])]]


def on_device(
    tokens, segment_ids, out_grad,
    t_qkv, t_qv_bias, t_out, t_up, t_up_bias, t_down, t_gains, t_shifts,
    s_qkv, s_qv_bias, s_out, s_up, s_up_bias, s_down, s_gains, s_shifts,
):
    rows, half, width = tokens.shape
    first = lax.axis_index("mp") == 0
    own_row = lambda value: jnp.where(first, value[0], value[2])
    far_row = lambda value: jnp.where(first, value[2], value[0])

    norm_rows = jnp.concatenate([t_gains, t_shifts, s_gains, s_shifts], axis=0)
    norm_rows = jnp.pad(norm_rows, ((0, 128 - norm_rows.shape[0]), (0, 0)))
    t_width, s_width = t_qkv.shape[2], s_qkv.shape[2]
    size = s_up.shape[1]
    per = t_up.shape[1] // size
    count, block = lax.axis_size("dp") // 4, t_up.shape[0]
    together = lambda *values: lax.optimization_barrier(values)
    every = slice(None)

    def columns(start, width):
        return slice(start, start + width)

    t_cut, t_all = 2 * t_width, 4 * t_width + 128
    f_cut = per * size
    s_cut = size + 2 * s_width
    packed_t = moves(
        [t_qkv, t_out.T, norm_rows.T], [(block, t_all)],
        [(0, (i,), 0, (every, columns(i * t_width, t_width))) for i in range(3)]
        + [
            (1, (every,), 0, (every, columns(3 * t_width, t_width))),
            (2, (every,), 0, (every, columns(4 * t_width, 128))),
        ],
    )[0]
    packed_f, student_a, student_b = moves(
        [t_up, t_down.T, s_up, s_qkv, s_out.T, s_down.T],
        [(block, 2 * f_cut), (block, s_cut), (block, s_cut)],
        [
            (0, (every,), 0, (every, columns(0, f_cut))), (1, (every,), 0, (every, columns(f_cut, f_cut))),
            (2, (every,), 1, (every, columns(0, size))), (3, (0,), 1, (every, columns(size, s_width))),
            (4, (every,), 1, (every, columns(size + s_width, s_width))),
            (5, (every,), 2, (every, columns(0, size))), (3, (1,), 2, (every, columns(size, s_width))),
            (3, (2,), 2, (every, columns(size + s_width, s_width))),
        ],
    )

    def along_z(value):
        return [value] + [ring_shift(value, at) for at in range(1, count)]

    def of_line(pieces, cut):
        rest = pieces[0].shape[1] - cut
        return moves(
            pieces, [(count, block, cut), (count, block, rest)],
            [(i, (every, columns(start, wide)), at, (i,)) for i in range(count)
             for at, (start, wide) in enumerate(((0, cut), (cut, rest)))],
        )

    def first_plane(a, got_a, b, got_b):
        return moves(
            [a, got_a, b, got_b], [(2,) + a.shape, (2,) + b.shape],
            [(0, (every,), 0, (0,)), (1, (every,), 0, (1,)), (2, (every,), 1, (0,)), (3, (every,), 1, (1,))],
        )

    def both_planes(a, got_a, b, got_b, order):
        copies, col = [], 0
        for of_b, start, wide in order:
            taken, place = (every, every, every, columns(start, wide)), (every, every, columns(col, wide))
            if of_b:
                copies += [(2, taken, 0, (every, 0) + place), (3, taken, 0, (every, 1) + place)]
            else:
                copies += [(0, taken, 0, (0, every) + place), (1, taken, 0, (1, every) + place)]
            col += wide
        out = moves([a, got_a, b, got_b], [(2, 2, count, block, col)], copies)[0]
        return out.reshape(2, width // 2, col)

    def with_core(own):
        return own, swap_core(own)

    bias_parts = [t_qv_bias[0], t_qv_bias[1], t_up_bias, s_qv_bias[0], s_qv_bias[1], s_up_bias]
    to_own = feature_order(width)
    into = (lax.iota(jnp.int32, width)[:, None] == to_own[None, :]).astype(LOW)
    def reorder(value):
        return jnp.dot(value, into, preferred_element_type=F32).astype(LOW)


    spin = lambda segs: jnp.where(first, segs, jnp.roll(segs, half))
    segs = (spin(own_row(segment_ids)), spin(segment_ids[1]))

    line_t, got_own = along_z(packed_t), swap_y(far_row(tokens))
    *line_t, got_own, into, segs, packed_f, student_a, student_b = together(
        *line_t, got_own, into, segs, packed_f, student_a, student_b
    )
    attn_a, attn_b = of_line(line_t, t_cut)
    got_a, got_b = swap_x(attn_a), swap_y(attn_b)
    line_f = along_z(packed_f)
    student_x, student_y = swap_x(student_a), swap_y(student_b)
    got_a, got_b, student_x, student_y, line_f[1] = together(got_a, got_b, student_x, student_y, line_f[1])
    inputs = reorder(jnp.concatenate([own_row(tokens), got_own, tokens[1]], axis=0))
    attn_a, attn_b = first_plane(attn_a, got_a, attn_b, got_b)
    got_a, got_b = swap_y(attn_a), swap_x(attn_b)
    line_s = along_z(moves(
        [student_a, student_x, student_b, student_y], [(2, block, 2 * s_cut)],
        [(i, (every,), 0, (i % 2, every, columns(i // 2 * s_cut, s_cut))) for i in range(4)],
    )[0])
    got_a, got_b, inputs, *line_f[2:] = together(got_a, got_b, inputs, *line_f[2:])
    attn = both_planes(
        attn_a, got_a, attn_b, got_b, [(False, 0, t_cut), (True, 0, t_all - t_cut)]
    )
    attn = with_core(attn)
    ffn_a, ffn_b = of_line(list(after(line_f, attn[0])), f_cut)
    got_a, got_b = swap_x(ffn_a), swap_y(ffn_b)
    bias_own = jnp.concatenate(bias_parts)
    bias_far = swap_y(bias_own)
    attn, got_a, got_b, bias_far = together(attn, got_a, got_b, bias_far)
    ffn_a, ffn_b = first_plane(ffn_a, got_a, ffn_b, got_b)
    got_a, got_b = swap_y(ffn_a), swap_x(ffn_b)
    got_shared = swap_y(tokens[1])
    norms = jnp.concatenate([half[0, :, -128:-116] for half in attn], axis=0).T.astype(F32)
    norms_of = lambda at: jnp.pad(norms[at : at + 6], ((0, 2), (0, 0)))
    bias_all = jnp.stack([bias_own, bias_far]).astype(F32)
    cuts = [0]
    for part in bias_parts:
        cuts.append(cuts[-1] + part.shape[0])
    pick = [bias_all[:, cuts[i] : cuts[i + 1]] for i in range(6)]
    bias_qkv = lambda q, v: jnp.concatenate([q, jnp.zeros_like(q), v], axis=1)[:, None, :]
    teacher = Layer(
        t_width, None, None, [(attn, t_width, i, t_width) for i in range(3)], (attn, t_width, 3, t_width), 0,
        norms_of(0), bias_qkv(pick[0], pick[1]), pick[2].reshape(2 * per, 1, size),
    )

    grad_in = jnp.concatenate([own_row(out_grad), swap_y(far_row(out_grad)), out_grad[1]], axis=0)

    inputs, ffn_a, ffn_b = together(inputs, ffn_a, ffn_b)
    proj, context_own, logsum_own = project_call(teacher, inputs, segs[0], half)
    proj, got_shared, *line_s[1:-1] = together(proj, got_shared, *line_s[1:-1])
    away_low = reorder(got_shared)
    hidden, t_kept = forward_attn(
        teacher, inputs, proj, context_own, logsum_own, inputs, away_low, segs, half
    )
    hidden, got_a, got_b, line_s[-1] = together(hidden, got_a, got_b, line_s[-1])
    ffn = both_planes(ffn_a, got_a, ffn_b, got_b, [(False, 0, f_cut), (True, 0, f_cut)])
    ffn = with_core(ffn)
    student_a, student_b = moves(
        line_s, [(2, count, block, s_cut)] * 2,
        [(i, (every, every, columns(at * s_cut, s_cut)), at, (every, i)) for i in range(count) for at in range(2)],
    )
    got_a, got_b = swap_y(student_a), swap_x(student_b)
    hidden, ffn = together(hidden, ffn)
    teacher.up, teacher.down = (ffn, 0), (ffn, per)
    middle_low = forward_ffn(teacher, hidden, t_kept, False)
    away_low = swap_y(middle_low[2 * half :])
    middle_low, got_a, got_b, grad_in = together(middle_low, got_a, got_b, grad_in)
    grad_in = reorder(grad_in)
    student_w = with_core(both_planes(
        student_a, got_a, student_b, got_b,
        [(False, 0, size), (True, 0, size), (False, size, 2 * s_width), (True, size, 2 * s_width)],
    ))
    narrow = 2 * s_width
    place = 2 * size // narrow
    student = Layer(
        s_width, (student_w, 0), (student_w, 1),
        [(student_w, narrow, place, s_width), (student_w, narrow, place + 1, narrow)],
        (student_w, narrow, place, s_width), s_width, norms_of(6), bias_qkv(pick[3], pick[4]),
        pick[5].reshape(2, 1, size),
    )
    proj, context_own, logsum_own = project_call(student, middle_low, segs[0], half)
    proj, away_low = together(proj, away_low)
    hidden, s_kept = forward_attn(
        student, middle_low, proj, context_own, logsum_own, middle_low, away_low, segs, half
    )
    last = forward_ffn(student, hidden, s_kept, True)

    def far_half(value):
        return swap_y(value[half : 2 * half].astype(LOW))

    def to_rows(value, far):
        near = jnp.concatenate([value[:half], value[2 * half :]], axis=0)
        high = near.astype(LOW)
        low = (near - high.astype(F32)).astype(LOW)
        back = lambda part: jnp.einsum("nr,dr->nd", part, into, preferred_element_type=F32)
        near, far = back(high) + back(low), back(far)
        return jnp.stack([jnp.where(first, near[:half], far), near[half:], jnp.where(first, far, near[:half])])

    far_last = far_half(last)

    d_mid_low, s_norm_grads, s_up_grad, s_entries = backward_ffn(student, grad_in, None, s_kept, half)
    d_shared, d_away, s_sums_b, back = shared_back_call(student, d_mid_low, s_kept, segs[1], half)
    extra = swap_y(back)
    d_shared, far_last = together(d_shared, far_last)
    d_proj, s_sums_a, d_rows = own_back_call(
        student, d_mid_low, d_shared, s_kept, segs[0], half, True
    )
    d_proj, extra = lax.optimization_barrier((d_proj, extra))
    s_entries += attn_entries(s_kept, d_proj, d_away, d_mid_low)
    s_columns = [(0, 0, size), (2, 0, s_width), (3, 0, s_width), (1, 0, size), (2, s_width, 3 * s_width)]
    reduce_s = Reduce(Grads(s_entries, s_columns, 3))

    d_rows = after(d_rows, reduce_s.sends)
    d_final_low, d_pre, t_sums_two, t_up_grad = ffn_back_first_call(
        teacher, d_rows, extra, t_kept, half
    )
    d_pre = before(d_pre, reduce_s)
    reduce_s.step()
    d_pre = after(d_pre, reduce_s.sends)
    f_entries = [[(t_kept["hidden_low"], d_pre)], [(d_final_low, t_kept["act"])]]
    reduce_f = Reduce(Grads(f_entries, [(0, 0, per * size), (1, 0, per * size)], 1))
    d_pre = after(d_pre, reduce_f.sends)
    d_mid_low, t_sums_one = ffn_back_second_call(teacher, d_final_low, d_pre, t_kept)
    t_norm_grads = (t_sums_one + t_sums_two)[:6]
    d_mid_low = before(d_mid_low, reduce_f)
    reduce_f.step()
    reduce_s.got = after(reduce_s.got, reduce_f.sends)
    d_mid_low = before(d_mid_low, reduce_s)
    reduce_s.step()
    d_mid_low = after(d_mid_low, reduce_s.sends)
    d_shared, d_away, t_sums_b, back = shared_back_call(teacher, d_mid_low, t_kept, segs[1], half)
    extra = swap_y(back)
    d_shared = before(d_shared, reduce_s)
    reduce_s.step()
    d_shared = after(d_shared, reduce_s.sends)
    d_proj, t_sums_a = own_back_call(teacher, d_mid_low, d_shared, t_kept, segs[0], half, False)
    t_entries = attn_entries(t_kept, d_proj, d_away, d_mid_low)
    reduce_t = Reduce(
        Grads(t_entries, [(0, 0, 2 * t_width), (0, 2 * t_width, 3 * t_width), (1, 0, t_width)], 1)
    )

    def qv_grad(one, two, wide):
        sums = one[:, 0] + two[:, 0]
        sums = jnp.concatenate([sums[:, :wide], sums[:, 2 * wide :]], axis=1)
        return jnp.pad(sums, ((0, 0), (0, width - 2 * wide)))

    norm_grads = jnp.concatenate([t_norm_grads, s_norm_grads], axis=0)
    norm_grads = jnp.einsum("nr,dr->nd", norm_grads, into.astype(F32), precision=lax.Precision.HIGHEST)
    qv_t, qv_s = qv_grad(t_sums_a, t_sums_b, t_width), qv_grad(s_sums_a, s_sums_b, s_width)
    mine = jnp.concatenate([t_up_grad[:per, 0], s_up_grad[:1, 0], qv_t[:1], qv_s[:1]], axis=0)
    other = jnp.concatenate([t_up_grad[per:, 0], s_up_grad[1:, 0], qv_t[1:], qv_s[1:]], axis=0)
    small = Total(jnp.concatenate(
        [norm_grads, jnp.where(first, mine, other), jnp.where(first, other, mine)], axis=0
    ))
    reduce_f.got = after(reduce_f.got, reduce_t.sends)
    round_of(reduce_f, small)
    reduce_t.got = after(reduce_t.got, reduce_f.sends)
    reduce_t.step()
    reduce_f.got = after(reduce_f.got, reduce_t.sends)
    round_of(reduce_f, reduce_s, small)
    d_rows = rows_back_call(teacher, *after((d_mid_low, d_proj), reduce_t.sends))
    reduce_t.got = after(reduce_t.got, d_rows)
    far_rows = far_half(d_rows)
    round_of(reduce_t, small)
    d_rows, last = after((d_rows, last), reduce_t.sends)
    d_rows = jnp.concatenate([d_rows[: 2 * half], d_rows[2 * half :] + extra.astype(F32)], axis=0)
    input_grad, output = to_rows(d_rows, far_rows), to_rows(last, far_last)
    round_of(reduce_t, reduce_f, small)
    round_of(reduce_t, small)
    for work in (reduce_f, reduce_s, small):
        while work.got:
            work.step()
    s_sum, f_sum, small = reduce_s.total, reduce_f.total, small.total

    piece = width // lax.axis_size("dp")
    norm_sum = lax.dynamic_slice_in_dim(small[:12], lax.axis_index("dp") * piece, piece, 1)
    bias_sum = small[12:].reshape(2, -1, width)
    bias_sum = jnp.where(first, bias_sum[0], bias_sum[1])
    t_qv_sum, s_qv_sum = bias_sum[per + 1], bias_sum[per + 2, : 2 * s_width]

    def cut(value, *sizes):
        out = []
        for one in sizes:
            out.append(value[:, :one])
            value = value[:, one:]
        return out

    t_up_sum, t_down_sum = cut(f_sum, per * size, per * size)
    s_up_sum, sq, so, s_down_sum, sk, sv = cut(s_sum, size, s_width, s_width, size, s_width, s_width)
    done = (
        output, input_grad, t_qv_sum.reshape(2, -1), t_up_sum, bias_sum[:per].reshape(-1), t_down_sum.T,
        norm_sum[0:2], norm_sum[2:6], jnp.stack([sq, sk, sv]), s_qv_sum.reshape(2, -1), so.T, s_up_sum,
        bias_sum[per], s_down_sum.T, norm_sum[6:8], norm_sum[8:12],
    )
    done, reduce_t.got = together(done, reduce_t.got)
    while reduce_t.got:
        reduce_t.step()
    tq, tk, tv, to = cut(reduce_t.total, t_width, t_width, t_width, t_width)
    return done[:2] + (jnp.stack([tq, tk, tv]), done[2], to.T) + done[3:]


def solution(mesh):
    layer = (
        P(None, "dp", "mp"), P(None, "mp"), P("mp", "dp"), P("dp", "mp"), P("mp"), P("mp", "dp"),
        P(None, "dp"), P(None, "dp"),
    )
    rows = P("dp", "mp", None)
    return jax.shard_map(
        on_device,
        mesh=mesh,
        in_specs=(rows, P("dp", None), rows) + layer + layer,
        out_specs=(rows, rows) + layer + layer,
        check_vma=False,
    )
```
